32 devices in a mesh: batch: 4 (over z), seq: 8 (over y, x, core).
Axes of the slice: x: 2, y: 2, z: 4, core: 2. Of those that a mesh axis runs over, the one named last changes fastest.
Arguments:
- token_ids: int32 [4, 4096], P('batch', 'seq'), may hold values from 0 to 31999
- book_lengths: int32 [4, 8], P('batch'), may hold values from 1 to 4089, as said below
- loss_mask: int32 [4, 4096], P('batch', 'seq'), may hold values from 0 to 1, as said below
- table_master: float32 [32000, 1024], P(('batch', 'seq')), may hold values from -0.375 to 0.375
- attn_in_master: float32 [1024, 3072], P(('batch', 'seq')), may hold values from -0.1875 to 0.1875
- attn_out_master: float32 [1024, 1024], P(('batch', 'seq')), may hold values from -3 to 3
- compress_master: float32 [3072, 1024], P(('batch', 'seq')), may hold values from -0.109375 to 0.109375
- ffn_in_master: float32 [1024, 4096], P(('batch', 'seq')), may hold values from -0.1875 to 0.1875
- ffn_out_master: float32 [4096, 1024], P(('batch', 'seq')), may hold values from -0.25 to 0.25
- gains_master: float32 [1024, 3], P(('batch', 'seq')), may hold values from 0.5 to 1.5
- table_first: float32 [32000, 1024], P(('batch', 'seq')), may hold values from -0.00021362305 to 0.00021362305
- attn_in_first: float32 [1024, 3072], P(('batch', 'seq')), may hold values from -0.0009765625 to 0.0009765625
- attn_out_first: float32 [1024, 1024], P(('batch', 'seq')), may hold values from -0.0009765625 to 0.0009765625
- compress_first: float32 [3072, 1024], P(('batch', 'seq')), may hold values from -0.0009765625 to 0.0009765625
- ffn_in_first: float32 [1024, 4096], P(('batch', 'seq')), may hold values from -0.0009765625 to 0.0009765625
- ffn_out_first: float32 [4096, 1024], P(('batch', 'seq')), may hold values from -0.0009765625 to 0.0009765625
- gains_first: float32 [1024, 3], P(('batch', 'seq')), may hold values from -0.001953125 to 0.001953125
- table_second: float32 [32000, 1024], P(('batch', 'seq')), may hold values from 4.8828124e-09 to 1.953125e-08
- attn_in_second: float32 [1024, 3072], P(('batch', 'seq')), may hold values from 3.8146973e-06 to 6.1035156e-05
- attn_out_second: float32 [1024, 1024], P(('batch', 'seq')), may hold values from 1.5258789e-07 to 6.1035155e-07
- compress_second: float32 [3072, 1024], P(('batch', 'seq')), may hold values from 1.5258789e-07 to 6.1035155e-07
- ffn_in_second: float32 [1024, 4096], P(('batch', 'seq')), may hold values from 1.5258789e-07 to 6.1035155e-07
- ffn_out_second: float32 [4096, 1024], P(('batch', 'seq')), may hold values from 1.5258789e-07 to 6.1035155e-07
- gains_second: float32 [1024, 3], P(('batch', 'seq')), may hold values from 6.1035155e-07 to 2.4414062e-06
Outputs:
- loss: float32 [], replicated
- table_first_new: float32 [32000, 1024], P(('batch', 'seq'))
- table_second_new: float32 [32000, 1024], P(('batch', 'seq'))
- table_new: float32 [32000, 1024], P(('batch', 'seq'))
- attn_in_first_new: float32 [1024, 3072], P(('batch', 'seq'))
- attn_in_second_new: float32 [1024, 3072], P(('batch', 'seq'))
- attn_in_new: float32 [1024, 3072], P(('batch', 'seq'))
- attn_out_first_new: float32 [1024, 1024], P(('batch', 'seq'))
- attn_out_second_new: float32 [1024, 1024], P(('batch', 'seq'))
- attn_out_new: float32 [1024, 1024], P(('batch', 'seq'))
- compress_first_new: float32 [3072, 1024], P(('batch', 'seq'))
- compress_second_new: float32 [3072, 1024], P(('batch', 'seq'))
- compress_new: float32 [3072, 1024], P(('batch', 'seq'))
- ffn_in_first_new: float32 [1024, 4096], P(('batch', 'seq'))
- ffn_in_second_new: float32 [1024, 4096], P(('batch', 'seq'))
- ffn_in_new: float32 [1024, 4096], P(('batch', 'seq'))
- ffn_out_first_new: float32 [4096, 1024], P(('batch', 'seq'))
- ffn_out_second_new: float32 [4096, 1024], P(('batch', 'seq'))
- ffn_out_new: float32 [4096, 1024], P(('batch', 'seq'))
- gains_first_new: float32 [1024, 3], P(('batch', 'seq'))
- gains_second_new: float32 [1024, 3], P(('batch', 'seq'))
- gains_new: float32 [1024, 3], P(('batch', 'seq'))
The draws below stay inside these ranges and needn't reach their ends.
Inputs may be any that keep to these rules, and one draw needn't show every extreme that they name: `book_lengths`: a row's lengths sum to 4096; its fourth book starts within the first 512 positions and ends within the last 512; in some row every other book has length 1. `loss_mask`: each aligned run of 512 positions of a row holds at most 256 ones, the last run of every row exactly that many.
All inputs are finite; a program needn't handle non-finite values.
Results may differ from the reference program's by a relative error of at most 0.018.
The reference program's roundings to bfloat16 on the way count: a program that leaves them out, or rounds other values in their place, can miss the bound.
Values may be sent and summed in bfloat16 or wider, within the bound.
No kernel may reach another device: no remote copies, remote signals or barrier semaphores. Data moves between devices by JAX's collectives and lax.ppermute only.
A program may use at most 576 MiB of HBM per device.

```python
import math
import jax
import jax.numpy as jnp
import numpy as np
from jax import lax

MODEL_WIDTH = 1024
HEADS = 8
HEAD = 128
FF = 4096
V = 32000
SEG = 512
NBOOK = 8
STEP = 5
B_ROWS = 4
LEN = 4096


def draw_book_lengths(key, part):
    key = jax.random.fold_in(key, 11)
    lead_key, trail_key, pick_key = jax.random.split(key, 3)
    leading = jax.random.randint(lead_key, (B_ROWS, 3), 1, (SEG - 1) // 3 + 1)
    trailing = jax.random.randint(trail_key, (B_ROWS, NBOOK - 4), 1, (SEG - 1) // 4 + 1)
    chosen = jax.random.randint(pick_key, (), 0, B_ROWS)
    row_index = jnp.arange(B_ROWS, dtype=jnp.int32)[:, None]
    leading = jnp.where(row_index == chosen, 1, leading)
    trailing = jnp.where(row_index == chosen, 1, trailing)
    middle = LEN - jnp.sum(leading, -1, keepdims=True) - jnp.sum(trailing, -1, keepdims=True)
    return jnp.concatenate([leading, middle, trailing], -1).astype(jnp.int32)


def draw_loss_mask(key, part):
    key = jax.random.fold_in(key, 23)
    score_key, jitter_key = jax.random.split(key, 2)
    runs = LEN // SEG
    scores = jax.random.randint(score_key, (B_ROWS, runs, SEG), 0, 1 << 30)
    order = jnp.argsort(scores, -1, stable=True)
    ranks = jnp.argsort(order, -1, stable=True)
    run_index = jnp.arange(runs, dtype=jnp.int32)[None, :]
    jitter = jax.random.randint(jitter_key, (B_ROWS, runs), 0, max(SEG // 16, 2))
    wanted = jnp.minimum(SEG // 2, SEG // 6 + SEG // 3 * run_index // max(runs - 1, 1) + jitter)
    wanted = jnp.where(run_index == runs - 1, SEG // 2, wanted)
    return (ranks < wanted[:, :, None]).astype(jnp.int32).reshape(B_ROWS, LEN)


def touch_ends(entries, own_key, smallest, largest):
    longest = entries.shape.index(max(entries.shape))
    spots = []
    for shift in (0, 1):
        where = [jax.random.randint(jax.random.fold_in(own_key, axis), (), 0, length) for axis, length in enumerate(entries.shape)]
        where[longest] = (where[longest] + shift) % entries.shape[longest]
        spots.append(tuple(where))
    return entries.at[spots[0]].set(smallest).at[spots[1]].set(largest)


def steps_of(key, shape, cuts, smallest, top_value):
    level, own = 1.0, jax.random.fold_in(key, 6)
    for position, shards_of in cuts:
        draws = jnp.exp(jax.random.uniform(jax.random.fold_in(own, position), (shards_of,), jnp.float32, smallest / len(cuts), top_value / len(cuts)))
        level = level * jnp.repeat(draws, shape[position] // shards_of).reshape([-1 if axis == position else 1 for axis in range(len(shape))])
    return level


def rank_table(count, skew):
    portions = [(1 << 20) // math.isqrt(standing ** skew) + 1 for standing in range(1, count + 1)]
    width = 1 + sum(portions) // (1 << 30)
    return np.cumsum(np.array([max(1, weight // width) for weight in portions]))


def ranked(own_key, shape, count, skew):
    listing = rank_table(count, skew)
    ticket = jax.random.randint(jax.random.fold_in(own_key, 1), shape, 0, int(listing[count - 1]))
    standing = jnp.searchsorted(jnp.asarray(listing, jnp.int32), ticket, side="right")
    return jax.random.permutation(jax.random.fold_in(own_key, 2), count)[standing].astype(jnp.int32)


def noise(rng, shape, width, most, pieces=(), kind=jnp.bfloat16):
    array = jax.random.normal(rng, shape, jnp.float32) * width
    if len(pieces) > 0:
        array = steps_of(rng, shape, pieces, -0.22, 0.18) * array
    return jnp.clip(array, min=-most, max=most).astype(kind)


def setup_inputs(seed: int = 0) -> dict:
    key_of = jax.random.split(jax.random.key(seed), 25)
    return {
        "token_ids": touch_ends(ranked(key_of[0], (B_ROWS, LEN), V, 1), jax.random.fold_in(key_of[0], 3), 0, V - 1).astype(jnp.int32),
        "book_lengths": draw_book_lengths(jax.random.fold_in(key_of[24], 71), 0),
        "loss_mask": draw_loss_mask(jax.random.fold_in(key_of[24], 71), 0),
        "table_master": noise(key_of[3], (V, MODEL_WIDTH), (MODEL_WIDTH // 4) ** -0.5, 0.375, ((0, 32),), jnp.float32),
        "attn_in_master": noise(key_of[4], (MODEL_WIDTH, 3 * MODEL_WIDTH), MODEL_WIDTH ** -0.5, 0.1875, ((0, 32),), jnp.float32),
        "attn_out_master": noise(key_of[5], (MODEL_WIDTH, MODEL_WIDTH), (max(MODEL_WIDTH // 256, 1)) ** -0.5, 3.0, ((0, 32),), jnp.float32),
        "compress_master": noise(key_of[6], (3 * MODEL_WIDTH, MODEL_WIDTH), (3 * MODEL_WIDTH) ** -0.5, 0.109375, ((0, 32),), jnp.float32),
        "ffn_in_master": noise(key_of[7], (MODEL_WIDTH, FF), MODEL_WIDTH ** -0.5, 0.1875, ((0, 32),), jnp.float32),
        "ffn_out_master": noise(key_of[8], (FF, MODEL_WIDTH), (FF // 8) ** -0.5, 0.25, ((0, 32),), jnp.float32),
        "gains_master": jnp.clip(1.0 + 0.1 * jax.random.normal(key_of[9], (MODEL_WIDTH, 3), jnp.float32), 0.5, 1.5),
        "table_first": noise(key_of[10], (V, MODEL_WIDTH), (0.11 * (3 * B_ROWS * (LEN * V) ** -1) ** 0.5), 0.00021362305, ((0, 32),), jnp.float32),
        "attn_in_first": noise(key_of[11], (MODEL_WIDTH, 3 * MODEL_WIDTH), (0.11 * (3 * B_ROWS * (LEN * MODEL_WIDTH) ** -1) ** 0.5), 0.0009765625, ((0, 32),), jnp.float32),
        "attn_out_first": noise(key_of[12], (MODEL_WIDTH, MODEL_WIDTH), (0.11 * (3 * B_ROWS * (LEN * MODEL_WIDTH) ** -1) ** 0.5), 0.0009765625, ((0, 32),), jnp.float32),
        "compress_first": noise(key_of[13], (3 * MODEL_WIDTH, MODEL_WIDTH), (0.11 * (3 * B_ROWS * (LEN * MODEL_WIDTH) ** -1) ** 0.5), 0.0009765625, ((0, 32),), jnp.float32),
        "ffn_in_first": noise(key_of[14], (MODEL_WIDTH, FF), (0.11 * (3 * B_ROWS * (LEN * MODEL_WIDTH) ** -1) ** 0.5), 0.0009765625, ((0, 32),), jnp.float32),
        "ffn_out_first": noise(key_of[15], (FF, MODEL_WIDTH), (0.11 * (3 * B_ROWS * (LEN * MODEL_WIDTH) ** -1) ** 0.5), 0.0009765625, ((0, 32),), jnp.float32),
        "gains_first": noise(key_of[16], (MODEL_WIDTH, 3), (0.22 * (3 * B_ROWS * (LEN * MODEL_WIDTH) ** -1) ** 0.5), 0.001953125, ((0, 32),), jnp.float32),
        "table_second": jnp.clip(jnp.exp(math.log(1.9531249506599124e-08) - 1.3862944 * jax.random.uniform(key_of[17], (V, MODEL_WIDTH), jnp.float32) ** steps_of(key_of[17], (V, MODEL_WIDTH), ((0, 32),), -0.2, 0.2)), 4.882812376649781e-09, 1.9531249506599124e-08),
        "attn_in_second": jnp.clip(jnp.exp(math.log(6.103515625e-05) - 2.7725887 * jax.random.uniform(key_of[18], (MODEL_WIDTH, 3 * MODEL_WIDTH), jnp.float32) ** steps_of(key_of[18], (MODEL_WIDTH, 3 * MODEL_WIDTH), ((0, 32),), -0.2, 0.2)), 3.814697265625e-06, 6.103515625e-05),
        "attn_out_second": jnp.clip(jnp.exp(math.log(6.103515488575795e-07) - 1.3862944 * jax.random.uniform(key_of[19], (MODEL_WIDTH, MODEL_WIDTH), jnp.float32) ** steps_of(key_of[19], (MODEL_WIDTH, MODEL_WIDTH), ((0, 32),), -0.2, 0.2)), 1.5258788721439487e-07, 6.103515488575795e-07),
        "compress_second": jnp.clip(jnp.exp(math.log(6.103515488575795e-07) - 1.3862944 * jax.random.uniform(key_of[20], (3 * MODEL_WIDTH, MODEL_WIDTH), jnp.float32) ** steps_of(key_of[20], (3 * MODEL_WIDTH, MODEL_WIDTH), ((0, 32),), -0.2, 0.2)), 1.5258788721439487e-07, 6.103515488575795e-07),
        "ffn_in_second": jnp.clip(jnp.exp(math.log(6.103515488575795e-07) - 1.3862944 * jax.random.uniform(key_of[21], (MODEL_WIDTH, FF), jnp.float32) ** steps_of(key_of[21], (MODEL_WIDTH, FF), ((0, 32),), -0.2, 0.2)), 1.5258788721439487e-07, 6.103515488575795e-07),
        "ffn_out_second": jnp.clip(jnp.exp(math.log(6.103515488575795e-07) - 1.3862944 * jax.random.uniform(key_of[22], (FF, MODEL_WIDTH), jnp.float32) ** steps_of(key_of[22], (FF, MODEL_WIDTH), ((0, 32),), -0.2, 0.2)), 1.5258788721439487e-07, 6.103515488575795e-07),
        "gains_second": jnp.clip(jnp.exp(math.log(2.441406195430318e-06) - 1.3862944 * jax.random.uniform(key_of[23], (MODEL_WIDTH, 3), jnp.float32) ** steps_of(key_of[23], (MODEL_WIDTH, 3), ((0, 32),), -0.2, 0.2)), 6.103515488575795e-07, 2.441406195430318e-06),
    }


EPSILON = 1e-05
NEGATIVE = -1e+30
BETA_ONE = 0.9
BETA_TWO = 0.95
ADAM_EPSILON = 1e-08
WEIGHT_DECAY = 0.1
STEP_RATES = (0.06, 0.03, 0.4, 0.02, 0.03, 0.04, 0.5)

@jax.custom_vjp
def low(v):
    return lax.optimization_barrier(v.astype(jnp.bfloat16)).astype(jnp.float32)

@jax.custom_vjp
def low_back(v):
    return v

def low_keep(v):
    return (low(v), None)

def low_pass(kept, grad):
    return (grad,)

def back_keep(v):
    return (v, None)

def back_low(kept, grad):
    return (low(grad),)
low.defvjp(low_keep, low_pass)
low_back.defvjp(back_keep, back_low)

def matmul(left_operand, right_operand):
    return jnp.dot(left_operand, right_operand, precision=lax.Precision.HIGHEST, preferred_element_type=jnp.float32)

def layer_norm(values, gain):
    center = values - lax.optimization_barrier(jnp.mean(values, -1, keepdims=True))
    return center * lax.rsqrt(lax.optimization_barrier(jnp.mean(center * center, -1, keepdims=True)) + EPSILON) * gain

def book_of(positions, book_ends):
    inside = lax.optimization_barrier(jnp.sum((positions[:, None] >= book_ends[None, :]).astype(jnp.int32), -1))
    return jnp.where(positions < 0, -1, inside)

def row_weights(ids_row, mask_row, ends_row):
    positions = jnp.arange(LEN, dtype=jnp.int32)
    book_now = book_of(positions, ends_row)
    book_next = book_of(positions + 1, ends_row)
    live = mask_row.astype(jnp.float32) * (book_next == book_now).astype(jnp.float32)
    member = (book_now[:, None] == jnp.arange(NBOOK, dtype=jnp.int32)[None, :]).astype(jnp.float32)
    counts = lax.optimization_barrier(jnp.sum(member * live[:, None], 0))
    return live * lax.optimization_barrier(jnp.sum(member / jnp.maximum(counts, 1.0)[None, :], -1))

def row_loss(weights, ids_row, ends_row, weight_row):
    table, attention_input_weight, attention_output_weight, w_compress, w_ffn_in, w_ffn_out, gains = weights
    length_value = ids_row.shape[0]
    embedded = table[ids_row] * MODEL_WIDTH ** 0.5
    attention_input = low(layer_norm(embedded, gains[:, 0]))
    projected = low(low_back(matmul(attention_input, attention_input_weight)))
    query = projected[:, :MODEL_WIDTH]
    pairs = projected[:, MODEL_WIDTH:]
    slot_total = length_value // 3
    memory_slot_rows = attention_input[:3 * slot_total].reshape(slot_total, 3 * MODEL_WIDTH)
    compressed_memory = low(low_back(matmul(memory_slot_rows, w_compress)))
    comp_pairs = low(low_back(matmul(compressed_memory, attention_input_weight[:, MODEL_WIDTH:])))
    final_slot_index = 3 * jnp.arange(slot_total, dtype=jnp.int32) + 2
    last_book = book_of(final_slot_index, ends_row)
    slot_book = jnp.where(book_of(final_slot_index - 2, ends_row) == last_book, last_book, -2)
    padded = jnp.concatenate([jnp.zeros((SEG, 2 * MODEL_WIDTH), jnp.float32), pairs], 0)

    def block(offset):
        query_rows = lax.dynamic_slice_in_dim(query, offset, SEG, 0)
        raw_rows = lax.dynamic_slice_in_dim(padded, offset, 2 * SEG, 0)
        key_rows = jnp.concatenate([raw_rows, comp_pairs], 0)
        query_pos = offset + jnp.arange(SEG, dtype=jnp.int32)
        unpacked_positions = offset - SEG + jnp.arange(2 * SEG, dtype=jnp.int32)
        in_range = (final_slot_index >= offset - 4 * SEG) & (final_slot_index < offset - SEG)
        key_book = jnp.concatenate([book_of(unpacked_positions, ends_row), jnp.where(in_range, slot_book, -2)])
        key_positions = jnp.concatenate([unpacked_positions, jnp.full((slot_total,), -1, jnp.int32)])
        allowed = (key_book[None, :] == book_of(query_pos, ends_row)[:, None]) & (key_positions[None, :] <= query_pos[:, None])
        query_heads = query_rows.reshape(SEG, HEADS, HEAD)
        key_heads = key_rows[:, :MODEL_WIDTH].reshape(-1, HEADS, HEAD)
        value_heads = key_rows[:, MODEL_WIDTH:].reshape(-1, HEADS, HEAD)
        raw_scores = low_back(jnp.einsum('qhd,khd->hqk', query_heads, key_heads, precision=lax.Precision.HIGHEST))
        scores = jnp.where(allowed[None], raw_scores * HEAD ** (-0.5), NEGATIVE)
        probs = jax.nn.softmax(scores, -1)
        mixed = jnp.einsum('hqk,khd->qhd', low(probs), value_heads, precision=lax.Precision.HIGHEST)
        return mixed.reshape(SEG, MODEL_WIDTH)
    offsets = SEG * jnp.arange(length_value // SEG, dtype=jnp.int32)
    attention_result = lax.map(jax.checkpoint(block), offsets).reshape(length_value, MODEL_WIDTH)
    attention_result = low(low_back(attention_result))
    residual = embedded + low_back(matmul(attention_result, attention_output_weight))
    ffn_input = low(layer_norm(residual, gains[:, 1]))
    pre_act = low_back(matmul(ffn_input, w_ffn_in))
    branch = low_back(matmul(low(jax.nn.gelu(pre_act)), w_ffn_out))
    output_rows = residual + branch
    final_rows = low(layer_norm(output_rows, gains[:, 2]))
    targets = jnp.concatenate([ids_row[1:], ids_row[:1]])

    def head(block_index):
        offset = block_index * SEG
        rows = lax.dynamic_slice_in_dim(final_rows, offset, SEG, 0)
        wanted = lax.dynamic_slice_in_dim(targets, offset, SEG, 0)
        scale_rows = lax.dynamic_slice_in_dim(weight_row, offset, SEG, 0)
        logits = low_back(matmul(rows, table.T))
        log_norm = jax.nn.logsumexp(logits, -1)
        picked = jnp.take_along_axis(logits, wanted[:, None], 1)[:, 0]
        return jnp.sum(scale_rows * (log_norm - picked))
    return jnp.sum(lax.map(jax.checkpoint(head), jnp.arange(length_value // SEG, dtype=jnp.int32)))

def adam_update(master, first, second, grad, rate):
    new_first = BETA_ONE * first + (1.0 - BETA_ONE) * grad
    new_second = BETA_TWO * second + (1.0 - BETA_TWO) * grad * grad
    first_hat = new_first / (1.0 - BETA_ONE ** STEP)
    second_hat = new_second / (1.0 - BETA_TWO ** STEP)
    new_master = master - rate * (first_hat / (jnp.sqrt(second_hat) + ADAM_EPSILON) + WEIGHT_DECAY * master)
    return (new_first, new_second, new_master)

def reference(token_ids, book_lengths, loss_mask, table_master, attn_in_master, attn_out_master, compress_master, ffn_in_master, ffn_out_master, gains_master, table_first, attn_in_first, attn_out_first, compress_first, ffn_in_first, ffn_out_first, gains_first, table_second, attn_in_second, attn_out_second, compress_second, ffn_in_second, ffn_out_second, gains_second):
    masters = (table_master, attn_in_master, attn_out_master, compress_master, ffn_in_master, ffn_out_master, gains_master)
    firsts = (table_first, attn_in_first, attn_out_first, compress_first, ffn_in_first, ffn_out_first, gains_first)
    seconds = (table_second, attn_in_second, attn_out_second, compress_second, ffn_in_second, ffn_out_second, gains_second)
    copies = tuple((low(master) for master in masters))
    book_ends = jnp.cumsum(book_lengths, -1).astype(jnp.int32)
    token_weight = jax.vmap(row_weights)(token_ids, loss_mask, book_ends)

    def total(weights):

        def step_row(accum, row):
            return (accum + row_loss(weights, row[0], row[1], row[2]), None)
        return lax.scan(step_row, jnp.float32(0.0), (token_ids, book_ends, token_weight))[0]
    loss, pullback = jax.vjp(total, copies)
    grads = pullback(jnp.float32(1.0))[0]
    table_out = adam_update(masters[0], firsts[0], seconds[0], grads[0], STEP_RATES[0])
    attn_in_out = adam_update(masters[1], firsts[1], seconds[1], grads[1], STEP_RATES[1])
    attn_out_out = adam_update(masters[2], firsts[2], seconds[2], grads[2], STEP_RATES[2])
    compress_out = adam_update(masters[3], firsts[3], seconds[3], grads[3], STEP_RATES[3])
    ffn_in_out = adam_update(masters[4], firsts[4], seconds[4], grads[4], STEP_RATES[4])
    ffn_out_out = adam_update(masters[5], firsts[5], seconds[5], grads[5], STEP_RATES[5])
    gains_out = adam_update(masters[6], firsts[6], seconds[6], grads[6], STEP_RATES[6])
    return (loss, table_out[0], table_out[1], table_out[2], attn_in_out[0], attn_in_out[1], attn_in_out[2], attn_out_out[0], attn_out_out[1], attn_out_out[2], compress_out[0], compress_out[1], compress_out[2], ffn_in_out[0], ffn_in_out[1], ffn_in_out[2], ffn_out_out[0], ffn_out_out[1], ffn_out_out[2], gains_out[0], gains_out[1], gains_out[2])
```

```python
import jax
import jax.numpy as jnp
from jax import lax
from jax.sharding import Mesh
from jax.sharding import PartitionSpec as P

MODEL_WIDTH = 1024
HEADS = 8
HEAD = 128
NBOOK = 8
STEP = 5

EPSILON = 1e-05
NEGATIVE = -1e30
BETA_ONE = 0.9
BETA_TWO = 0.95
ADAM_EPSILON = 1e-08
WEIGHT_DECAY = 0.1
STEP_RATES = (0.06, 0.03, 0.4, 0.02, 0.03, 0.04, 0.5)

SEQ = ("y", "x", "core")
PLANE = ("y", "x")
SHARE = ("batch", "core")
ALL = ("batch", "y", "x", "core")
BF16 = jnp.bfloat16
F32 = jnp.float32


def passed_along(value, steps):
    count = lax.axis_size(SEQ)
    initial, last = (max(0, -steps), min(count, count - steps))
    return lax.ppermute(value, SEQ, [(source, source + steps) for source in range(initial, last)])


def norm_forward(values, gain):
    center = values - jnp.mean(values, -1, keepdims=True)
    scaler = lax.rsqrt(jnp.mean(center * center, -1, keepdims=True) + EPSILON)
    unit_rows = center * scaler
    return (unit_rows * gain, unit_rows, scaler)


def norm_backward(grad_out, unit_rows, scaler, gain):
    scaled = grad_out * gain
    grad_gain = jnp.sum(grad_out * unit_rows, axis=0)
    grad_in = scaler * (
        scaled
        - jnp.mean(scaled, -1, keepdims=True)
        - unit_rows * jnp.mean(scaled * unit_rows, -1, keepdims=True)
    )
    return (grad_in, grad_gain)


def book_number(positions, book_ends):
    inside = jnp.sum((positions[:, None] >= book_ends[None, :]).astype(jnp.int32), -1)
    return jnp.where(positions < 0, -1, inside)


def matmul(left, right):
    return jnp.dot(left, right, preferred_element_type=F32)


def matmul_nt(left, right):
    return lax.dot_general(left, right, (((1,), (1,)), ((), ())), preferred_element_type=F32)


def matmul_tn(left, right):
    return lax.dot_general(left, right, (((0,), (0,)), ((), ())), preferred_element_type=F32)


def split_heads(rows):
    return rows.reshape(rows.shape[0], HEADS, HEAD)


def attention_scores(query, keys, allowed):
    scores = jnp.einsum(
        "qhd,khd->hqk", split_heads(query), split_heads(keys), preferred_element_type=F32
    ) * HEAD ** (-0.5)
    return jnp.where(allowed[None], scores, NEGATIVE)


def adam_update(master, first, second, grad, rate):
    new_first = BETA_ONE * first + (1.0 - BETA_ONE) * grad
    new_second = BETA_TWO * second + (1.0 - BETA_TWO) * grad * grad
    first_hat = new_first / (1.0 - BETA_ONE**STEP)
    second_hat = new_second / (1.0 - BETA_TWO**STEP)
    new_master = master - rate * (
        first_hat / (jnp.sqrt(second_hat) + ADAM_EPSILON) + WEIGHT_DECAY * master
    )
    return [new_first, new_second, new_master]


def bf16_parts(values):
    high = values.astype(BF16)
    rest = values - high.astype(F32)
    middle = rest.astype(BF16)
    low = (rest - middle.astype(F32)).astype(BF16)
    return high, middle, low


def per_device(token_ids, book_lengths, loss_mask, *state):
    masters, firsts, seconds = state[:7], state[7:14], state[14:]
    table_master, attn_in_m, attn_out_m, compress_m, ffn_in_m, ffn_out_m, gains_m = masters
    vocab_block = table_master.shape[0]
    batch_count = lax.axis_size("batch")
    seq_count = lax.axis_size(SEQ)
    plane_count = seq_count // 2
    share_count = batch_count * 2
    device_count = batch_count * seq_count
    segment = token_ids.shape[1]
    slots = segment // 3 + 1
    keep = segment // 2
    place = lax.axis_index(SEQ)
    offset = place * segment
    share_place = lax.axis_index(SHARE)
    width = MODEL_WIDTH

    own_tokens = token_ids.reshape(segment)
    share_tokens = lax.all_gather(own_tokens, SHARE, axis=0, tiled=True)
    table = lax.all_gather(table_master.astype(BF16), PLANE, axis=0, tiled=True)

    def vocab_place(tokens):
        block = tokens // vocab_block
        seq_index = block % seq_count
        owner = block // seq_count * 2 + seq_index % 2
        return owner, seq_index // 2 * vocab_block + tokens % vocab_block

    share_owner, share_local = vocab_place(share_tokens)
    share_row = jnp.where(share_owner == share_place, share_local, -1)
    looked = jnp.where(
        (share_row >= 0)[:, None], table[jnp.maximum(share_row, 0)], jnp.zeros((), BF16)
    )
    token_rows = lax.psum_scatter(looked, SHARE, scatter_dimension=0, tiled=True)

    rows_in = attn_in_m.size // width
    rows_out = attn_out_m.size // width
    rows_comp = compress_m.size // width
    rows_ffn = ffn_in_m.size // width
    rows_ffn_out = ffn_out_m.size // width
    gain_count = gains_m.size
    gain_block = jnp.zeros((16, width), BF16).at[0, :gain_count].set(
        gains_m.astype(BF16).reshape(-1)
    )
    mixer_block = jnp.concatenate(
        [
            attn_in_m.astype(BF16).reshape(rows_in, width),
            compress_m.astype(BF16),
            attn_out_m.astype(BF16),
            gain_block,
        ],
        0,
    )
    ffn_block = jnp.concatenate(
        [ffn_in_m.astype(BF16).reshape(rows_ffn, width), ffn_out_m.astype(BF16)], 0
    )
    mixer_all = lax.all_gather(mixer_block, ALL, axis=0, tiled=False)
    ffn_all = lax.all_gather(ffn_block, ALL, axis=0, tiled=False)
    at = 0
    w_in = mixer_all[:, at : at + rows_in].reshape(width, 3 * width)
    at += rows_in
    w_compress = mixer_all[:, at : at + rows_comp].reshape(3 * width, width)
    at += rows_comp
    w_out = mixer_all[:, at : at + rows_out].reshape(width, width)
    at += rows_out
    gains = mixer_all[:, at, :gain_count].reshape(width, 3).astype(F32)
    w_ffn_in = ffn_all[:, :rows_ffn].reshape(width, -1)
    w_ffn_out = ffn_all[:, rows_ffn:].reshape(-1, width)
    w_pairs = w_in[:, width:]

    book_ends = jnp.cumsum(book_lengths.reshape(-1))
    own_pos = offset + jnp.arange(segment, dtype=jnp.int32)
    own_book = book_number(own_pos, book_ends)
    next_book = book_number(own_pos + 1, book_ends)
    own_mask = loss_mask.reshape(segment)
    live = own_mask.astype(F32) * (next_book == own_book).astype(F32)
    member = (own_book[:, None] == jnp.arange(NBOOK, dtype=jnp.int32)[None, :]).astype(F32)
    book_counts = lax.psum(jnp.sum(member * live[:, None], 0), SEQ)
    weight = live * jnp.sum(member / jnp.maximum(book_counts, 1.0)[None, :], -1)
    following = passed_along(own_tokens[:1], -1)
    targets = jnp.concatenate([own_tokens[1:], following])
    rank = jnp.cumsum(own_mask) - 1
    chosen = (rank[None, :] == jnp.arange(keep, dtype=jnp.int32)[:, None]) & (
        own_mask[None, :] > 0
    )
    picked_targets = jnp.sum(jnp.where(chosen, targets[None, :], 0), 1)
    picked_weight = jnp.sum(jnp.where(chosen, weight[None, :], 0.0), 1)

    embedded = token_rows.astype(F32) * width**0.5
    normed_one, unit_one, scale_one = norm_forward(embedded, gains[:, 0])
    attention_input = normed_one.astype(BF16)
    projected = matmul(attention_input, w_in).astype(BF16)
    query = projected[:, :width]
    pairs = projected[:, width:]
    memory_pairs = passed_along(pairs, 1)
    tail_rows = passed_along(attention_input[segment - 2 :], 1)
    first_cell = jnp.mod(2 - offset, 3)
    extended = jnp.concatenate([tail_rows, attention_input, jnp.zeros((4, width), BF16)], 0)
    slot_rows = lax.dynamic_slice_in_dim(extended, first_cell, 3 * slots, 0).reshape(
        slots, 3 * width
    )
    compressed = matmul(slot_rows, w_compress).astype(BF16)
    comp_pairs = matmul(compressed, w_pairs).astype(BF16)
    key_parts = [pairs, memory_pairs]
    book_parts = [own_book, book_number(own_pos - segment, book_ends)]
    pos_parts = [own_pos, own_pos - segment]
    for hop in (2, 3, 4):
        key_parts.append(passed_along(comp_pairs, hop))
        owner = place - hop
        last_pos = (
            owner * segment
            + jnp.mod(2 - owner * segment, 3)
            + 3 * jnp.arange(slots, dtype=jnp.int32)
        )
        last_book = book_number(last_pos, book_ends)
        usable = (owner >= 0) & (last_pos < owner * segment + segment)
        usable = usable & (book_number(last_pos - 2, book_ends) == last_book)
        book_parts.append(jnp.where(usable, last_book, -2))
        pos_parts.append(jnp.full((slots,), -1, jnp.int32))
    key_side = jnp.concatenate(key_parts, 0)
    key_book = jnp.concatenate(book_parts)
    key_pos = jnp.concatenate(pos_parts)
    allowed = (key_book[None, :] == own_book[:, None]) & (key_pos[None, :] <= own_pos[:, None])
    value_heads = split_heads(key_side[:, width:])
    scores = attention_scores(query, key_side[:, :width], allowed)
    top_score = jnp.max(scores, -1, keepdims=True)
    log_total = top_score + jnp.log(jnp.sum(jnp.exp(scores - top_score), -1, keepdims=True))
    attn_probs = jnp.exp(scores - log_total)
    attended = jnp.einsum(
        "hqk,khd->qhd", attn_probs.astype(BF16), value_heads, preferred_element_type=F32
    )
    attended = attended.reshape(segment, width).astype(BF16)
    residual = embedded + matmul(attended, w_out)

    normed_two, unit_two, scale_two = norm_forward(residual, gains[:, 1])
    ffn_input = normed_two.astype(BF16)
    pre_act = matmul(ffn_input, w_ffn_in)
    activated, gelu_back = jax.vjp(jax.nn.gelu, pre_act)
    activated = activated.astype(BF16)
    output_rows = residual + matmul(activated, w_ffn_out)
    normed_three, unit_three, scale_three = norm_forward(output_rows, gains[:, 2])
    final_rows = normed_three.astype(BF16)

    chosen_bf16 = chosen.astype(BF16)
    picked_rows = matmul(chosen_bf16, final_rows).astype(BF16)
    high, middle, low = bf16_parts(picked_weight)
    side = jnp.concatenate(
        [
            (picked_targets // 256).astype(BF16),
            (picked_targets % 256).astype(BF16),
            high,
            middle,
            low,
        ]
    )
    side_rows = jnp.zeros((16 * width,), BF16).at[: 5 * keep].set(side).reshape(16, width)
    head_all = lax.all_gather(
        jnp.concatenate([picked_rows, side_rows], 0), SHARE, axis=0, tiled=False
    )
    rows = head_all[:, :keep].reshape(share_count * keep, width)
    side_all = head_all[:, keep:].reshape(share_count, 16 * width)[:, : 5 * keep]
    side_all = side_all.reshape(share_count, 5, keep).astype(F32)
    wanted = (side_all[:, 0] * 256.0 + side_all[:, 1]).astype(jnp.int32).reshape(-1)
    row_weight = (side_all[:, 2] + side_all[:, 3] + side_all[:, 4]).reshape(-1)
    wanted_owner, wanted_local = vocab_place(wanted)
    wanted_row = jnp.where(wanted_owner == share_place, wanted_local, -1)
    logits = matmul_nt(rows, table)
    top_logit = jnp.max(logits, -1)
    total = jnp.sum(jnp.exp(logits - top_logit[:, None]), -1)
    stats = lax.all_gather(jnp.stack([top_logit, total]), SHARE, axis=0, tiled=False)
    top_all = jnp.max(stats[:, 0], 0)
    log_norm = top_all + jnp.log(jnp.sum(stats[:, 1] * jnp.exp(stats[:, 0] - top_all[None]), 0))
    hit = wanted_row[:, None] == jnp.arange(logits.shape[1], dtype=jnp.int32)[None, :]
    target_logit = jnp.sum(jnp.where(hit, logits, 0.0), -1)
    mine = (jnp.arange(share_count * keep) // keep == share_place).astype(F32)
    loss_local = jnp.sum(row_weight * (mine * log_norm - target_logit))
    grad_logits = row_weight[:, None] * (
        jnp.exp(logits - log_norm[:, None]) - hit.astype(F32)
    )
    grad_logits = grad_logits.astype(BF16)
    grad_rows = matmul(grad_logits, table).astype(BF16)
    grad_table = matmul_tn(grad_logits, rows)
    grad_picked = lax.psum_scatter(grad_rows, SHARE, scatter_dimension=0, tiled=True)
    grad_final = matmul_tn(chosen_bf16, grad_picked)

    grad_output_rows, grad_gain_three = norm_backward(
        grad_final, unit_three, scale_three, gains[:, 2]
    )
    grad_branch = grad_output_rows.astype(BF16)
    grad_ffn_out = matmul_tn(activated, grad_branch).astype(BF16)
    grad_act = matmul_nt(grad_branch, w_ffn_out)
    grad_pre = gelu_back(grad_act)[0].astype(BF16)
    grad_ffn_in = matmul_tn(ffn_input, grad_pre).astype(BF16)
    ffn_grads = jnp.concatenate(
        [
            grad_ffn_in.reshape(device_count, rows_ffn, width),
            grad_ffn_out.reshape(device_count, rows_ffn_out, width),
        ],
        1,
    )
    ffn_grads = lax.psum_scatter(ffn_grads, ALL, scatter_dimension=0, tiled=False)
    grad_norm_two = matmul_nt(grad_pre, w_ffn_in)
    grad_res_two, grad_gain_two = norm_backward(grad_norm_two, unit_two, scale_two, gains[:, 1])
    grad_residual = grad_output_rows + grad_res_two

    grad_attn_branch = grad_residual.astype(BF16)
    grad_attn_out = matmul_tn(attended, grad_attn_branch).astype(BF16)
    grad_attended = matmul_nt(grad_attn_branch, w_out).astype(BF16)
    scores = attention_scores(query, key_side[:, :width], allowed)
    attn_probs = jnp.exp(scores - log_total)
    grad_heads = split_heads(grad_attended)
    grad_probs = jnp.einsum("qhd,khd->hqk", grad_heads, value_heads, preferred_element_type=F32)
    grad_scores = attn_probs * (grad_probs - jnp.sum(attn_probs * grad_probs, -1, keepdims=True))
    grad_scores = (grad_scores * HEAD ** (-0.5)).astype(BF16)
    grad_query = jnp.einsum(
        "hqk,khd->qhd",
        grad_scores,
        split_heads(key_side[:, :width]),
        preferred_element_type=F32,
    ).reshape(segment, width)
    grad_keys = jnp.einsum(
        "hqk,qhd->khd", grad_scores, split_heads(query), preferred_element_type=F32
    ).reshape(-1, width)
    grad_values = jnp.einsum(
        "hqk,qhd->khd", attn_probs.astype(BF16), grad_heads, preferred_element_type=F32
    ).reshape(-1, width)
    grad_pairs = jnp.concatenate([grad_keys, grad_values], -1)
    received = jnp.zeros((slots, 2 * width), F32)
    for hop in (2, 3, 4):
        first_row = 2 * segment + (hop - 2) * slots
        received = received + passed_along(
            grad_pairs[first_row : first_row + slots].astype(BF16), -hop
        ).astype(F32)
    grad_comp_pairs = received.astype(BF16)
    grad_pairs_comp = matmul_tn(compressed, grad_comp_pairs)
    grad_compressed = matmul_nt(grad_comp_pairs, w_pairs).astype(BF16)
    grad_compress = matmul_tn(slot_rows, grad_compressed).astype(BF16)
    grad_slots = matmul_nt(grad_compressed, w_compress).reshape(3 * slots, width)
    grad_extended = lax.dynamic_update_slice_in_dim(
        jnp.zeros((segment + 6, width), F32), grad_slots, first_cell, 0
    )
    back_memory = passed_along(grad_pairs[segment : 2 * segment].astype(BF16), -1).astype(F32)
    back_tail = passed_along(grad_extended[:2].astype(BF16), -1).astype(F32)
    grad_own_pairs = (grad_pairs[:segment] + back_memory).astype(BF16)
    projected_gradient = jnp.concatenate([grad_query.astype(BF16), grad_own_pairs], -1)
    grad_attn_in = matmul_tn(attention_input, projected_gradient)
    grad_attn_in = grad_attn_in + jnp.concatenate(
        [jnp.zeros((width, width), F32), grad_pairs_comp], 1
    )
    grad_input = matmul_nt(projected_gradient, w_in) + grad_extended[2 : segment + 2]
    grad_input = grad_input.at[segment - 2 :].add(back_tail)
    grad_embed, grad_gain_one = norm_backward(grad_input, unit_one, scale_one, gains[:, 0])
    grad_scaled = ((grad_embed + grad_residual) * width**0.5).astype(BF16)

    share_grads = lax.all_gather(grad_scaled, SHARE, axis=0, tiled=True)
    spread = (
        jnp.arange(table.shape[0], dtype=jnp.int32)[:, None] == share_row[None, :]
    ).astype(BF16)
    grad_table = (grad_table + matmul(spread, share_grads)).astype(BF16)
    grad_table = lax.psum_scatter(grad_table, PLANE, scatter_dimension=0, tiled=True)

    mixer_grads = jnp.concatenate(
        [
            grad_attn_in.astype(BF16).reshape(device_count, rows_in, width),
            grad_compress.reshape(device_count, rows_comp, width),
            grad_attn_out.reshape(device_count, rows_out, width),
        ],
        1,
    )
    mixer_grads = lax.psum_scatter(mixer_grads, ALL, scatter_dimension=0, tiled=False)
    small = jnp.concatenate(
        [
            jnp.stack([grad_gain_one, grad_gain_two, grad_gain_three], 1).reshape(-1),
            jnp.full((128,), loss_local, F32),
        ]
    )
    small = lax.psum(small, ALL)
    loss_total = small[3 * width]
    device = lax.axis_index(ALL)
    gain_grads = lax.dynamic_slice_in_dim(small, device * gain_count, gain_count, 0)
    grads = (
        grad_table,
        mixer_grads[:rows_in].reshape(attn_in_m.shape),
        mixer_grads[rows_in + rows_comp :].reshape(attn_out_m.shape),
        mixer_grads[rows_in : rows_in + rows_comp].reshape(compress_m.shape),
        ffn_grads[:rows_ffn].reshape(ffn_in_m.shape),
        ffn_grads[rows_ffn:].reshape(ffn_out_m.shape),
        gain_grads.reshape(gains_m.shape),
    )
    results = []
    for master, first, second, grad, rate in zip(masters, firsts, seconds, grads, STEP_RATES):
        results.extend(adam_update(master, first, second, grad.astype(F32), rate))
    return (loss_total,) + tuple(results)


def solution(mesh):
    batch_count, seq_count = mesh.shape["batch"], mesh.shape["seq"]
    devices = mesh.devices.reshape(batch_count, seq_count // 4, 2, 2)
    grid = Mesh(devices, ALL)
    rows = P(ALL, None)
    return jax.shard_map(
        per_device,
        mesh=grid,
        in_specs=(P("batch", SEQ), P("batch", None), P("batch", SEQ)) + (rows,) * 21,
        out_specs=(P(),) + (rows,) * 21,
        check_vma=False,
    )
```

```python
import jax
import jax.numpy as jnp
from jax import lax
from jax.experimental import pallas as pl
from jax.experimental.pallas import tpu as pltpu
from jax.sharding import Mesh
from jax.sharding import PartitionSpec as P

MODEL_WIDTH = 1024
HEADS = 8
HEAD = 128
NBOOK = 8
STEP = 5

EPSILON = 1e-05
NEGATIVE = -1e30
BETA_ONE = 0.9
BETA_TWO = 0.95
ADAM_EPSILON = 1e-08
WEIGHT_DECAY = 0.1
STEP_RATES = (0.06, 0.03, 0.4, 0.02, 0.03, 0.04, 0.5)

SEQ = ("far", "y", "x", "core")
PLANE = ("far", "y", "x")
SHARE = ("batch", "core")
LINE = ("batch", "far")
ALL = ("batch", "far", "y", "x", "core")
PIECE = 512
BLOCK = 128
GROUPS = 32
BF16 = jnp.bfloat16
F32 = jnp.float32


def passed_along(value, steps):
    count = lax.axis_size(SEQ)
    initial, last = (max(0, -steps), min(count, count - steps))
    return lax.ppermute(value, SEQ, [(source, source + steps) for source in range(initial, last)])


def norm_forward(values, gain):
    center = values - jnp.mean(values, -1, keepdims=True)
    scaler = lax.rsqrt(jnp.mean(center * center, -1, keepdims=True) + EPSILON)
    unit_rows = center * scaler
    return (unit_rows * gain, unit_rows, scaler)


def norm_backward(grad_out, unit_rows, scaler, gain):
    scaled = grad_out * gain
    grad_gain = jnp.sum(grad_out * unit_rows, axis=0)
    grad_in = scaler * (
        scaled
        - jnp.mean(scaled, -1, keepdims=True)
        - unit_rows * jnp.mean(scaled * unit_rows, -1, keepdims=True)
    )
    return (grad_in, grad_gain)


def book_number(positions, book_ends):
    inside = jnp.sum((positions[:, None] >= book_ends[None, :]).astype(jnp.int32), -1)
    return jnp.where(positions < 0, -1, inside)


def matmul(left, right):
    return jnp.dot(left, right, preferred_element_type=F32)


def matmul_nt(left, right):
    return lax.dot_general(left, right, (((1,), (1,)), ((), ())), preferred_element_type=F32)


def matmul_tn(left, right):
    return lax.dot_general(left, right, (((0,), (0,)), ((), ())), preferred_element_type=F32)


def fill_bias(bias, key_book, key_pos, query_book, query_pos):
    allowed = (key_book[...] == query_book[...]) & (key_pos[...] <= query_pos[...])
    bias[...] = jnp.where(allowed, 0.0, NEGATIVE)


def attention_forward_body(*refs):
    query, own_k, own_v, mem_k, mem_v = refs[:5]
    marks, (out, log_total, bias) = refs[5:9], refs[9:]

    @pl.when(pl.program_id(0) == 0)
    def _():
        fill_bias(bias, *marks)

    keys = jnp.concatenate([own_k[...], mem_k[...]], 0)
    values = jnp.concatenate([own_v[...], mem_v[...]], 0)
    scores = matmul_nt(keys, query[...]) * HEAD ** (-0.5) + bias[...]
    top = jnp.max(scores, 0, keepdims=True)
    probs = jnp.exp(scores - top)
    total = jnp.sum(probs, 0, keepdims=True)
    log_total[0] = top + jnp.log(total)
    probs = (probs * (1.0 / total)).astype(BF16)
    out[...] = matmul_tn(values, probs).T.astype(BF16)


def attention_backward_body(*refs):
    query, own_k, own_v, mem_k, mem_v = refs[:5]
    marks = refs[5:9]
    log_total, grad_out, grad_query, grad_own, grad_mem, g2, g3, g4, bias = refs[9:]

    @pl.when(pl.program_id(0) == 0)
    def _():
        fill_bias(bias, *marks)

    keys = jnp.concatenate([own_k[...], mem_k[...]], 0)
    values = jnp.concatenate([own_v[...], mem_v[...]], 0)
    scores = matmul_nt(keys, query[...]) * HEAD ** (-0.5) + bias[...]
    probs = jnp.exp(scores - log_total[0])
    grad_probs = matmul_nt(values, grad_out[...])
    inner = jnp.sum(probs * grad_probs, 0, keepdims=True)
    grad_scores = (probs * (grad_probs - inner) * HEAD ** (-0.5)).astype(BF16)
    grad_query[...] = matmul_tn(keys, grad_scores).T.astype(BF16)
    pair = (matmul(grad_scores, query[...]), matmul(probs.astype(BF16), grad_out[...]))
    at = 0
    for part in (grad_own, grad_mem, g2, g3, g4):
        count = part.shape[1]
        for side in (0, 1):
            part[side] = pair[side][at : at + count].astype(part.dtype)
        at += count


def attention_specs(segment, others):
    def column(rows, shift):
        return pl.BlockSpec((rows, HEAD), lambda h: (0, h + shift * HEADS))

    mark_k = pl.BlockSpec((segment + others, 1), lambda h: (0, 0))
    mark_q = pl.BlockSpec((1, segment), lambda h: (0, 0))
    specs = [column(segment, 0), column(segment, 1), column(segment, 2)]
    specs += [column(others, 0), column(others, 1)]
    return specs + [mark_k, mark_k, mark_q, mark_q]


def attention_forward(projected, memory, marks):
    segment, others = projected.shape[0], memory.shape[0]
    keys = segment + others
    return pl.pallas_call(
        attention_forward_body,
        grid=(HEADS,),
        in_specs=attention_specs(segment, others),
        out_specs=[
            pl.BlockSpec((segment, HEAD), lambda h: (0, h)),
            pl.BlockSpec((1, 1, segment), lambda h: (h, 0, 0)),
        ],
        out_shape=[
            jax.ShapeDtypeStruct((segment, HEADS * HEAD), BF16),
            jax.ShapeDtypeStruct((HEADS, 1, segment), F32),
        ],
        scratch_shapes=[pltpu.VMEM((keys, segment), F32)],
        compiler_params=pltpu.CompilerParams(vmem_limit_bytes=48 << 20),
        cost_estimate=pl.CostEstimate(
            flops=4 * HEADS * keys * segment * HEAD,
            bytes_accessed=12 << 20,
            transcendentals=HEADS * keys * segment,
        ),
        name="attention_forward",
    )(projected, projected, projected, memory, memory, *marks)


def attention_backward(projected, memory, marks, log_total, grad_out):
    segment, others = projected.shape[0], memory.shape[0]
    keys, slots = segment + others, (others - segment) // 3
    width = HEADS * HEAD

    def pair_spec(rows):
        return pl.BlockSpec((2, rows, HEAD), lambda h: (0, 0, h))

    return pl.pallas_call(
        attention_backward_body,
        grid=(HEADS,),
        in_specs=attention_specs(segment, others)
        + [
            pl.BlockSpec((1, 1, segment), lambda h: (h, 0, 0)),
            pl.BlockSpec((segment, HEAD), lambda h: (0, h)),
        ],
        out_specs=[pl.BlockSpec((segment, HEAD), lambda h: (0, h))]
        + [pair_spec(segment)] * 2
        + [pair_spec(slots)] * 3,
        out_shape=[
            jax.ShapeDtypeStruct((segment, width), BF16),
            jax.ShapeDtypeStruct((2, segment, width), F32),
            jax.ShapeDtypeStruct((2, segment, width), BF16),
        ]
        + [jax.ShapeDtypeStruct((2, slots, width), BF16)] * 3,
        scratch_shapes=[pltpu.VMEM((keys, segment), F32)],
        compiler_params=pltpu.CompilerParams(vmem_limit_bytes=48 << 20),
        cost_estimate=pl.CostEstimate(
            flops=10 * HEADS * keys * segment * HEAD,
            bytes_accessed=24 << 20,
            transcendentals=HEADS * keys * segment,
        ),
        name="attention_backward",
    )(projected, projected, projected, memory, memory, *marks, log_total, grad_out)


def adam_update(master, first, second, grad, rate):
    new_first = BETA_ONE * first + (1.0 - BETA_ONE) * grad
    new_second = BETA_TWO * second + (1.0 - BETA_TWO) * grad * grad
    first_hat = new_first / (1.0 - BETA_ONE**STEP)
    second_hat = new_second / (1.0 - BETA_TWO**STEP)
    new_master = master - rate * (
        first_hat / (jnp.sqrt(second_hat) + ADAM_EPSILON) + WEIGHT_DECAY * master
    )
    return [new_first, new_second, new_master]


def swapped(value, axis):
    return lax.ppermute(value, axis, [(0, 1), (1, 0)])


def grouped(buffer, sections):
    if buffer.shape[0] == GROUPS:
        return buffer
    parts, at = [], 0
    for count in sections:
        parts.append(buffer[:, at : at + count].reshape(GROUPS, -1, buffer.shape[2]))
        at += count
    return jnp.concatenate(parts, 1)


def matmul_packed(value, buffer, rows, first, count):
    size, depth = value.shape

    def body(value_ref, weight_ref, out):
        weight = weight_ref[...].reshape(depth, PIECE)
        out[...] = matmul(value_ref[...], weight).astype(BF16)

    return pl.pallas_call(
        body,
        grid=(count, 2),
        in_specs=[
            pl.BlockSpec((size, depth), lambda j, h: (0, 0)),
            pl.BlockSpec((GROUPS, rows, PIECE), lambda j, h: (0, first + j, h)),
        ],
        out_specs=pl.BlockSpec((size, PIECE), lambda j, h: (0, 2 * j + h)),
        out_shape=jax.ShapeDtypeStruct((size, count * 2 * PIECE), BF16),
        compiler_params=pltpu.CompilerParams(vmem_limit_bytes=48 << 20),
        cost_estimate=pl.CostEstimate(
            flops=4 * size * depth * count * PIECE,
            bytes_accessed=2 * depth * count * 1024,
            transcendentals=0,
        ),
        name="matmul_packed",
    )(value, buffer)


def matmul_packed_back(grads, buffer, rows, first, start=None):
    count, size, width = grads.shape
    depth = GROUPS * rows
    extra = [] if start is None else [start]

    def body(grad_ref, weight_ref, *rest):
        out = rest[-1]

        @pl.when(pl.program_id(0) == 0)
        def _():
            out[...] = jnp.zeros(out.shape, F32) if start is None else rest[0][...]

        out[...] += matmul_nt(grad_ref[0], weight_ref[...].reshape(depth, width))

    return pl.pallas_call(
        body,
        grid=(count,),
        in_specs=[
            pl.BlockSpec((1, size, width), lambda j: (j, 0, 0)),
            pl.BlockSpec((GROUPS, rows, width), lambda j: (0, first + j, 0)),
        ]
        + [pl.BlockSpec((size, depth), lambda j: (0, 0)) for _ in extra],
        out_specs=pl.BlockSpec((size, depth), lambda j: (0, 0)),
        out_shape=jax.ShapeDtypeStruct((size, depth), F32),
        compiler_params=pltpu.CompilerParams(vmem_limit_bytes=48 << 20),
        cost_estimate=pl.CostEstimate(
            flops=2 * size * depth * count * width,
            bytes_accessed=2 * depth * count * width,
            transcendentals=0,
        ),
        name="matmul_packed_back",
    )(grads, buffer, *extra)


GELU_SCALE = 0.7978845608028654
GELU_CUBE = 0.044715


def feed_forward(value, buffer, residual, chunk):
    size, width = value.shape
    blocks = (buffer.shape[1] - BLOCK) * GROUPS // width
    lines = width // (8 * chunk)

    def body(value_ref, first_ref, second_ref, residual_ref, out, pre, turned):
        hidden = matmul(value_ref[...], first_ref[...].reshape(width, width))
        pre[...] = hidden
        inner = jnp.tanh(GELU_SCALE * (hidden + GELU_CUBE * hidden * hidden * hidden))
        active = (0.5 * hidden * (1.0 + inner)).astype(BF16)

        @pl.when(pl.program_id(0) == 0)
        def _():
            out[...] = residual_ref[...]

        out[...] += matmul(active, second_ref[...].reshape(width, width))
        columns = active.T
        for line in range(lines):
            for place in range(8):
                target = place % 2 * 4 + place // 2
                at = (line * 8 + place) * chunk
                turned[target, line * chunk : (line + 1) * chunk] = columns[at : at + chunk]

    return pl.pallas_call(
        body,
        grid=(blocks,),
        in_specs=[
            pl.BlockSpec((size, width), lambda j: (0, 0)),
            pl.BlockSpec((GROUPS, width // GROUPS, width), lambda j: (0, j, 0)),
            pl.BlockSpec((width // BLOCK, BLOCK, width), lambda j: (j, 1, 0)),
            pl.BlockSpec((size, width), lambda j: (0, 0)),
        ],
        out_specs=[
            pl.BlockSpec((size, width), lambda j: (0, 0)),
            pl.BlockSpec((size, width), lambda j: (0, j)),
            pl.BlockSpec((8, width // 8, size), lambda j: (0, j, 0)),
        ],
        out_shape=[
            jax.ShapeDtypeStruct((size, width), F32),
            jax.ShapeDtypeStruct((size, blocks * width), F32),
            jax.ShapeDtypeStruct((8, blocks * width // 8, size), BF16),
        ],
        compiler_params=pltpu.CompilerParams(vmem_limit_bytes=56 << 20),
        cost_estimate=pl.CostEstimate(
            flops=4 * size * width * width * blocks,
            bytes_accessed=32 << 20,
            transcendentals=size * width * blocks,
        ),
        name="feed_forward",
    )(value, buffer, buffer, residual)


def feed_forward_back(grad, pre, buffer):
    size, width = grad.shape
    blocks = pre.shape[1] // width

    def body(grad_ref, pre_ref, first_ref, second_ref, grad_pre, out):
        grad_active = matmul_nt(grad_ref[...], second_ref[...].reshape(width, width))
        hidden = pre_ref[...]
        square = hidden * hidden
        inner = jnp.tanh(GELU_SCALE * hidden * (1.0 + GELU_CUBE * square))
        slope = 0.5 * (1.0 + inner) + 0.5 * hidden * (1.0 - inner * inner) * GELU_SCALE * (
            1.0 + 3.0 * GELU_CUBE * square
        )
        back = (grad_active * slope).astype(BF16)
        grad_pre[...] = back

        @pl.when(pl.program_id(0) == 0)
        def _():
            out[...] = jnp.zeros(out.shape, F32)

        out[...] += matmul_nt(back, first_ref[...].reshape(width, width))

    return pl.pallas_call(
        body,
        grid=(blocks,),
        in_specs=[
            pl.BlockSpec((size, width), lambda j: (0, 0)),
            pl.BlockSpec((size, width), lambda j: (0, j)),
            pl.BlockSpec((GROUPS, width // GROUPS, width), lambda j: (0, j, 0)),
            pl.BlockSpec((width // BLOCK, BLOCK, width), lambda j: (j, 1, 0)),
        ],
        out_specs=[
            pl.BlockSpec((size, width), lambda j: (0, j)),
            pl.BlockSpec((size, width), lambda j: (0, 0)),
        ],
        out_shape=[
            jax.ShapeDtypeStruct((size, blocks * width), BF16),
            jax.ShapeDtypeStruct((size, width), F32),
        ],
        compiler_params=pltpu.CompilerParams(vmem_limit_bytes=56 << 20),
        cost_estimate=pl.CostEstimate(
            flops=4 * size * width * width * blocks,
            bytes_accessed=32 << 20,
            transcendentals=size * width * blocks,
        ),
        name="feed_forward_back",
    )(grad, pre, buffer, buffer)


def grouped_transpose(rows):
    tokens, columns = rows.shape
    line = lax.axis_size(LINE)
    split = rows.reshape(tokens, line, 2, 2, 2, columns // (line * 8))
    return split.transpose(4, 2, 3, 1, 5, 0).reshape(8, columns // 8, tokens)


def core_halves(grouped):
    core = lax.axis_index("core")
    mine = lax.dynamic_slice_in_dim(grouped, 4 * core, 4, 0)
    other = lax.dynamic_slice_in_dim(grouped, 4 * (1 - core), 4, 0)
    return mine, swapped(other, "core")


def gradient_piece(weights, place, half, axis, moved, dtype):
    operands, specs, plan = [], [], []
    first = 0
    for products, blocks, wide in weights:
        for own, other, rhs_own, rhs_other, lead in products:
            tokens = own.shape[2]

            def inner(step, first=first, blocks=blocks):
                return jnp.clip(step - first, 0, blocks - 1)

            for side in (own, other):
                for free in (0, 1):
                    flip = 2 * free + moved if axis == "x" else 2 * moved + free

                    def lhs_map(step, me, flip=flip, inner=inner, wide=wide):
                        return (me[0] ^ flip, 0 if wide else inner(step), 0)

                    operands.append(side)
                    specs.append(pl.BlockSpec((1, BLOCK, tokens), lhs_map))
            for side in (rhs_own, rhs_other):

                def rhs_map(step, me, inner=inner, wide=wide, lead=lead):
                    return (lead, 0, 2 * inner(step) + half if wide else half)

                operands.append(side)
                specs.append(pl.BlockSpec((1, tokens, PIECE), rhs_map))
        plan.append((first, blocks, len(products)))
        first += blocks

    def body(me, *refs):
        out = refs[-1]
        step = pl.program_id(0)
        at = 0
        for start, blocks, count in plan:
            group = refs[at : at + 6 * count]

            @pl.when((step >= start) & (step < start + blocks))
            def _():
                total = jnp.zeros((2 * BLOCK, PIECE), F32)
                for k in range(0, 6 * count, 6):
                    near = jnp.concatenate([group[k][0], group[k + 1][0]], 0)
                    far = jnp.concatenate([group[k + 2][0], group[k + 3][0]], 0)
                    total += matmul(near, group[k + 4][0]) + matmul(far, group[k + 5][0])
                out[0] = total.astype(out.dtype)

            at += 6 * count

    return pl.pallas_call(
        body,
        grid_spec=pltpu.PrefetchScalarGridSpec(
            num_scalar_prefetch=1,
            grid=(first,),
            in_specs=specs,
            out_specs=pl.BlockSpec((1, 2 * BLOCK, PIECE), lambda step, me: (step, 0, 0)),
        ),
        out_shape=jax.ShapeDtypeStruct((first, 2 * BLOCK, PIECE), dtype),
        compiler_params=pltpu.CompilerParams(vmem_limit_bytes=40 << 20),
        cost_estimate=pl.CostEstimate(
            flops=first * 2 * 2 * BLOCK * PIECE * 1024,
            bytes_accessed=first * (3 << 20),
            transcendentals=0,
        ),
        name="gradient_piece",
    )(place, *operands)


def line_scatter(value):
    count = lax.axis_size(LINE)
    index = lax.axis_index(LINE)
    total = lax.dynamic_index_in_dim(value, index, 0, False)
    upward = downward = jnp.zeros(total.shape, F32)
    for steps in range(count - 1, 0, -1):
        above = lax.dynamic_index_in_dim(value, jnp.minimum(index + steps, count - 1), 0, False)
        below = lax.dynamic_index_in_dim(value, jnp.maximum(index - steps, 0), 0, False)
        up = [(i, i + 1) for i in range(count - steps)]
        down = [(i, i - 1) for i in range(steps, count)]
        upward = lax.ppermute((above + upward).astype(BF16), LINE, up).astype(F32)
        downward = lax.ppermute((below + downward).astype(BF16), LINE, down).astype(F32)
    return total + upward + downward


def chip_place():
    place = lax.axis_index("y") * 2 + lax.axis_index("x")
    return jnp.reshape(place, (1,)).astype(jnp.int32)


def gradient_sends(weights):
    return [
        gradient_piece(weights, chip_place(), 0, "x", 1, BF16),
        gradient_piece(weights, chip_place(), 1, "y", 1, BF16),
    ]


def gradient_keeps(weights):
    return [
        gradient_piece(weights, chip_place(), 0, "x", 0, F32),
        gradient_piece(weights, chip_place(), 1, "y", 0, F32),
    ]


def plane_sums(sends, keeps):
    result = []
    for arrived, keep in zip(sends, keeps):
        count = keep.shape[1] // 2
        other = (keep[:, count:] + arrived[:, count:].astype(F32)).astype(BF16)
        result.append((keep[:, :count] + arrived[:, :count].astype(F32), other))
    return result


def line_parts(weights, sums):
    line = lax.axis_size(LINE)
    joined = [
        mine + swapped(other, axis).astype(F32) for (mine, other), axis in zip(sums, ("y", "x"))
    ]
    first, chunks = 0, []
    for weight in weights:
        blocks, wide = weight[1:]
        for part in range(blocks if wide else 1):
            count = 1 if wide else blocks
            pair = [
                half[first : first + count].reshape(line, count * BLOCK // line, PIECE)
                for half in joined
            ]
            chunks.append(jnp.concatenate(pair, -1))
            first += count
    return jnp.concatenate(chunks, 1)


def small_sum(value):
    for axis in ("core", "x", "y"):
        value = value + swapped(value, axis)
    count = lax.axis_size(LINE)
    step = 1
    while step < count:
        pairs = [(i, i ^ step) for i in range(count)]
        value = value + lax.ppermute(value, LINE, pairs)
        step *= 2
    return value


def spread_body(row_of, token_row, grads, table_grad, *refs):
    outs, total = refs[:2], refs[2]
    task, step = pl.program_id(0), pl.program_id(1)
    rows, tokens = total.shape[0], grads.shape[0]
    first = row_of(task) * rows

    @pl.when(step == 0)
    def _():
        total[...] = table_grad[0]

    wanted = token_row[...] - first
    hit = lax.broadcasted_iota(jnp.int32, (rows, tokens), 0) == wanted
    total[...] += matmul(jnp.where(hit, 1.0, 0.0).astype(BF16), grads[...])

    for side in (0, 1):

        @pl.when((step == pl.num_programs(1) - 1) & (task // 2 == side))
        def _():
            outs[side][0] = total[...].astype(outs[side].dtype)


def spread_piece(token_row, grads, table_grad, row_of, dtype):
    blocks, rows, width = table_grad.shape
    tokens = 1024

    def body(*refs):
        spread_body(row_of, *refs)

    return pl.pallas_call(
        body,
        grid=(4, grads.shape[0] // tokens),
        in_specs=[
            pl.BlockSpec((1, tokens), lambda task, step: (0, step)),
            pl.BlockSpec((tokens, PIECE), lambda task, step: (step, task // 2)),
            pl.BlockSpec((1, rows, PIECE), lambda task, step: (row_of(task), 0, task // 2)),
        ],
        out_specs=[
            pl.BlockSpec((1, rows, PIECE), lambda task, step: (jnp.minimum(task, 1), 0, 0)),
            pl.BlockSpec((1, rows, PIECE), lambda task, step: (jnp.maximum(task - 2, 0), 0, 0)),
        ],
        out_shape=[jax.ShapeDtypeStruct((2, rows, PIECE), dtype)] * 2,
        scratch_shapes=[pltpu.VMEM((rows, PIECE), F32)],
        compiler_params=pltpu.CompilerParams(vmem_limit_bytes=48 << 20),
        cost_estimate=pl.CostEstimate(
            flops=4 * 2 * rows * PIECE * grads.shape[0],
            bytes_accessed=24 << 20,
            transcendentals=0,
        ),
        name="spread_piece",
    )(token_row, grads, table_grad)


def column_blocks(rows):
    return jnp.concatenate(jnp.split(rows, rows.shape[1] // MODEL_WIDTH, 1), 0)


def bf16_parts(values):
    high = values.astype(BF16)
    rest = values - high.astype(F32)
    middle = rest.astype(BF16)
    low = (rest - middle.astype(F32)).astype(BF16)
    return high, middle, low


def per_device(token_ids, book_lengths, loss_mask, *state):
    masters, firsts, seconds = state[:7], state[7:14], state[14:]
    table_master, attn_in_m, attn_out_m, compress_m, ffn_in_m, ffn_out_m, gains_m = masters
    vocab_block = table_master.shape[0]
    batch_count = lax.axis_size("batch")
    seq_count = lax.axis_size(SEQ)
    plane_count = seq_count // 2
    share_count = batch_count * 2
    device_count = batch_count * seq_count
    segment = token_ids.shape[1]
    slots = -(-(segment // 3 + 1) // 16) * 16
    keep = segment // 2
    place = lax.axis_index(SEQ)
    offset = place * segment
    share_place = lax.axis_index(SHARE)
    width = MODEL_WIDTH

    own_tokens = token_ids.reshape(segment)
    share_tokens = lax.all_gather(own_tokens, SHARE, axis=0, tiled=True)
    own_table = lax.all_gather(table_master.astype(BF16), "far", axis=0, tiled=True)
    table_x, table_y = swapped(own_table, "x"), swapped(own_table, "y")
    part_rows = own_table.shape[0]
    table = jnp.zeros((4 * part_rows, width), BF16)
    for value, row, column in (
        (own_table, 0, 0),
        (table_x, 1, 0),
        (table_y, 2, 0),
        (swapped(table_x[:, :PIECE], "y"), 3, 0),
        (swapped(table_y[:, PIECE:], "x"), 3, PIECE),
    ):
        table = lax.dynamic_update_slice(table, value, (row * part_rows, column))

    def vocab_place(tokens):
        block = tokens // vocab_block
        seq_index = block % seq_count
        owner = block // seq_count * 2 + seq_index % 2
        chip = seq_index // 2 % 4
        part = chip ^ (lax.axis_index("y") * 2 + lax.axis_index("x"))
        inside = seq_index // 8 * vocab_block + tokens % vocab_block
        return owner, part * part_rows + inside

    share_owner, share_local = vocab_place(share_tokens)
    share_row = jnp.where(share_owner == share_place, share_local, -1)
    looked = jnp.where(
        (share_row >= 0)[:, None], table[jnp.maximum(share_row, 0)], jnp.zeros((), BF16)
    )

    rows_in = attn_in_m.size // width
    rows_out = attn_out_m.size // width
    rows_comp = compress_m.size // width
    rows_ffn = ffn_in_m.size // width
    rows_ffn_out = ffn_out_m.size // width
    gain_count = gains_m.size
    gain_block = jnp.zeros((16, width), BF16).at[0, :gain_count].set(
        gains_m.astype(BF16).reshape(-1)
    )
    mixer_block = jnp.concatenate(
        [
            column_blocks(attn_in_m.astype(BF16)),
            compress_m.astype(BF16),
            attn_out_m.astype(BF16),
            gain_block,
        ],
        0,
    )
    ffn_block = jnp.concatenate(
        [column_blocks(ffn_in_m.astype(BF16)), ffn_out_m.astype(BF16)], 0
    )
    mixer_all = lax.all_gather(mixer_block, ALL, axis=0, tiled=False)
    ffn_all = lax.all_gather(ffn_block, ALL, axis=0, tiled=False)
    token_rows = lax.psum_scatter(looked, SHARE, scatter_dimension=0, tiled=True)
    gains = mixer_all[:, rows_in + rows_comp + rows_out, :gain_count]
    gains = gains.reshape(width, 3).astype(F32)
    part = attn_in_m.shape[0]
    mixer_all = grouped(mixer_all, (part, part, part, rows_comp, rows_out, 16))
    ffn_all = grouped(ffn_all, (part,) * (rows_ffn // part) + (rows_ffn_out,))
    thin = width // GROUPS

    book_ends = jnp.cumsum(book_lengths.reshape(-1))
    own_pos = offset + jnp.arange(segment, dtype=jnp.int32)
    own_book = book_number(own_pos, book_ends)
    next_book = book_number(own_pos + 1, book_ends)
    own_mask = loss_mask.reshape(segment)
    numbers = jnp.arange(NBOOK, dtype=jnp.int32)
    live = own_mask.astype(F32) * (next_book == own_book).astype(F32)
    member = (own_book[:, None] == numbers[None, :]).astype(F32)
    book_counts = jnp.sum(member * live[:, None], 0)
    for axis in ("core", "x", "y"):
        book_counts = book_counts + swapped(book_counts, axis)
    book_counts = lax.psum(book_counts, "far")
    weight = live * jnp.sum(member / jnp.maximum(book_counts, 1.0)[None, :], -1)
    following = passed_along(own_tokens[:1], -1)
    targets = jnp.concatenate([own_tokens[1:], following])
    rank = jnp.cumsum(own_mask) - 1
    chosen = (rank[None, :] == jnp.arange(keep, dtype=jnp.int32)[:, None]) & (
        own_mask[None, :] > 0
    )
    picked_targets = jnp.sum(jnp.where(chosen, targets[None, :], 0), 1)
    picked_weight = jnp.sum(jnp.where(chosen, weight[None, :], 0.0), 1)

    embedded = token_rows.astype(F32) * width**0.5
    normed_one, unit_one, scale_one = norm_forward(embedded, gains[:, 0])
    attention_input = normed_one.astype(BF16)
    projected = matmul_packed(attention_input, mixer_all, thin, 0, 3)
    memory_rows = passed_along(attention_input, 1)
    tail_rows = passed_along(attention_input[segment - 2 :], 1)
    first_cell = jnp.mod(2 - offset, 3)
    padding = 3 * slots - segment + 2
    extended = jnp.concatenate([tail_rows, attention_input, jnp.zeros((padding, width), BF16)], 0)
    slot_rows = lax.dynamic_slice_in_dim(extended, first_cell, 3 * slots, 0).reshape(
        slots, 3 * width
    )
    compressed = matmul_packed(slot_rows, mixer_all, 3 * thin, 1, 1)
    other_rows = [memory_rows]
    book_parts = [own_book, book_number(own_pos - segment, book_ends)]
    pos_parts = [own_pos, own_pos - segment]
    for hop in (2, 3, 4):
        other_rows.append(passed_along(compressed, hop))
        owner = place - hop
        last_pos = (
            owner * segment
            + jnp.mod(2 - owner * segment, 3)
            + 3 * jnp.arange(slots, dtype=jnp.int32)
        )
        last_book = book_number(last_pos, book_ends)
        usable = (owner >= 0) & (last_pos < owner * segment + segment)
        usable = usable & (book_number(last_pos - 2, book_ends) == last_book)
        book_parts.append(jnp.where(usable, last_book, -2))
        pos_parts.append(jnp.full((slots,), -1, jnp.int32))
    marks = (
        jnp.concatenate(book_parts)[:, None],
        jnp.concatenate(pos_parts)[:, None],
        own_book[None, :],
        own_pos[None, :],
    )
    memory_pairs = matmul_packed(jnp.concatenate(other_rows, 0), mixer_all, thin, 1, 2)
    attended, log_total = attention_forward(projected, memory_pairs, marks)
    w_out = mixer_all[:, 6 * thin : 7 * thin].reshape(width, width)
    residual = embedded + matmul(attended, w_out)

    normed_two, unit_two, scale_two = norm_forward(residual, gains[:, 1])
    ffn_input = normed_two.astype(BF16)
    output_rows, pre_act, activated_turned = feed_forward(
        ffn_input, ffn_all, residual, rows_ffn_out
    )
    normed_three, unit_three, scale_three = norm_forward(output_rows, gains[:, 2])
    final_rows = normed_three.astype(BF16)

    chosen_bf16 = chosen.astype(BF16)
    picked_rows = matmul(chosen_bf16, final_rows).astype(BF16)
    high, middle, low = bf16_parts(picked_weight)
    side = jnp.concatenate(
        [
            (picked_targets // 256).astype(BF16),
            (picked_targets % 256).astype(BF16),
            high,
            middle,
            low,
        ]
    )
    side_rows = jnp.zeros((16 * width,), BF16).at[: 5 * keep].set(side).reshape(16, width)
    head_all = lax.all_gather(
        jnp.concatenate([picked_rows, side_rows], 0), SHARE, axis=0, tiled=False
    )
    spare = -slots % BLOCK
    comp_tall = jnp.concatenate([compressed, jnp.zeros((spare, width), BF16)], 0)
    slot_tall = jnp.concatenate([slot_rows, jnp.zeros((spare, 3 * width), BF16)], 0)
    halves = [
        core_halves(value)
        for value in (
            grouped_transpose(ffn_input),
            activated_turned,
            grouped_transpose(attention_input),
            grouped_transpose(comp_tall),
            grouped_transpose(slot_tall),
            grouped_transpose(attended),
        )
    ]
    rows = head_all[:, :keep].reshape(share_count * keep, width)
    rows, halves = lax.optimization_barrier((rows, halves))
    side_all = head_all[:, keep:].reshape(share_count, 16 * width)[:, : 5 * keep]
    side_all = side_all.reshape(share_count, 5, keep).astype(F32)
    wanted = (side_all[:, 0] * 256.0 + side_all[:, 1]).astype(jnp.int32).reshape(-1)
    row_weight = (side_all[:, 2] + side_all[:, 3] + side_all[:, 4]).reshape(-1)
    wanted_owner, wanted_local = vocab_place(wanted)
    wanted_row = jnp.where(wanted_owner == share_place, wanted_local, -1)
    logits = matmul_nt(rows, table)
    top_logit = jnp.max(logits, -1)
    total = jnp.sum(jnp.exp(logits - top_logit[:, None]), -1)
    stats = lax.all_gather(jnp.stack([top_logit, total]), SHARE, axis=0, tiled=False)
    top_all = jnp.max(stats[:, 0], 0)
    log_norm = top_all + jnp.log(jnp.sum(stats[:, 1] * jnp.exp(stats[:, 0] - top_all[None]), 0))
    hit = wanted_row[:, None] == jnp.arange(logits.shape[1], dtype=jnp.int32)[None, :]
    target_logit = jnp.sum(jnp.where(hit, logits, 0.0), -1)
    mine = (jnp.arange(share_count * keep) // keep == share_place).astype(F32)
    loss_local = jnp.sum(row_weight * (mine * log_norm - target_logit))
    grad_logits = row_weight[:, None] * (
        jnp.exp(logits - log_norm[:, None]) - hit.astype(F32)
    )
    grad_logits = grad_logits.astype(BF16)
    grad_rows = matmul(grad_logits, table).astype(BF16)
    grad_table = matmul_tn(grad_logits, rows)
    grad_picked = lax.psum_scatter(grad_rows, SHARE, scatter_dimension=0, tiled=True)
    grad_picked, grad_table = lax.optimization_barrier((grad_picked, grad_table))
    grad_final = matmul_tn(chosen_bf16, grad_picked)

    grad_output_rows, grad_gain_three = norm_backward(
        grad_final, unit_three, scale_three, gains[:, 2]
    )
    grad_branch = grad_output_rows.astype(BF16)
    grad_pre, grad_norm_two = feed_forward_back(grad_branch, pre_act, ffn_all)

    def product(pair, grad, lead=0):
        return pair + (grad[0], grad[1], lead)

    def with_other(grad):
        grad = grad if grad.ndim == 3 else grad[None]
        return grad, swapped(grad, "core")

    ffn_weights = [
        ([product(halves[0], with_other(grad_pre))], ffn_in_m.shape[1] // width, True),
        (
            [product(halves[1], with_other(grad_branch))],
            rows_ffn_out * device_count // width,
            False,
        ),
    ]
    grad_res_two, grad_gain_two = norm_backward(grad_norm_two, unit_two, scale_two, gains[:, 1])
    grad_residual = grad_output_rows + grad_res_two

    grad_attn_branch = grad_residual.astype(BF16)
    grad_attended = matmul_nt(grad_attn_branch, w_out).astype(BF16)
    ffn_sends = gradient_sends(ffn_weights)
    *ffn_sends, grad_attended = lax.optimization_barrier((*ffn_sends, grad_attended))
    ffn_arrived = [swapped(send, axis) for send, axis in zip(ffn_sends, ("x", "y"))]
    grad_query, grad_own, grad_memory, *grad_comps = attention_backward(
        projected, memory_pairs, marks, log_total, grad_attended
    )
    back_memory = passed_along(grad_memory, -1)
    ffn_keeps = gradient_keeps(ffn_weights)
    received = jnp.zeros((2, slots, width), F32)
    for hop, grad_comp in zip((2, 3, 4), grad_comps):
        received = received + passed_along(grad_comp, -hop).astype(F32)
    received = received.astype(BF16)
    ffn_sums = plane_sums(ffn_arrived, ffn_keeps)
    ffn_sums, grad_comp_pairs = lax.optimization_barrier((ffn_sums, received))
    ffn_parts = line_parts(ffn_weights, ffn_sums)
    grad_compressed = matmul_packed_back(grad_comp_pairs, mixer_all, thin, 1).astype(BF16)
    grad_slots = matmul_packed_back(grad_compressed[None], mixer_all, 3 * thin, 1)
    grad_slots = grad_slots.reshape(3 * slots, width)
    grad_first = jnp.concatenate([jnp.zeros((2, width), F32), grad_slots[:2]], 0)
    grad_first = lax.dynamic_slice_in_dim(grad_first, 2 - first_cell, 2, 0)
    back_tail = passed_along(grad_first.astype(BF16), -1).astype(F32)
    grad_own_pairs = (grad_own + back_memory.astype(F32)).astype(BF16)
    grad_input = matmul_packed_back(grad_query[None], mixer_all, thin, 0)
    grad_input = matmul_packed_back(grad_own_pairs, mixer_all, thin, 1, grad_input)
    grad_input = grad_input + lax.dynamic_slice_in_dim(grad_slots, 2 - first_cell, segment, 0)
    grad_input = grad_input.at[segment - 2 :].add(back_tail)
    grad_embed, grad_gain_one = norm_backward(grad_input, unit_one, scale_one, gains[:, 0])
    grad_scaled = ((grad_embed + grad_residual) * width**0.5).astype(BF16)

    share_grads = lax.all_gather(grad_scaled, SHARE, axis=0, tiled=True)
    query_pair, own_pair = with_other(grad_query), with_other(grad_own_pairs)
    comp_pair = with_other(jnp.pad(grad_comp_pairs, ((0, 0), (0, spare), (0, 0))))
    slot_pair = with_other(jnp.pad(grad_compressed, ((0, spare), (0, 0))))
    mixer_weights = [
        ([product(halves[2], query_pair)], 1, True),
        ([product(halves[2], own_pair, 0), product(halves[3], comp_pair, 0)], 1, True),
        ([product(halves[2], own_pair, 1), product(halves[3], comp_pair, 1)], 1, True),
        ([product(halves[4], slot_pair)], 3, False),
        ([product(halves[5], with_other(grad_attn_branch))], 1, True),
    ]
    mixer_sends = gradient_sends(mixer_weights)
    mixer_arrived = [swapped(send, axis) for send, axis in zip(mixer_sends, ("x", "y"))]
    mixer_keeps = gradient_keeps(mixer_weights)
    ffn_grads = line_scatter(ffn_parts)
    table_parts = grad_table.reshape(4, part_rows, width)
    token_row, mixer_keeps, ffn_grads = lax.optimization_barrier(
        (share_row[None, :], mixer_keeps, ffn_grads)
    )
    table_sends = spread_piece(
        token_row, share_grads, table_parts, lambda t: jnp.where(t < 2, 2 * t + 1, t), BF16
    )
    table_sends, mixer_keeps = lax.optimization_barrier((table_sends, mixer_keeps))
    table_arrived = [swapped(send, axis) for send, axis in zip(table_sends, ("x", "y"))]
    table_keeps = spread_piece(
        token_row, share_grads, table_parts, lambda t: jnp.where(t < 2, 2 * t, t - 2), F32
    )
    mixer_sums = plane_sums(mixer_arrived, mixer_keeps)
    mixer_grads = line_scatter(line_parts(mixer_weights, mixer_sums))
    halves_new = []
    for arrived, keep_part, axis in zip(table_arrived, table_keeps, ("y", "x")):
        other = (keep_part[1] + arrived[1].astype(F32)).astype(BF16)
        mine = keep_part[0] + arrived[0].astype(F32)
        halves_new.append(mine + swapped(other, axis).astype(F32))
    grad_table = jnp.concatenate(halves_new, 1)
    if lax.axis_size("far") > 1:
        grad_table = lax.psum_scatter(
            grad_table.astype(BF16), "far", scatter_dimension=0, tiled=True
        )

    small = jnp.concatenate(
        [
            jnp.stack([grad_gain_one, grad_gain_two, grad_gain_three], 1).reshape(-1),
            jnp.full((128,), loss_local, F32),
        ]
    )
    small = small_sum(small)
    loss_total = small[3 * width]
    device = lax.axis_index(ALL)
    gain_grads = lax.dynamic_slice_in_dim(small, device * gain_count, gain_count, 0)

    def side_by_side(rows, count):
        return jnp.concatenate(jnp.split(rows, count, 0), 1)

    low, high = rows_in, rows_in + rows_comp
    grads = (
        grad_table,
        side_by_side(mixer_grads[:low], 3),
        mixer_grads[high:],
        mixer_grads[low:high],
        side_by_side(ffn_grads[:rows_ffn], rows_ffn // attn_in_m.shape[0]),
        ffn_grads[rows_ffn:],
        gain_grads.reshape(gains_m.shape),
    )
    results = []
    for master, first, second, grad, rate in zip(masters, firsts, seconds, grads, STEP_RATES):
        results.extend(adam_update(master, first, second, grad.astype(F32), rate))
    return (loss_total,) + tuple(results)


def solution(mesh):
    batch_count, seq_count = mesh.shape["batch"], mesh.shape["seq"]
    devices = mesh.devices.reshape(batch_count, seq_count // 8, 2, 2, 2)
    grid = Mesh(devices, ALL)
    rows = P(ALL, None)
    return jax.shard_map(
        per_device,
        mesh=grid,
        in_specs=(P("batch", SEQ), P("batch", None), P("batch", SEQ)) + (rows,) * 21,
        out_specs=(P(),) + (rows,) * 21,
        check_vma=False,
    )
```

```python
import jax
import jax.numpy as jnp
from jax import lax
from jax.experimental import pallas as pl
from jax.experimental.pallas import tpu as pltpu
from jax.sharding import Mesh
from jax.sharding import PartitionSpec as P

MODEL_WIDTH = 1024
HEADS = 8
HEAD = 128
NBOOK = 8
STEP = 5

EPSILON = 1e-05
NEGATIVE = -1e30
BETA_ONE = 0.9
BETA_TWO = 0.95
ADAM_EPSILON = 1e-08
WEIGHT_DECAY = 0.1
STEP_RATES = (0.06, 0.03, 0.4, 0.02, 0.03, 0.04, 0.5)

SEQ = ("far", "y", "x", "core")
PLANE = ("far", "y", "x")
SHARE = ("batch", "core")
LINE = ("batch", "far")
ALL = ("batch", "far", "y", "x", "core")
PIECE = 512
BLOCK = 128
GROUPS = 32
CHUNK = 256
BF16 = jnp.bfloat16
F32 = jnp.float32


def passed_along(value, steps):
    count = lax.axis_size(SEQ)
    initial, last = (max(0, -steps), min(count, count - steps))
    return lax.ppermute(value, SEQ, [(source, source + steps) for source in range(initial, last)])


def norm_forward(values, gain):
    center = values - jnp.mean(values, -1, keepdims=True)
    scaler = lax.rsqrt(jnp.mean(center * center, -1, keepdims=True) + EPSILON)
    unit_rows = center * scaler
    return (unit_rows * gain, unit_rows, scaler)


def norm_backward(grad_out, unit_rows, scaler, gain):
    scaled = grad_out * gain
    grad_gain = jnp.sum(grad_out * unit_rows, axis=0)
    grad_in = scaler * (
        scaled
        - jnp.mean(scaled, -1, keepdims=True)
        - unit_rows * jnp.mean(scaled * unit_rows, -1, keepdims=True)
    )
    return (grad_in, grad_gain)


def book_number(positions, book_ends):
    inside = jnp.sum((positions[:, None] >= book_ends[None, :]).astype(jnp.int32), -1)
    return jnp.where(positions < 0, -1, inside)


def matmul(left, right):
    return jnp.dot(left, right, preferred_element_type=F32)


def matmul_nt(left, right):
    return lax.dot_general(left, right, (((1,), (1,)), ((), ())), preferred_element_type=F32)


def matmul_tn(left, right):
    return lax.dot_general(left, right, (((0,), (0,)), ((), ())), preferred_element_type=F32)


def fill_bias(bias, key_book, key_pos, query_book, query_pos):
    allowed = (key_book[...] == query_book[...]) & (key_pos[...] <= query_pos[...])
    bias[...] = jnp.where(allowed, 0.0, NEGATIVE)


def attention_forward_body(*refs):
    query, own_k, own_v, mem_k, mem_v = refs[:5]
    marks, (out, log_total, bias) = refs[5:9], refs[9:]

    @pl.when(pl.program_id(0) == 0)
    def _():
        fill_bias(bias, *marks)

    keys = jnp.concatenate([own_k[...], mem_k[...]], 0)
    values = jnp.concatenate([own_v[...], mem_v[...]], 0)
    scores = matmul_nt(keys, query[...]) * HEAD ** (-0.5) + bias[...]
    top = jnp.max(scores, 0, keepdims=True)
    probs = jnp.exp(scores - top)
    total = jnp.sum(probs, 0, keepdims=True)
    log_total[0] = top + jnp.log(total)
    probs = (probs * (1.0 / total)).astype(BF16)
    out[...] = matmul_tn(values, probs).T.astype(BF16)


def attention_backward_body(*refs):
    query, own_k, own_v, mem_k, mem_v = refs[:5]
    marks = refs[5:9]
    log_total, grad_out, grad_query, grad_own, grad_mem, bias = refs[9:]

    @pl.when(pl.program_id(0) == 0)
    def _():
        fill_bias(bias, *marks)

    keys = jnp.concatenate([own_k[...], mem_k[...]], 0)
    values = jnp.concatenate([own_v[...], mem_v[...]], 0)
    scores = matmul_nt(keys, query[...]) * HEAD ** (-0.5) + bias[...]
    probs = jnp.exp(scores - log_total[0])
    grad_probs = matmul_nt(values, grad_out[...])
    inner = jnp.sum(probs * grad_probs, 0, keepdims=True)
    grad_scores = (probs * (grad_probs - inner) * HEAD ** (-0.5)).astype(BF16)
    grad_query[...] = matmul_tn(keys, grad_scores).T.astype(BF16)
    pair = (matmul(grad_scores, query[...]), matmul(probs.astype(BF16), grad_out[...]))
    at = 0
    for part in (grad_own, grad_mem):
        count = part.shape[1]
        for side in (0, 1):
            part[side] = pair[side][at : at + count].astype(part.dtype)
        at += count


def attention_specs(segment, others):
    def column(rows, shift):
        return pl.BlockSpec((rows, HEAD), lambda h: (0, h + shift * HEADS))

    mark_k = pl.BlockSpec((segment + others, 1), lambda h: (0, 0))
    mark_q = pl.BlockSpec((1, segment), lambda h: (0, 0))
    specs = [column(segment, 0), column(segment, 1), column(segment, 2)]
    specs += [column(others, 0), column(others, 1)]
    return specs + [mark_k, mark_k, mark_q, mark_q]


def attention_forward(projected, memory, marks):
    segment, others = projected.shape[0], memory.shape[0]
    keys = segment + others
    return pl.pallas_call(
        attention_forward_body,
        grid=(HEADS,),
        in_specs=attention_specs(segment, others),
        out_specs=[
            pl.BlockSpec((segment, HEAD), lambda h: (0, h)),
            pl.BlockSpec((1, 1, segment), lambda h: (h, 0, 0)),
        ],
        out_shape=[
            jax.ShapeDtypeStruct((segment, HEADS * HEAD), BF16),
            jax.ShapeDtypeStruct((HEADS, 1, segment), F32),
        ],
        scratch_shapes=[pltpu.VMEM((keys, segment), F32)],
        compiler_params=pltpu.CompilerParams(vmem_limit_bytes=48 << 20),
        cost_estimate=pl.CostEstimate(
            flops=4 * HEADS * keys * segment * HEAD,
            bytes_accessed=12 << 20,
            transcendentals=HEADS * keys * segment,
        ),
        name="attention_forward",
    )(projected, projected, projected, memory, memory, *marks)


def attention_backward(projected, memory, marks, log_total, grad_out):
    segment, others = projected.shape[0], memory.shape[0]
    keys = segment + others
    width = HEADS * HEAD

    def pair_spec(rows):
        return pl.BlockSpec((2, rows, HEAD), lambda h: (0, 0, h))

    return pl.pallas_call(
        attention_backward_body,
        grid=(HEADS,),
        in_specs=attention_specs(segment, others)
        + [
            pl.BlockSpec((1, 1, segment), lambda h: (h, 0, 0)),
            pl.BlockSpec((segment, HEAD), lambda h: (0, h)),
        ],
        out_specs=[pl.BlockSpec((segment, HEAD), lambda h: (0, h))]
        + [pair_spec(segment), pair_spec(others)],
        out_shape=[
            jax.ShapeDtypeStruct((segment, width), BF16),
            jax.ShapeDtypeStruct((2, segment, width), BF16),
            jax.ShapeDtypeStruct((2, others, width), BF16),
        ],
        scratch_shapes=[pltpu.VMEM((keys, segment), F32)],
        compiler_params=pltpu.CompilerParams(vmem_limit_bytes=48 << 20),
        cost_estimate=pl.CostEstimate(
            flops=10 * HEADS * keys * segment * HEAD,
            bytes_accessed=24 << 20,
            transcendentals=HEADS * keys * segment,
        ),
        name="attention_backward",
    )(projected, projected, projected, memory, memory, *marks, log_total, grad_out)


def adam_update(master, first, second, grad, rate):
    new_first = BETA_ONE * first + (1.0 - BETA_ONE) * grad
    new_second = BETA_TWO * second + (1.0 - BETA_TWO) * grad * grad
    first_hat = new_first / (1.0 - BETA_ONE**STEP)
    second_hat = new_second / (1.0 - BETA_TWO**STEP)
    new_master = master - rate * (
        first_hat / (jnp.sqrt(second_hat) + ADAM_EPSILON) + WEIGHT_DECAY * master
    )
    return [new_first, new_second, new_master]


def swapped(value, axis):
    return lax.ppermute(value, axis, [(0, 1), (1, 0)])


def grouped(buffer, sections):
    if buffer.shape[0] == GROUPS:
        return buffer
    parts, at = [], 0
    for count in sections:
        parts.append(buffer[:, at : at + count].reshape(GROUPS, -1, buffer.shape[2]))
        at += count
    return jnp.concatenate(parts, 1)


def matmul_packed(value, buffer, rows, first, count):
    size, depth = value.shape

    def body(value_ref, weight_ref, out):
        weight = weight_ref[...].reshape(depth, PIECE)
        out[...] = matmul(value_ref[...], weight).astype(BF16)

    return pl.pallas_call(
        body,
        grid=(count, 2),
        in_specs=[
            pl.BlockSpec((size, depth), lambda j, h: (0, 0)),
            pl.BlockSpec((GROUPS, rows, PIECE), lambda j, h: (0, first + j, h)),
        ],
        out_specs=pl.BlockSpec((size, PIECE), lambda j, h: (0, 2 * j + h)),
        out_shape=jax.ShapeDtypeStruct((size, count * 2 * PIECE), BF16),
        compiler_params=pltpu.CompilerParams(vmem_limit_bytes=48 << 20),
        cost_estimate=pl.CostEstimate(
            flops=4 * size * depth * count * PIECE,
            bytes_accessed=2 * depth * count * 1024,
            transcendentals=0,
        ),
        name="matmul_packed",
    )(value, buffer)


def matmul_packed_back(grads, buffer, rows, first, start=None):
    count, size, width = grads.shape
    depth = GROUPS * rows
    extra = [] if start is None else [start]

    def body(grad_ref, weight_ref, *rest):
        out = rest[-1]

        @pl.when(pl.program_id(0) == 0)
        def _():
            out[...] = jnp.zeros(out.shape, F32) if start is None else rest[0][...]

        out[...] += matmul_nt(grad_ref[0], weight_ref[...].reshape(depth, width))

    return pl.pallas_call(
        body,
        grid=(count,),
        in_specs=[
            pl.BlockSpec((1, size, width), lambda j: (j, 0, 0)),
            pl.BlockSpec((GROUPS, rows, width), lambda j: (0, first + j, 0)),
        ]
        + [pl.BlockSpec((size, depth), lambda j: (0, 0)) for _ in extra],
        out_specs=pl.BlockSpec((size, depth), lambda j: (0, 0)),
        out_shape=jax.ShapeDtypeStruct((size, depth), F32),
        compiler_params=pltpu.CompilerParams(vmem_limit_bytes=48 << 20),
        cost_estimate=pl.CostEstimate(
            flops=2 * size * depth * count * width,
            bytes_accessed=2 * depth * count * width,
            transcendentals=0,
        ),
        name="matmul_packed_back",
    )(grads, buffer, *extra)


GELU_SCALE = 0.7978845608028654
GELU_CUBE = 0.044715


def feed_forward(value, buffer, residual, chunk):
    size, width = value.shape
    blocks = (buffer.shape[1] - BLOCK) * GROUPS // width
    lines = width // (8 * chunk)

    def body(value_ref, first_ref, second_ref, residual_ref, out, pre, turned):
        hidden = matmul(value_ref[...], first_ref[...].reshape(width, width))
        pre[...] = hidden
        inner = jnp.tanh(GELU_SCALE * (hidden + GELU_CUBE * hidden * hidden * hidden))
        active = (0.5 * hidden * (1.0 + inner)).astype(BF16)

        @pl.when(pl.program_id(0) == 0)
        def _():
            out[...] = residual_ref[...]

        out[...] += matmul(active, second_ref[...].reshape(width, width))
        columns = active.T
        for line in range(lines):
            for place in range(8):
                target = place % 2 * 4 + place // 2
                at = (line * 8 + place) * chunk
                turned[target, line * chunk : (line + 1) * chunk] = columns[at : at + chunk]

    return pl.pallas_call(
        body,
        grid=(blocks,),
        in_specs=[
            pl.BlockSpec((size, width), lambda j: (0, 0)),
            pl.BlockSpec((GROUPS, width // GROUPS, width), lambda j: (0, j, 0)),
            pl.BlockSpec((width // BLOCK, BLOCK, width), lambda j: (j, 1, 0)),
            pl.BlockSpec((size, width), lambda j: (0, 0)),
        ],
        out_specs=[
            pl.BlockSpec((size, width), lambda j: (0, 0)),
            pl.BlockSpec((size, width), lambda j: (0, j)),
            pl.BlockSpec((8, width // 8, size), lambda j: (0, j, 0)),
        ],
        out_shape=[
            jax.ShapeDtypeStruct((size, width), F32),
            jax.ShapeDtypeStruct((size, blocks * width), F32),
            jax.ShapeDtypeStruct((8, blocks * width // 8, size), BF16),
        ],
        compiler_params=pltpu.CompilerParams(vmem_limit_bytes=56 << 20),
        cost_estimate=pl.CostEstimate(
            flops=4 * size * width * width * blocks,
            bytes_accessed=32 << 20,
            transcendentals=size * width * blocks,
        ),
        name="feed_forward",
    )(value, buffer, buffer, residual)


def feed_forward_back(grad, pre, buffer):
    size, width = grad.shape
    blocks = pre.shape[1] // width

    def body(grad_ref, pre_ref, first_ref, second_ref, grad_pre, out):
        grad_active = matmul_nt(grad_ref[...], second_ref[...].reshape(width, width))
        hidden = pre_ref[...]
        square = hidden * hidden
        inner = jnp.tanh(GELU_SCALE * hidden * (1.0 + GELU_CUBE * square))
        slope = 0.5 * (1.0 + inner) + 0.5 * hidden * (1.0 - inner * inner) * GELU_SCALE * (
            1.0 + 3.0 * GELU_CUBE * square
        )
        back = (grad_active * slope).astype(BF16)
        grad_pre[...] = back

        @pl.when(pl.program_id(0) == 0)
        def _():
            out[...] = jnp.zeros(out.shape, F32)

        out[...] += matmul_nt(back, first_ref[...].reshape(width, width))

    return pl.pallas_call(
        body,
        grid=(blocks,),
        in_specs=[
            pl.BlockSpec((size, width), lambda j: (0, 0)),
            pl.BlockSpec((size, width), lambda j: (0, j)),
            pl.BlockSpec((GROUPS, width // GROUPS, width), lambda j: (0, j, 0)),
            pl.BlockSpec((width // BLOCK, BLOCK, width), lambda j: (j, 1, 0)),
        ],
        out_specs=[
            pl.BlockSpec((size, width), lambda j: (0, j)),
            pl.BlockSpec((size, width), lambda j: (0, 0)),
        ],
        out_shape=[
            jax.ShapeDtypeStruct((size, blocks * width), BF16),
            jax.ShapeDtypeStruct((size, width), F32),
        ],
        compiler_params=pltpu.CompilerParams(vmem_limit_bytes=56 << 20),
        cost_estimate=pl.CostEstimate(
            flops=4 * size * width * width * blocks,
            bytes_accessed=32 << 20,
            transcendentals=size * width * blocks,
        ),
        name="feed_forward_back",
    )(grad, pre, buffer, buffer)


def grouped_transpose(rows):
    tokens, columns = rows.shape
    line = lax.axis_size(LINE)
    split = rows.reshape(tokens, line, 2, 2, 2, columns // (line * 8))
    return split.transpose(4, 2, 3, 1, 5, 0).reshape(8, columns // 8, tokens)


def core_halves(grouped):
    core = lax.axis_index("core")
    mine = lax.dynamic_slice_in_dim(grouped, 4 * core, 4, 0)
    other = lax.dynamic_slice_in_dim(grouped, 4 * (1 - core), 4, 0)
    return mine, swapped(other, "core")


def gradient_piece(weights, place, half, axis, moved, dtype):
    operands, specs, plan = [], [], []
    first = 0
    for products, blocks, wide in weights:
        for own, other, rhs_own, rhs_other, lead in products:
            tokens = own.shape[2]

            def inner(step, first=first, blocks=blocks):
                return jnp.clip(step - first, 0, blocks - 1)

            for side in (own, other):
                for free in (0, 1):
                    flip = 2 * free + moved if axis == "x" else 2 * moved + free

                    def lhs_map(step, me, flip=flip, inner=inner, wide=wide):
                        return (me[0] ^ flip, 0 if wide else inner(step), 0)

                    operands.append(side)
                    specs.append(pl.BlockSpec((1, BLOCK, tokens), lhs_map))
            for side in (rhs_own, rhs_other):

                def rhs_map(step, me, inner=inner, wide=wide, lead=lead):
                    return (lead, 0, 2 * inner(step) + half if wide else half)

                operands.append(side)
                specs.append(pl.BlockSpec((1, tokens, PIECE), rhs_map))
        plan.append((first, blocks, len(products)))
        first += blocks

    def body(me, *refs):
        out = refs[-1]
        step = pl.program_id(0)
        at = 0
        for start, blocks, count in plan:
            group = refs[at : at + 6 * count]

            @pl.when((step >= start) & (step < start + blocks))
            def _():
                total = jnp.zeros((2 * BLOCK, PIECE), F32)
                for k in range(0, 6 * count, 6):
                    near = jnp.concatenate([group[k][0], group[k + 1][0]], 0)
                    far = jnp.concatenate([group[k + 2][0], group[k + 3][0]], 0)
                    total += matmul(near, group[k + 4][0]) + matmul(far, group[k + 5][0])
                out[0] = total.astype(out.dtype)

            at += 6 * count

    return pl.pallas_call(
        body,
        grid_spec=pltpu.PrefetchScalarGridSpec(
            num_scalar_prefetch=1,
            grid=(first,),
            in_specs=specs,
            out_specs=pl.BlockSpec((1, 2 * BLOCK, PIECE), lambda step, me: (step, 0, 0)),
        ),
        out_shape=jax.ShapeDtypeStruct((first, 2 * BLOCK, PIECE), dtype),
        compiler_params=pltpu.CompilerParams(vmem_limit_bytes=40 << 20),
        cost_estimate=pl.CostEstimate(
            flops=first * 2 * 2 * BLOCK * PIECE * 1024,
            bytes_accessed=first * (3 << 20),
            transcendentals=0,
        ),
        name="gradient_piece",
    )(place, *operands)


def line_open(value):
    shape = value.shape[1:]
    count = lax.axis_size(LINE)
    return value, jnp.zeros(shape, BF16), jnp.zeros(shape, BF16), count - 1


def line_sends(state):
    value, upward, downward, steps = state
    count, index = lax.axis_size(LINE), lax.axis_index(LINE)
    above = lax.dynamic_index_in_dim(value, jnp.minimum(index + steps, count - 1), 0, False)
    below = lax.dynamic_index_in_dim(value, jnp.maximum(index - steps, 0), 0, False)
    return (above + upward.astype(F32)).astype(BF16), (below + downward.astype(F32)).astype(BF16)


def line_move(state, sends):
    steps = state[3]
    count = lax.axis_size(LINE)
    up = [(i, i + 1) for i in range(count - steps)]
    down = [(i, i - 1) for i in range(steps, count)]
    upward = lax.ppermute(sends[0], LINE, up)
    downward = lax.ppermute(sends[1], LINE, down)
    return state[0], upward, downward, steps - 1


def line_close(state):
    while state[3] > 0:
        state = line_move(state, line_sends(state))
    value, upward, downward, _ = state
    total = lax.dynamic_index_in_dim(value, lax.axis_index(LINE), 0, False)
    return total + upward.astype(F32) + downward.astype(F32)


def chip_place():
    place = lax.axis_index("y") * 2 + lax.axis_index("x")
    return jnp.reshape(place, (1,)).astype(jnp.int32)


def gradient_sends(weights, place):
    return [
        gradient_piece(weights, place, 0, "x", 1, BF16),
        gradient_piece(weights, place, 1, "y", 1, BF16),
    ]


def gradient_keeps(weights, place):
    return [
        gradient_piece(weights, place, 0, "x", 0, F32),
        gradient_piece(weights, place, 1, "y", 0, F32),
    ]


def plane_sums(sends, keeps):
    result = []
    for arrived, keep in zip(sends, keeps):
        count = keep.shape[1] // 2
        other = (keep[:, count:] + arrived[:, count:].astype(F32)).astype(BF16)
        result.append((keep[:, :count] + arrived[:, :count].astype(F32), other))
    return result


def plane_others(sums):
    return [swapped(other, axis) for (_, other), axis in zip(sums, ("y", "x"))]


def line_parts(weights, sums, others):
    line = lax.axis_size(LINE)
    joined = [mine + other.astype(F32) for (mine, _), other in zip(sums, others)]
    first, chunks = 0, []
    for weight in weights:
        blocks, wide = weight[1:]
        for part in range(blocks if wide else 1):
            count = 1 if wide else blocks
            pair = [
                half[first : first + count].reshape(line, count * BLOCK // line, PIECE)
                for half in joined
            ]
            chunks.append(jnp.concatenate(pair, -1))
            first += count
    return jnp.concatenate(chunks, 1)


class SmallSum:
    def __init__(self, value):
        count = lax.axis_size(LINE)
        self.value = value
        self.steps = [("core", 1), ("x", 1), ("y", 1)]
        step = 1
        while step < count:
            self.steps.append((LINE, step))
            step *= 2

    def exchange(self):
        axis, step = self.steps.pop(0)
        size = lax.axis_size(axis)
        return lax.ppermute(self.value, axis, [(i, i ^ step) for i in range(size)])

    def total(self):
        while self.steps:
            self.value = self.value + self.exchange()
        return self.value


def line_gather(block):
    return lax.all_gather(block, LINE, axis=0, tiled=False)


def plane_swaps(value):
    return swapped(value, "x"), swapped(value, "y")


def plane_corners(swaps):
    return swapped(swaps[0][..., :PIECE], "y"), swapped(swaps[1][..., PIECE:], "x")


def plane_gather(value, swaps, corners):
    line, rows, width = value.shape
    along_x, along_y = swaps
    pieces = (
        (value, 0, 0, 0),
        (along_x, 0, 1, 0),
        (along_y, 1, 0, 0),
        (corners[0], 1, 1, 0),
        (corners[1], 1, 1, PIECE),
    )
    y, x, core = (lax.axis_index(axis) for axis in ("y", "x", "core"))
    result = jnp.zeros((line, 2, 2, 2, rows, width), BF16)
    for piece, flip_y, flip_x, column in pieces:
        for flip in (0, 1):
            part = swapped(piece, "core") if flip else piece
            start = (0, y ^ flip_y, x ^ flip_x, core ^ flip, 0, column)
            result = lax.dynamic_update_slice(result, part[:, None, None, None], start)
    return result.reshape(8 * line, rows, width)


def share_combine(top, total):
    def merged(top, total, axis, pairs):
        pair = lax.ppermute(jnp.concatenate([top, total], 0), axis, pairs)
        best = jnp.maximum(top, pair[:1])
        return best, total * jnp.exp(top - best) + pair[1:] * jnp.exp(pair[:1] - best)

    top, total = merged(top, total, "core", [(0, 1), (1, 0)])
    count = lax.axis_size("batch")
    step = 1
    while step < count:
        top, total = merged(top, total, "batch", [(i, i ^ step) for i in range(count)])
        step *= 2
    return top + jnp.log(total)


def head_logits(rows, table, wanted):
    parts, part_rows, width = table.shape
    count = rows.shape[0]

    def body(rows_ref, table_ref, wanted_ref, logits, top, total, target):
        part = pl.program_id(0)

        @pl.when(part == 0)
        def _():
            top[...] = jnp.full(top.shape, NEGATIVE, F32)
            total[...] = jnp.zeros(total.shape, F32)
            target[...] = jnp.zeros(target.shape, F32)

        for at in range(0, count, CHUNK):
            span = slice(at, at + CHUNK)
            scores = matmul_nt(table_ref[0], rows_ref[span])
            logits[0, :, span] = scores
            best = jnp.maximum(top[:, span], jnp.max(scores, 0, keepdims=True))
            total[:, span] = total[:, span] * jnp.exp(top[:, span] - best) + jnp.sum(
                jnp.exp(scores - best), 0, keepdims=True
            )
            top[:, span] = best
            place = lax.broadcasted_iota(jnp.int32, scores.shape, 0)
            hit = place == wanted_ref[:, span] - part * part_rows
            target[:, span] += jnp.sum(jnp.where(hit, scores, 0.0), 0, keepdims=True)

    row = pl.BlockSpec((1, count), lambda p: (0, 0))
    return pl.pallas_call(
        body,
        grid=(parts,),
        in_specs=[
            pl.BlockSpec((count, width), lambda p: (0, 0)),
            pl.BlockSpec((1, part_rows, width), lambda p: (p, 0, 0)),
            row,
        ],
        out_specs=[pl.BlockSpec((1, part_rows, count), lambda p: (p, 0, 0)), row, row, row],
        out_shape=[jax.ShapeDtypeStruct((parts, part_rows, count), F32)]
        + [jax.ShapeDtypeStruct((1, count), F32)] * 3,
        compiler_params=pltpu.CompilerParams(vmem_limit_bytes=56 << 20),
        cost_estimate=pl.CostEstimate(
            flops=2 * parts * part_rows * count * width,
            bytes_accessed=4 * parts * part_rows * (count + width // 2),
            transcendentals=parts * part_rows * count,
        ),
        name="head_logits",
    )(rows, table, wanted)


def head_grad(logits, log_norm, weight, wanted, first):
    place = lax.broadcasted_iota(jnp.int32, logits.shape, 0)
    probs = jnp.exp(logits - log_norm)
    return (weight * jnp.where(place == wanted - first, probs - 1.0, probs)).astype(BF16)


def head_row_grads(logits, log_norm, weight, wanted, turned):
    parts, part_rows, count = logits.shape
    width, deep = turned.shape[1:]

    def body(logits_ref, log_norm_ref, weight_ref, wanted_ref, turned_ref, out, total):
        part = pl.program_id(0)
        @pl.when(part == 0)
        def _():
            total[...] = jnp.zeros(total.shape, F32)

        for at in range(0, count, CHUNK):
            span = slice(at, at + CHUNK)
            grad = head_grad(
                logits_ref[0, :, span],
                log_norm_ref[:, span],
                weight_ref[:, span],
                wanted_ref[:, span],
                part * part_rows,
            )
            if deep > part_rows:
                grad = jnp.concatenate([grad, jnp.zeros((deep - part_rows, CHUNK), BF16)], 0)
            total[:, span] += matmul(turned_ref[0], grad)

        @pl.when(part == parts - 1)
        def _():
            out[...] = total[...].T.astype(BF16)

    row = pl.BlockSpec((1, count), lambda p: (0, 0))
    return pl.pallas_call(
        body,
        grid=(parts,),
        in_specs=[
            pl.BlockSpec((1, part_rows, count), lambda p: (p, 0, 0)),
            row,
            row,
            row,
            pl.BlockSpec((1, width, deep), lambda p: (p, 0, 0)),
        ],
        out_specs=pl.BlockSpec((count, width), lambda p: (0, 0)),
        out_shape=jax.ShapeDtypeStruct((count, width), BF16),
        scratch_shapes=[pltpu.VMEM((width, count), F32)],
        compiler_params=pltpu.CompilerParams(vmem_limit_bytes=56 << 20),
        cost_estimate=pl.CostEstimate(
            flops=2 * parts * part_rows * count * width,
            bytes_accessed=4 * parts * part_rows * (count + width // 2),
            transcendentals=parts * part_rows * count,
        ),
        name="head_row_grads",
    )(logits, log_norm, weight, wanted, turned)


def head_table_grads(groups):
    parts, part_rows, count = groups[0][0].shape
    width = groups[0][4].shape[1]

    def body(*refs):
        out = refs[-1]
        total = jnp.zeros((part_rows, width), F32)
        for at in range(0, 5 * len(groups), 5):
            logits, log_norm, weight, wanted, rows = refs[at : at + 5]
            for start in range(0, count, CHUNK):
                span = slice(start, start + CHUNK)
                grad = head_grad(
                    logits[0, :, span],
                    log_norm[:, span],
                    weight[:, span],
                    wanted[:, span],
                    pl.program_id(0) * part_rows,
                )
                total += matmul(grad, rows[span])
        out[0] = total

    row = pl.BlockSpec((1, count), lambda p: (0, 0))
    specs = [
        pl.BlockSpec((1, part_rows, count), lambda p: (p, 0, 0)),
        row,
        row,
        row,
        pl.BlockSpec((count, width), lambda p: (0, 0)),
    ]
    return pl.pallas_call(
        body,
        grid=(parts,),
        in_specs=specs * len(groups),
        out_specs=pl.BlockSpec((1, part_rows, width), lambda p: (p, 0, 0)),
        out_shape=jax.ShapeDtypeStruct((parts, part_rows, width), F32),
        compiler_params=pltpu.CompilerParams(vmem_limit_bytes=58 << 20),
        cost_estimate=pl.CostEstimate(
            flops=2 * parts * part_rows * count * width * len(groups),
            bytes_accessed=4 * parts * part_rows * (count * len(groups) + width),
            transcendentals=parts * part_rows * count * len(groups),
        ),
        name="head_table_grads",
    )(*[value for group in groups for value in group])


def spread_body(row_of, token_row, grads, table_grad, *refs):
    outs, total = refs[:2], refs[2]
    task, step = pl.program_id(0), pl.program_id(1)
    rows, tokens = total.shape[0], grads.shape[0]
    first = row_of(task) * rows

    @pl.when(step == 0)
    def _():
        total[...] = table_grad[0]

    wanted = token_row[...] - first
    hit = lax.broadcasted_iota(jnp.int32, (rows, tokens), 0) == wanted
    total[...] += matmul(jnp.where(hit, 1.0, 0.0).astype(BF16), grads[...])

    for side in (0, 1):

        @pl.when((step == pl.num_programs(1) - 1) & (task // 2 == side))
        def _():
            outs[side][0] = total[...].astype(outs[side].dtype)


def spread_piece(token_row, grads, table_grad, row_of, dtype):
    blocks, rows, width = table_grad.shape
    tokens = 1024

    def body(*refs):
        spread_body(row_of, *refs)

    return pl.pallas_call(
        body,
        grid=(4, grads.shape[0] // tokens),
        in_specs=[
            pl.BlockSpec((1, tokens), lambda task, step: (0, step)),
            pl.BlockSpec((tokens, PIECE), lambda task, step: (step, task // 2)),
            pl.BlockSpec((1, rows, PIECE), lambda task, step: (row_of(task), 0, task // 2)),
        ],
        out_specs=[
            pl.BlockSpec((1, rows, PIECE), lambda task, step: (jnp.minimum(task, 1), 0, 0)),
            pl.BlockSpec((1, rows, PIECE), lambda task, step: (jnp.maximum(task - 2, 0), 0, 0)),
        ],
        out_shape=[jax.ShapeDtypeStruct((2, rows, PIECE), dtype)] * 2,
        scratch_shapes=[pltpu.VMEM((rows, PIECE), F32)],
        compiler_params=pltpu.CompilerParams(vmem_limit_bytes=48 << 20),
        cost_estimate=pl.CostEstimate(
            flops=4 * 2 * rows * PIECE * grads.shape[0],
            bytes_accessed=24 << 20,
            transcendentals=0,
        ),
        name="spread_piece",
    )(token_row, grads, table_grad)


def column_blocks(rows):
    return jnp.concatenate(jnp.split(rows, rows.shape[1] // MODEL_WIDTH, 1), 0)


def bf16_parts(values):
    high = values.astype(BF16)
    rest = values - high.astype(F32)
    middle = rest.astype(BF16)
    low = (rest - middle.astype(F32)).astype(BF16)
    return high, middle, low


def per_device(token_ids, book_lengths, loss_mask, *state):
    masters, firsts, seconds = state[:7], state[7:14], state[14:]
    table_master, attn_in_m, attn_out_m, compress_m, ffn_in_m, ffn_out_m, gains_m = masters
    vocab_block = table_master.shape[0]
    batch_count = lax.axis_size("batch")
    seq_count = lax.axis_size(SEQ)
    plane_count = seq_count // 2
    share_count = batch_count * 2
    device_count = batch_count * seq_count
    segment = token_ids.shape[1]
    slots = -(-(segment // 3 + 1) // 16) * 16
    keep = segment // 2
    place = lax.axis_index(SEQ)
    offset = place * segment
    share_place = lax.axis_index(SHARE)
    width = MODEL_WIDTH

    own_tokens = token_ids.reshape(segment)
    share_tokens = lax.all_gather(own_tokens, SHARE, axis=0, tiled=True)
    rows_in = attn_in_m.size // width
    rows_out = attn_out_m.size // width
    rows_comp = compress_m.size // width
    rows_ffn = ffn_in_m.size // width
    rows_ffn_out = ffn_out_m.size // width
    gain_count = gains_m.size
    gain_block = jnp.zeros((16, width), BF16).at[0, :gain_count].set(
        gains_m.astype(BF16).reshape(-1)
    )
    mixer_block = jnp.concatenate(
        [
            column_blocks(attn_in_m.astype(BF16)),
            compress_m.astype(BF16),
            attn_out_m.astype(BF16),
            gain_block,
        ],
        0,
    )
    ffn_block = jnp.concatenate(
        [column_blocks(ffn_in_m.astype(BF16)), ffn_out_m.astype(BF16)], 0
    )
    own_table = lax.all_gather(table_master.astype(BF16), "far", axis=0, tiled=True)
    table_x, table_y = plane_swaps(own_table)
    mixer_line_all, ffn_line_all = line_gather(mixer_block), line_gather(ffn_block)
    table_x, table_y, mixer_line_all = lax.optimization_barrier(
        (table_x, table_y, mixer_line_all)
    )
    mixer_swaps = plane_swaps(mixer_line_all)
    part_rows = own_table.shape[0]
    table = jnp.zeros((4 * part_rows, width), BF16)
    for value, row, column in (
        (own_table, 0, 0),
        (table_x, 1, 0),
        (table_y, 2, 0),
        (swapped(table_x[:, :PIECE], "y"), 3, 0),
        (swapped(table_y[:, PIECE:], "x"), 3, PIECE),
    ):
        table = lax.dynamic_update_slice(table, value, (row * part_rows, column))

    def vocab_place(tokens):
        block = tokens // vocab_block
        seq_index = block % seq_count
        owner = block // seq_count * 2 + seq_index % 2
        chip = seq_index // 2 % 4
        part = chip ^ (lax.axis_index("y") * 2 + lax.axis_index("x"))
        inside = seq_index // 8 * vocab_block + tokens % vocab_block
        return owner, part * part_rows + inside

    share_owner, share_local = vocab_place(share_tokens)
    share_row = jnp.where(share_owner == share_place, share_local, -1)
    looked = jnp.where(
        (share_row >= 0)[:, None], table[jnp.maximum(share_row, 0)], jnp.zeros((), BF16)
    )

    looked, mixer_swaps, ffn_line_all = lax.optimization_barrier(
        (looked, mixer_swaps, ffn_line_all)
    )
    mixer_corners = plane_corners(mixer_swaps)
    table_again, mixer_corners, ffn_line_all = lax.optimization_barrier(
        (table, mixer_corners, ffn_line_all)
    )
    ffn_swaps = plane_swaps(ffn_line_all)
    mixer_all = plane_gather(mixer_line_all, mixer_swaps, mixer_corners)
    gains = mixer_all[:, rows_in + rows_comp + rows_out, :gain_count]
    token_rows = lax.psum_scatter(looked, SHARE, scatter_dimension=0, tiled=True)
    gains = gains.reshape(width, 3).astype(F32)
    table = table_again.reshape(4, part_rows, width)
    turned = jnp.pad(table, ((0, 0), (0, -part_rows % 128), (0, 0))).transpose(0, 2, 1)
    token_rows, turned, ffn_swaps = lax.optimization_barrier((token_rows, turned, ffn_swaps))
    part = attn_in_m.shape[0]
    mixer_all = grouped(mixer_all, (part, part, part, rows_comp, rows_out, 16))
    thin = width // GROUPS

    book_ends = jnp.cumsum(book_lengths.reshape(-1))
    own_pos = offset + jnp.arange(segment, dtype=jnp.int32)
    own_book = book_number(own_pos, book_ends)
    next_book = book_number(own_pos + 1, book_ends)
    own_mask = loss_mask.reshape(segment)
    numbers = jnp.arange(NBOOK, dtype=jnp.int32)
    live = own_mask.astype(F32) * (next_book == own_book).astype(F32)
    member = (own_book[:, None] == numbers[None, :]).astype(F32)
    book_counts = jnp.sum(member * live[:, None], 0)
    for axis in ("core", "x", "y"):
        book_counts = book_counts + swapped(book_counts, axis)
    book_counts = lax.psum(book_counts, "far")
    weight = live * jnp.sum(member / jnp.maximum(book_counts, 1.0)[None, :], -1)
    following = passed_along(own_tokens[:1], -1)
    targets = jnp.concatenate([own_tokens[1:], following])
    rank = jnp.cumsum(own_mask) - 1
    chosen = (rank[None, :] == jnp.arange(keep, dtype=jnp.int32)[:, None]) & (
        own_mask[None, :] > 0
    )
    picked_targets = jnp.sum(jnp.where(chosen, targets[None, :], 0), 1)
    picked_weight = jnp.sum(jnp.where(chosen, weight[None, :], 0.0), 1)

    embedded = token_rows.astype(F32) * width**0.5
    normed_one, unit_one, scale_one = norm_forward(embedded, gains[:, 0])
    attention_input = normed_one.astype(BF16)
    attention_input, ffn_swaps = lax.optimization_barrier((attention_input, ffn_swaps))
    ffn_all = plane_gather(ffn_line_all, ffn_swaps, plane_corners(ffn_swaps))
    ffn_all = grouped(ffn_all, (part,) * (rows_ffn // part) + (rows_ffn_out,))
    projected = matmul_packed(attention_input, mixer_all, thin, 0, 3)
    memory_rows = passed_along(attention_input, 1)
    tail_rows = passed_along(attention_input[segment - 2 :], 1)
    first_cell = jnp.mod(2 - offset, 3)
    padding = 3 * slots - segment + 2
    extended = jnp.concatenate([tail_rows, attention_input, jnp.zeros((padding, width), BF16)], 0)
    slot_rows = lax.dynamic_slice_in_dim(extended, first_cell, 3 * slots, 0).reshape(
        slots, 3 * width
    )
    compressed = matmul_packed(slot_rows, mixer_all, 3 * thin, 1, 1)
    other_rows = [memory_rows]
    spare = -(segment + 3 * slots) % BLOCK
    book_parts = [own_book, book_number(own_pos - segment, book_ends)]
    pos_parts = [own_pos, own_pos - segment]
    for hop in (2, 3, 4):
        other_rows.append(passed_along(compressed, hop))
        owner = place - hop
        last_pos = (
            owner * segment
            + jnp.mod(2 - owner * segment, 3)
            + 3 * jnp.arange(slots, dtype=jnp.int32)
        )
        last_book = book_number(last_pos, book_ends)
        usable = (owner >= 0) & (last_pos < owner * segment + segment)
        usable = usable & (book_number(last_pos - 2, book_ends) == last_book)
        book_parts.append(jnp.where(usable, last_book, -2))
        pos_parts.append(jnp.full((slots,), -1, jnp.int32))
    book_parts.append(jnp.full((spare,), -2, jnp.int32))
    pos_parts.append(jnp.full((spare,), -1, jnp.int32))
    other_rows.append(jnp.zeros((spare, width), BF16))
    marks = (
        jnp.concatenate(book_parts)[:, None],
        jnp.concatenate(pos_parts)[:, None],
        own_book[None, :],
        own_pos[None, :],
    )
    other_rows = jnp.concatenate(other_rows, 0)
    memory_pairs = matmul_packed(other_rows, mixer_all, thin, 1, 2)
    attended, log_total = attention_forward(projected, memory_pairs, marks)
    w_out = mixer_all[:, 6 * thin : 7 * thin].reshape(width, width)
    residual = embedded + matmul(attended, w_out)

    normed_two, unit_two, scale_two = norm_forward(residual, gains[:, 1])
    ffn_input = normed_two.astype(BF16)
    output_rows, pre_act, activated_turned = feed_forward(
        ffn_input, ffn_all, residual, rows_ffn_out
    )
    normed_three, unit_three, scale_three = norm_forward(output_rows, gains[:, 2])
    final_rows = normed_three.astype(BF16)

    chosen_bf16 = chosen.astype(BF16)
    picked_rows = matmul(chosen_bf16, final_rows).astype(BF16)
    high, middle, low = bf16_parts(picked_weight)
    side = jnp.concatenate(
        [
            (picked_targets // 256).astype(BF16),
            (picked_targets % 256).astype(BF16),
            high,
            middle,
            low,
        ]
    )
    side_rows = jnp.zeros((16 * width,), BF16).at[: 5 * keep].set(side).reshape(16, width)
    half = keep // 2
    head_all = lax.all_gather(
        jnp.concatenate([picked_rows, side_rows], 0), SHARE, axis=0, tiled=False
    )
    slot_spare = -slots % BLOCK
    slot_tall = jnp.concatenate([slot_rows, jnp.zeros((slot_spare, 3 * width), BF16)], 0)
    halves = [
        core_halves(value)
        for value in (
            grouped_transpose(ffn_input),
            activated_turned,
            grouped_transpose(attention_input),
            grouped_transpose(other_rows),
            grouped_transpose(slot_tall),
            grouped_transpose(attended),
        )
    ]
    rows_one = head_all[:, :half].reshape(share_count * half, width)
    rows_two = head_all[:, half:keep].reshape(share_count * half, width)
    side_all = head_all[:, keep:].reshape(share_count, 16 * width)[:, : 5 * keep]
    rows_one, rows_two, halves = lax.optimization_barrier((rows_one, rows_two, halves))
    side_all = side_all.reshape(share_count, 5, 2, half).astype(F32)
    side_all = side_all.transpose(1, 2, 0, 3).reshape(5, 2, share_count * half)
    wanted_all = (side_all[0] * 256.0 + side_all[1]).astype(jnp.int32)
    weight_all = side_all[2] + side_all[3] + side_all[4]
    wanted_owner, wanted_local = vocab_place(wanted_all)
    wanted_all = jnp.where(wanted_owner == share_place, wanted_local, -1)
    mine = (jnp.arange(share_count * half) // half == share_place).astype(F32)
    loss_local = jnp.zeros((), F32)
    groups, stats = [], []
    for index, rows in enumerate((rows_one, rows_two)):
        wanted, row_weight = wanted_all[index][None], weight_all[index][None]
        logits, top, total, target_logit = head_logits(rows, table, wanted)
        loss_local -= jnp.sum(row_weight * target_logit)
        stats.append((top, total))
        groups.append([logits, row_weight, wanted, rows])
    log_norms = [share_combine(*stats[0]), None]
    stats[1], log_norms[0] = lax.optimization_barrier((stats[1], log_norms[0]))
    log_norms[1] = share_combine(*stats[1])
    for index, (logits, row_weight, wanted, rows) in enumerate(groups):
        loss_local += jnp.sum(row_weight * mine[None] * log_norms[index])
        groups[index] = (logits, log_norms[index], row_weight, wanted, rows)
    grad_picked = []
    for group in groups:
        grad_rows = head_row_grads(*group[:4], turned)
        grad_picked.append(lax.psum_scatter(grad_rows, SHARE, scatter_dimension=0, tiled=True))
    grad_picked = jnp.concatenate(grad_picked, 0)
    grad_table = head_table_grads(groups)
    grad_picked, grad_table = lax.optimization_barrier((grad_picked, grad_table))
    grad_final = matmul_tn(chosen_bf16, grad_picked)

    grad_output_rows, grad_gain_three = norm_backward(
        grad_final, unit_three, scale_three, gains[:, 2]
    )
    grad_branch = grad_output_rows.astype(BF16)
    grad_pre, grad_norm_two = feed_forward_back(grad_branch, pre_act, ffn_all)

    def product(pair, grad, lead=0):
        return pair + (grad[0], grad[1], lead)

    def with_other(grad):
        grad = grad if grad.ndim == 3 else grad[None]
        return grad, swapped(grad, "core")

    ffn_weights = [
        ([product(halves[0], with_other(grad_pre))], ffn_in_m.shape[1] // width, True),
        (
            [product(halves[1], with_other(grad_branch))],
            rows_ffn_out * device_count // width,
            False,
        ),
    ]
    ffn_rows = rows_ffn + rows_ffn_out
    grad_res_two, grad_gain_two = norm_backward(grad_norm_two, unit_two, scale_two, gains[:, 1])
    grad_residual = grad_output_rows + grad_res_two

    grad_attn_branch = grad_residual.astype(BF16)
    grad_attended = matmul_nt(grad_attn_branch, w_out).astype(BF16)
    ffn_weights.append(([product(halves[5], with_other(grad_attn_branch))], 1, True))
    grad_query, grad_own, grad_other = attention_backward(
        projected, memory_pairs, marks, log_total, grad_attended
    )
    grad_other_rows = matmul_packed_back(grad_other, mixer_all, thin, 1).astype(BF16)
    back_memory = passed_along(grad_other_rows[:segment], -1)
    returned = []
    for hop in (2, 3, 4):
        first_row = segment + (hop - 2) * slots
        returned.append(passed_along(grad_other_rows[first_row : first_row + slots], -hop))
    place, grad_query = lax.optimization_barrier((chip_place(), grad_query))
    ffn_sends = gradient_sends(ffn_weights, place)
    grad_input = matmul_packed_back(grad_query[None], mixer_all, thin, 0)
    grad_input = matmul_packed_back(grad_own, mixer_all, thin, 1, grad_input)
    returned, ffn_sends, grad_input = lax.optimization_barrier(
        (returned, ffn_sends, grad_input)
    )
    ffn_arrived = [swapped(send, axis) for send, axis in zip(ffn_sends, ("x", "y"))]
    grad_compressed = sum(part.astype(F32) for part in returned).astype(BF16)
    grad_slots = matmul_packed_back(grad_compressed[None], mixer_all, 3 * thin, 1)
    grad_slots = grad_slots.reshape(3 * slots, width)
    grad_first = jnp.concatenate([jnp.zeros((2, width), F32), grad_slots[:2]], 0)
    grad_first = lax.dynamic_slice_in_dim(grad_first, 2 - first_cell, 2, 0)
    back_tail = passed_along(grad_first.astype(BF16), -1).astype(F32)
    grad_input = grad_input + lax.dynamic_slice_in_dim(grad_slots, 2 - first_cell, segment, 0)
    grad_input = grad_input + back_memory.astype(F32)
    grad_input = grad_input.at[segment - 2 :].add(back_tail)
    grad_embed, grad_gain_one = norm_backward(grad_input, unit_one, scale_one, gains[:, 0])
    grad_scaled = ((grad_embed + grad_residual) * width**0.5).astype(BF16)

    query_pair, own_pair = with_other(grad_query), with_other(grad_own)
    other_pair = with_other(grad_other)
    slot_pair = with_other(jnp.pad(grad_compressed, ((0, slot_spare), (0, 0))))
    mixer_weights = [
        ([product(halves[2], query_pair)], 1, True),
        ([product(halves[2], own_pair, 0), product(halves[3], other_pair, 0)], 1, True),
        ([product(halves[2], own_pair, 1), product(halves[3], other_pair, 1)], 1, True),
        ([product(halves[4], slot_pair)], 3, False),
    ]
    small = jnp.concatenate(
        [
            jnp.stack([grad_gain_one, grad_gain_two, grad_gain_three], 1).reshape(-1),
            jnp.full((128,), loss_local, F32),
        ]
    )
    grad_scaled, place = lax.optimization_barrier((grad_scaled, place))
    small = SmallSum(small)
    share_grads = lax.all_gather(grad_scaled, SHARE, axis=0, tiled=True)
    mixer_sends = gradient_sends(mixer_weights, place)
    mixer_sends, place, arrived = lax.optimization_barrier(
        (mixer_sends, place, small.exchange())
    )
    small.value += arrived
    mixer_arrived = [swapped(send, axis) for send, axis in zip(mixer_sends, ("x", "y"))]
    ffn_sums = plane_sums(ffn_arrived, gradient_keeps(ffn_weights, place))
    ffn_sums, place, arrived = lax.optimization_barrier((ffn_sums, place, small.exchange()))
    small.value += arrived
    mixer_keeps = gradient_keeps(mixer_weights, place)
    mixer_sums = plane_sums(mixer_arrived, mixer_keeps)
    token_row, mixer_sums, arrived = lax.optimization_barrier(
        (share_row[None, :], mixer_sums, small.exchange())
    )
    small.value += arrived
    table_sends = spread_piece(
        token_row, share_grads, grad_table, lambda t: jnp.where(t < 2, 2 * t + 1, t), BF16
    )
    ffn_others, mixer_others = plane_others(ffn_sums), plane_others(mixer_sums)
    table_sends, token_row, ffn_others, mixer_others, arrived = lax.optimization_barrier(
        (table_sends, token_row, ffn_others, mixer_others, small.exchange())
    )
    small.value += arrived
    table_arrived = [swapped(send, axis) for send, axis in zip(table_sends, ("x", "y"))]
    lines = [
        line_open(line_parts(ffn_weights, ffn_sums, ffn_others)),
        line_open(line_parts(mixer_weights, mixer_sums, mixer_others)),
    ]
    lines = [line_move(line, line_sends(line)) for line in lines]
    table_keeps = spread_piece(
        token_row, share_grads, grad_table, lambda t: jnp.where(t < 2, 2 * t, t - 2), F32
    )
    table_keeps, table_arrived, moved, arrived = lax.optimization_barrier(
        (table_keeps, table_arrived, [line[1:3] for line in lines], small.exchange())
    )
    small.value += arrived
    lines = [(line[0], *pair, line[3]) for line, pair in zip(lines, moved)]
    lines = [line_move(line, line_sends(line)) for line in lines]
    summed, mixer_grads = [line_close(line) for line in lines]
    ffn_grads, attn_out_grad = summed[:ffn_rows], summed[ffn_rows : ffn_rows + rows_out]
    halves_new = []
    for arrived, keep_part, axis in zip(table_arrived, table_keeps, ("y", "x")):
        other = (keep_part[1] + arrived[1].astype(F32)).astype(BF16)
        mine = keep_part[0] + arrived[0].astype(F32)
        halves_new.append(mine + swapped(other, axis).astype(F32))
    grad_table = jnp.concatenate(halves_new, 1)
    if lax.axis_size("far") > 1:
        grad_table = lax.psum_scatter(
            grad_table.astype(BF16), "far", scatter_dimension=0, tiled=True
        )

    small = small.total()
    loss_total = small[3 * width]
    device = lax.axis_index(ALL)
    gain_grads = lax.dynamic_slice_in_dim(small, device * gain_count, gain_count, 0)

    def side_by_side(rows, count):
        return jnp.concatenate(jnp.split(rows, count, 0), 1)

    low, high = rows_in, rows_in + rows_comp
    grads = (
        grad_table,
        side_by_side(mixer_grads[:low], 3),
        attn_out_grad,
        mixer_grads[low:high],
        side_by_side(ffn_grads[:rows_ffn], rows_ffn // attn_in_m.shape[0]),
        ffn_grads[rows_ffn:],
        gain_grads.reshape(gains_m.shape),
    )
    results = []
    for master, first, second, grad, rate in zip(masters, firsts, seconds, grads, STEP_RATES):
        results.extend(adam_update(master, first, second, grad.astype(F32), rate))
    return (loss_total,) + tuple(results)


def solution(mesh):
    batch_count, seq_count = mesh.shape["batch"], mesh.shape["seq"]
    devices = mesh.devices.reshape(batch_count, seq_count // 8, 2, 2, 2)
    grid = Mesh(devices, ALL)
    rows = P(ALL, None)
    return jax.shard_map(
        per_device,
        mesh=grid,
        in_specs=(P("batch", SEQ), P("batch", None), P("batch", SEQ)) + (rows,) * 21,
        out_specs=(P(),) + (rows,) * 21,
        check_vma=False,
    )
```

```python
import jax
import jax.numpy as jnp
from jax import lax
from jax.experimental import pallas as pl
from jax.experimental.pallas import tpu as pltpu
from jax.sharding import Mesh
from jax.sharding import PartitionSpec as P

MODEL_WIDTH = 1024
HEADS = 8
HEAD = 128
NBOOK = 8
STEP = 5

EPSILON = 1e-05
NEGATIVE = -1e30
BETA_ONE = 0.9
BETA_TWO = 0.95
ADAM_EPSILON = 1e-08
WEIGHT_DECAY = 0.1
STEP_RATES = (0.06, 0.03, 0.4, 0.02, 0.03, 0.04, 0.5)

SEQ = ("far", "y", "x", "core")
PLANE = ("far", "y", "x")
SHARE = ("batch", "core")
LINE = ("batch", "far")
ALL = ("batch", "far", "y", "x", "core")
PIECE = 512
BLOCK = 128
GROUPS = 32
CHUNK = 256
BF16 = jnp.bfloat16
F32 = jnp.float32


def passed_along(value, steps):
    count = lax.axis_size(SEQ)
    initial, last = (max(0, -steps), min(count, count - steps))
    return lax.ppermute(value, SEQ, [(source, source + steps) for source in range(initial, last)])


def norm_forward(values, gain):
    center = values - jnp.mean(values, -1, keepdims=True)
    scaler = lax.rsqrt(jnp.mean(center * center, -1, keepdims=True) + EPSILON)
    unit_rows = center * scaler
    return (unit_rows * gain, unit_rows, scaler)


def norm_backward(grad_out, unit_rows, scaler, gain):
    scaled = grad_out * gain
    grad_gain = jnp.sum(grad_out * unit_rows, axis=0)
    grad_in = scaler * (
        scaled
        - jnp.mean(scaled, -1, keepdims=True)
        - unit_rows * jnp.mean(scaled * unit_rows, -1, keepdims=True)
    )
    return (grad_in, grad_gain)


def book_number(positions, book_ends):
    inside = jnp.sum((positions[:, None] >= book_ends[None, :]).astype(jnp.int32), -1)
    return jnp.where(positions < 0, -1, inside)


def matmul(left, right):
    return jnp.dot(left, right, preferred_element_type=F32)


def matmul_nt(left, right):
    return lax.dot_general(left, right, (((1,), (1,)), ((), ())), preferred_element_type=F32)


def matmul_tn(left, right):
    return lax.dot_general(left, right, (((0,), (0,)), ((), ())), preferred_element_type=F32)


def fill_bias(bias, key_book, key_pos, query_book, query_pos):
    allowed = (key_book[...] == query_book[...]) & (key_pos[...] <= query_pos[...])
    bias[...] = jnp.where(allowed, 0.0, NEGATIVE)


def attention_forward_body(*refs):
    query, own_k, own_v, mem_k, mem_v = refs[:5]
    marks, (out, log_total, bias) = refs[5:9], refs[9:]

    @pl.when(pl.program_id(0) == 0)
    def _():
        fill_bias(bias, *marks)

    keys = jnp.concatenate([own_k[...], mem_k[...]], 0)
    values = jnp.concatenate([own_v[...], mem_v[...]], 0)
    scores = matmul_nt(keys, query[...]) * HEAD ** (-0.5) + bias[...]
    top = jnp.max(scores, 0, keepdims=True)
    probs = jnp.exp(scores - top)
    total = jnp.sum(probs, 0, keepdims=True)
    log_total[0] = top + jnp.log(total)
    probs = (probs * (1.0 / total)).astype(BF16)
    out[...] = matmul_tn(values, probs).T.astype(BF16)


def attention_backward_body(*refs):
    query, own_k, own_v, mem_k, mem_v = refs[:5]
    marks = refs[5:9]
    log_total, grad_out, grad_query, grad_own, grad_mem, bias = refs[9:]

    @pl.when(pl.program_id(0) == 0)
    def _():
        fill_bias(bias, *marks)

    keys = jnp.concatenate([own_k[...], mem_k[...]], 0)
    values = jnp.concatenate([own_v[...], mem_v[...]], 0)
    scores = matmul_nt(keys, query[...]) * HEAD ** (-0.5) + bias[...]
    probs = jnp.exp(scores - log_total[0])
    grad_probs = matmul_nt(values, grad_out[...])
    inner = jnp.sum(probs * grad_probs, 0, keepdims=True)
    grad_scores = (probs * (grad_probs - inner) * HEAD ** (-0.5)).astype(BF16)
    grad_query[...] = matmul_tn(keys, grad_scores).T.astype(BF16)
    pair = (matmul(grad_scores, query[...]), matmul(probs.astype(BF16), grad_out[...]))
    at = 0
    for part in (grad_own, grad_mem):
        count = part.shape[1]
        for side in (0, 1):
            part[side] = pair[side][at : at + count].astype(part.dtype)
        at += count


def attention_specs(segment, others):
    def column(rows, shift):
        return pl.BlockSpec((rows, HEAD), lambda h: (0, h + shift * HEADS))

    mark_k = pl.BlockSpec((segment + others, 1), lambda h: (0, 0))
    mark_q = pl.BlockSpec((1, segment), lambda h: (0, 0))
    specs = [column(segment, 0), column(segment, 1), column(segment, 2)]
    specs += [column(others, 0), column(others, 1)]
    return specs + [mark_k, mark_k, mark_q, mark_q]


def attention_forward(projected, memory, marks):
    segment, others = projected.shape[0], memory.shape[0]
    keys = segment + others
    return pl.pallas_call(
        attention_forward_body,
        grid=(HEADS,),
        in_specs=attention_specs(segment, others),
        out_specs=[
            pl.BlockSpec((segment, HEAD), lambda h: (0, h)),
            pl.BlockSpec((1, 1, segment), lambda h: (h, 0, 0)),
        ],
        out_shape=[
            jax.ShapeDtypeStruct((segment, HEADS * HEAD), BF16),
            jax.ShapeDtypeStruct((HEADS, 1, segment), F32),
        ],
        scratch_shapes=[pltpu.VMEM((keys, segment), F32)],
        compiler_params=pltpu.CompilerParams(vmem_limit_bytes=48 << 20),
        cost_estimate=pl.CostEstimate(
            flops=4 * HEADS * keys * segment * HEAD,
            bytes_accessed=12 << 20,
            transcendentals=HEADS * keys * segment,
        ),
        name="attention_forward",
    )(projected, projected, projected, memory, memory, *marks)


def attention_backward(projected, memory, marks, log_total, grad_out):
    segment, others = projected.shape[0], memory.shape[0]
    keys = segment + others
    width = HEADS * HEAD

    def pair_spec(rows):
        return pl.BlockSpec((2, rows, HEAD), lambda h: (0, 0, h))

    return pl.pallas_call(
        attention_backward_body,
        grid=(HEADS,),
        in_specs=attention_specs(segment, others)
        + [
            pl.BlockSpec((1, 1, segment), lambda h: (h, 0, 0)),
            pl.BlockSpec((segment, HEAD), lambda h: (0, h)),
        ],
        out_specs=[pl.BlockSpec((segment, HEAD), lambda h: (0, h))]
        + [pair_spec(segment), pair_spec(others)],
        out_shape=[
            jax.ShapeDtypeStruct((segment, width), BF16),
            jax.ShapeDtypeStruct((2, segment, width), BF16),
            jax.ShapeDtypeStruct((2, others, width), BF16),
        ],
        scratch_shapes=[pltpu.VMEM((keys, segment), F32)],
        compiler_params=pltpu.CompilerParams(vmem_limit_bytes=48 << 20),
        cost_estimate=pl.CostEstimate(
            flops=10 * HEADS * keys * segment * HEAD,
            bytes_accessed=24 << 20,
            transcendentals=HEADS * keys * segment,
        ),
        name="attention_backward",
    )(projected, projected, projected, memory, memory, *marks, log_total, grad_out)


def adam_update(master, first, second, grad, rate):
    new_first = BETA_ONE * first + (1.0 - BETA_ONE) * grad
    new_second = BETA_TWO * second + (1.0 - BETA_TWO) * grad * grad
    first_hat = new_first / (1.0 - BETA_ONE**STEP)
    second_hat = new_second / (1.0 - BETA_TWO**STEP)
    new_master = master - rate * (
        first_hat / (jnp.sqrt(second_hat) + ADAM_EPSILON) + WEIGHT_DECAY * master
    )
    return [new_first, new_second, new_master]


def swapped(value, axis):
    return lax.ppermute(value, axis, [(0, 1), (1, 0)])


def grouped(buffer, sections):
    if buffer.shape[0] == GROUPS:
        return buffer
    parts, at = [], 0
    for count in sections:
        parts.append(buffer[:, at : at + count].reshape(GROUPS, -1, buffer.shape[2]))
        at += count
    return jnp.concatenate(parts, 1)


def matmul_packed(value, buffer, rows, first, count):
    size, depth = value.shape

    def body(value_ref, weight_ref, out):
        weight = weight_ref[...].reshape(depth, PIECE)
        out[...] = matmul(value_ref[...], weight).astype(BF16)

    return pl.pallas_call(
        body,
        grid=(count, 2),
        in_specs=[
            pl.BlockSpec((size, depth), lambda j, h: (0, 0)),
            pl.BlockSpec((GROUPS, rows, PIECE), lambda j, h: (0, first + j, h)),
        ],
        out_specs=pl.BlockSpec((size, PIECE), lambda j, h: (0, 2 * j + h)),
        out_shape=jax.ShapeDtypeStruct((size, count * 2 * PIECE), BF16),
        compiler_params=pltpu.CompilerParams(vmem_limit_bytes=48 << 20),
        cost_estimate=pl.CostEstimate(
            flops=4 * size * depth * count * PIECE,
            bytes_accessed=2 * depth * count * 1024,
            transcendentals=0,
        ),
        name="matmul_packed",
    )(value, buffer)


def matmul_packed_back(grads, buffer, rows, first, start=None):
    count, size, width = grads.shape
    depth = GROUPS * rows
    extra = [] if start is None else [start]

    def body(grad_ref, weight_ref, *rest):
        out = rest[-1]

        @pl.when(pl.program_id(0) == 0)
        def _():
            out[...] = jnp.zeros(out.shape, F32) if start is None else rest[0][...]

        out[...] += matmul_nt(grad_ref[0], weight_ref[...].reshape(depth, width))

    return pl.pallas_call(
        body,
        grid=(count,),
        in_specs=[
            pl.BlockSpec((1, size, width), lambda j: (j, 0, 0)),
            pl.BlockSpec((GROUPS, rows, width), lambda j: (0, first + j, 0)),
        ]
        + [pl.BlockSpec((size, depth), lambda j: (0, 0)) for _ in extra],
        out_specs=pl.BlockSpec((size, depth), lambda j: (0, 0)),
        out_shape=jax.ShapeDtypeStruct((size, depth), F32),
        compiler_params=pltpu.CompilerParams(vmem_limit_bytes=48 << 20),
        cost_estimate=pl.CostEstimate(
            flops=2 * size * depth * count * width,
            bytes_accessed=2 * depth * count * width,
            transcendentals=0,
        ),
        name="matmul_packed_back",
    )(grads, buffer, *extra)


GELU_SCALE = 0.7978845608028654
GELU_CUBE = 0.044715


def feed_forward(value, buffer, residual, chunk):
    size, width = value.shape
    blocks = (buffer.shape[1] - BLOCK) * GROUPS // width
    lines = width // (8 * chunk)

    def body(value_ref, first_ref, second_ref, residual_ref, out, pre, turned):
        hidden = matmul(value_ref[...], first_ref[...].reshape(width, width))
        pre[...] = hidden
        inner = jnp.tanh(GELU_SCALE * (hidden + GELU_CUBE * hidden * hidden * hidden))
        active = (0.5 * hidden * (1.0 + inner)).astype(BF16)

        @pl.when(pl.program_id(0) == 0)
        def _():
            out[...] = residual_ref[...]

        out[...] += matmul(active, second_ref[...].reshape(width, width))
        columns = active.T
        for line in range(lines):
            for place in range(8):
                target = place % 2 * 4 + place // 2
                at = (line * 8 + place) * chunk
                turned[target, line * chunk : (line + 1) * chunk] = columns[at : at + chunk]

    return pl.pallas_call(
        body,
        grid=(blocks,),
        in_specs=[
            pl.BlockSpec((size, width), lambda j: (0, 0)),
            pl.BlockSpec((GROUPS, width // GROUPS, width), lambda j: (0, j, 0)),
            pl.BlockSpec((width // BLOCK, BLOCK, width), lambda j: (j, 1, 0)),
            pl.BlockSpec((size, width), lambda j: (0, 0)),
        ],
        out_specs=[
            pl.BlockSpec((size, width), lambda j: (0, 0)),
            pl.BlockSpec((size, width), lambda j: (0, j)),
            pl.BlockSpec((8, width // 8, size), lambda j: (0, j, 0)),
        ],
        out_shape=[
            jax.ShapeDtypeStruct((size, width), F32),
            jax.ShapeDtypeStruct((size, blocks * width), F32),
            jax.ShapeDtypeStruct((8, blocks * width // 8, size), BF16),
        ],
        compiler_params=pltpu.CompilerParams(vmem_limit_bytes=56 << 20),
        cost_estimate=pl.CostEstimate(
            flops=4 * size * width * width * blocks,
            bytes_accessed=32 << 20,
            transcendentals=size * width * blocks,
        ),
        name="feed_forward",
    )(value, buffer, buffer, residual)


def feed_forward_back(grad, pre, buffer):
    size, width = grad.shape
    blocks = pre.shape[1] // width

    def body(grad_ref, pre_ref, first_ref, second_ref, grad_pre, out):
        grad_active = matmul_nt(grad_ref[...], second_ref[...].reshape(width, width))
        hidden = pre_ref[...]
        square = hidden * hidden
        inner = jnp.tanh(GELU_SCALE * hidden * (1.0 + GELU_CUBE * square))
        slope = 0.5 * (1.0 + inner) + 0.5 * hidden * (1.0 - inner * inner) * GELU_SCALE * (
            1.0 + 3.0 * GELU_CUBE * square
        )
        back = (grad_active * slope).astype(BF16)
        grad_pre[...] = back

        @pl.when(pl.program_id(0) == 0)
        def _():
            out[...] = jnp.zeros(out.shape, F32)

        out[...] += matmul_nt(back, first_ref[...].reshape(width, width))

    return pl.pallas_call(
        body,
        grid=(blocks,),
        in_specs=[
            pl.BlockSpec((size, width), lambda j: (0, 0)),
            pl.BlockSpec((size, width), lambda j: (0, j)),
            pl.BlockSpec((GROUPS, width // GROUPS, width), lambda j: (0, j, 0)),
            pl.BlockSpec((width // BLOCK, BLOCK, width), lambda j: (j, 1, 0)),
        ],
        out_specs=[
            pl.BlockSpec((size, width), lambda j: (0, j)),
            pl.BlockSpec((size, width), lambda j: (0, 0)),
        ],
        out_shape=[
            jax.ShapeDtypeStruct((size, blocks * width), BF16),
            jax.ShapeDtypeStruct((size, width), F32),
        ],
        compiler_params=pltpu.CompilerParams(vmem_limit_bytes=56 << 20),
        cost_estimate=pl.CostEstimate(
            flops=4 * size * width * width * blocks,
            bytes_accessed=32 << 20,
            transcendentals=size * width * blocks,
        ),
        name="feed_forward_back",
    )(grad, pre, buffer, buffer)


def grouped_transpose(rows):
    tokens, columns = rows.shape
    line = lax.axis_size(LINE)
    split = rows.reshape(tokens, line, 2, 2, 2, columns // (line * 8))
    return split.transpose(4, 2, 3, 1, 5, 0).reshape(8, columns // 8, tokens)


def core_halves(grouped):
    core = lax.axis_index("core")
    mine = lax.dynamic_slice_in_dim(grouped, 4 * core, 4, 0)
    other = lax.dynamic_slice_in_dim(grouped, 4 * (1 - core), 4, 0)
    return mine, swapped(other, "core")


def gradient_piece(weights, place, half, axis, moved, dtype):
    operands, specs, plan = [], [], []
    first = 0
    for products, blocks, wide in weights:
        for own, other, rhs_own, rhs_other, lead in products:
            tokens = own.shape[2]

            def inner(step, first=first, blocks=blocks):
                return jnp.clip(step - first, 0, blocks - 1)

            for side in (own, other):
                for free in (0, 1):
                    flip = 2 * free + moved if axis == "x" else 2 * moved + free

                    def lhs_map(step, me, flip=flip, inner=inner, wide=wide):
                        return (me[0] ^ flip, 0 if wide else inner(step), 0)

                    operands.append(side)
                    specs.append(pl.BlockSpec((1, BLOCK, tokens), lhs_map))
            for side in (rhs_own, rhs_other):

                def rhs_map(step, me, inner=inner, wide=wide, lead=lead):
                    return (lead, 0, 2 * inner(step) + half if wide else half)

                operands.append(side)
                specs.append(pl.BlockSpec((1, tokens, PIECE), rhs_map))
        plan.append((first, blocks, len(products)))
        first += blocks

    def body(me, *refs):
        out = refs[-1]
        step = pl.program_id(0)
        at = 0
        for start, blocks, count in plan:
            group = refs[at : at + 6 * count]

            @pl.when((step >= start) & (step < start + blocks))
            def _():
                total = jnp.zeros((2 * BLOCK, PIECE), F32)
                for k in range(0, 6 * count, 6):
                    near = jnp.concatenate([group[k][0], group[k + 1][0]], 0)
                    far = jnp.concatenate([group[k + 2][0], group[k + 3][0]], 0)
                    total += matmul(near, group[k + 4][0]) + matmul(far, group[k + 5][0])
                out[0] = total.astype(out.dtype)

            at += 6 * count

    return pl.pallas_call(
        body,
        grid_spec=pltpu.PrefetchScalarGridSpec(
            num_scalar_prefetch=1,
            grid=(first,),
            in_specs=specs,
            out_specs=pl.BlockSpec((1, 2 * BLOCK, PIECE), lambda step, me: (step, 0, 0)),
        ),
        out_shape=jax.ShapeDtypeStruct((first, 2 * BLOCK, PIECE), dtype),
        compiler_params=pltpu.CompilerParams(vmem_limit_bytes=40 << 20),
        cost_estimate=pl.CostEstimate(
            flops=first * 2 * 2 * BLOCK * PIECE * 1024,
            bytes_accessed=first * (3 << 20),
            transcendentals=0,
        ),
        name="gradient_piece",
    )(place, *operands)


def line_open(value):
    shape = value.shape[1:]
    count = lax.axis_size(LINE)
    return value, jnp.zeros(shape, BF16), jnp.zeros(shape, BF16), count - 1


def line_sends(state):
    value, upward, downward, steps = state
    count, index = lax.axis_size(LINE), lax.axis_index(LINE)
    above = lax.dynamic_index_in_dim(value, jnp.minimum(index + steps, count - 1), 0, False)
    below = lax.dynamic_index_in_dim(value, jnp.maximum(index - steps, 0), 0, False)
    return (above + upward.astype(F32)).astype(BF16), (below + downward.astype(F32)).astype(BF16)


def line_move(state, sends):
    steps = state[3]
    count = lax.axis_size(LINE)
    up = [(i, i + 1) for i in range(count - steps)]
    down = [(i, i - 1) for i in range(steps, count)]
    upward = lax.ppermute(sends[0], LINE, up)
    downward = lax.ppermute(sends[1], LINE, down)
    return state[0], upward, downward, steps - 1


def line_close(state):
    while state[3] > 0:
        state = line_move(state, lax.optimization_barrier(line_sends(state)))
    value, upward, downward, _ = state
    total = lax.dynamic_index_in_dim(value, lax.axis_index(LINE), 0, False)
    return total + upward.astype(F32) + downward.astype(F32)


def chip_place():
    place = lax.axis_index("y") * 2 + lax.axis_index("x")
    return jnp.reshape(place, (1,)).astype(jnp.int32)


def gradient_sends(weights, place):
    return [
        gradient_piece(weights, place, 0, "x", 1, BF16),
        gradient_piece(weights, place, 1, "y", 1, BF16),
    ]


def gradient_keeps(weights, place):
    return [
        gradient_piece(weights, place, 0, "x", 0, F32),
        gradient_piece(weights, place, 1, "y", 0, F32),
    ]


def plane_sums(sends, keeps):
    result = []
    for arrived, keep in zip(sends, keeps):
        count = keep.shape[1] // 2
        other = (keep[:, count:] + arrived[:, count:].astype(F32)).astype(BF16)
        result.append((keep[:, :count] + arrived[:, :count].astype(F32), other))
    return result


def plane_others(sums):
    return [swapped(other, axis) for (_, other), axis in zip(sums, ("y", "x"))]


def line_parts(weights, sums, others):
    line = lax.axis_size(LINE)
    joined = [mine + other.astype(F32) for (mine, _), other in zip(sums, others)]
    first, chunks = 0, []
    for weight in weights:
        blocks, wide = weight[1:]
        for part in range(blocks if wide else 1):
            count = 1 if wide else blocks
            pair = [
                half[first : first + count].reshape(line, count * BLOCK // line, PIECE)
                for half in joined
            ]
            chunks.append(jnp.concatenate(pair, -1))
            first += count
    return jnp.concatenate(chunks, 1)


class SmallSum:
    def __init__(self, value):
        count = lax.axis_size(LINE)
        self.value = value
        self.steps = [("core", 1)]
        step = 1
        while step < count:
            self.steps.append((LINE, step))
            step *= 2
        self.steps += [("x", 1), ("y", 1)]

    def exchange(self):
        axis, step = self.steps.pop(0)
        size = lax.axis_size(axis)
        return lax.ppermute(self.value, axis, [(i, i ^ step) for i in range(size)])

    def total(self):
        while self.steps:
            self.value = self.value + self.exchange()
        return self.value


def line_gather(block):
    return lax.all_gather(block, LINE, axis=0, tiled=False)


def plane_swaps(value):
    return swapped(value, "x"), swapped(value, "y")


def plane_corners(swaps):
    return swapped(swaps[0][..., :PIECE], "y"), swapped(swaps[1][..., PIECE:], "x")


def plane_gather(value, swaps, corners):
    line, rows, width = value.shape
    along_x, along_y = swaps
    pieces = (
        (value, 0, 0, 0),
        (along_x, 0, 1, 0),
        (along_y, 1, 0, 0),
        (corners[0], 1, 1, 0),
        (corners[1], 1, 1, PIECE),
    )
    y, x, core = (lax.axis_index(axis) for axis in ("y", "x", "core"))
    result = jnp.zeros((line, 2, 2, 2, rows, width), BF16)
    for piece, flip_y, flip_x, column in pieces:
        for flip in (0, 1):
            part = swapped(piece, "core") if flip else piece
            start = (0, y ^ flip_y, x ^ flip_x, core ^ flip, 0, column)
            result = lax.dynamic_update_slice(result, part[:, None, None, None], start)
    return result.reshape(8 * line, rows, width)


def share_combine(top, total):
    def merged(top, total, axis, pairs):
        pair = lax.ppermute(jnp.concatenate([top, total], 0), axis, pairs)
        best = jnp.maximum(top, pair[:1])
        return best, total * jnp.exp(top - best) + pair[1:] * jnp.exp(pair[:1] - best)

    top, total = merged(top, total, "core", [(0, 1), (1, 0)])
    count = lax.axis_size("batch")
    step = 1
    while step < count:
        top, total = merged(top, total, "batch", [(i, i ^ step) for i in range(count)])
        step *= 2
    return top + jnp.log(total)


def head_logits(rows, table, wanted):
    parts, part_rows, width = table.shape
    count = rows.shape[0]

    def body(rows_ref, table_ref, wanted_ref, logits, top, total, target):
        part = pl.program_id(0)

        @pl.when(part == 0)
        def _():
            top[...] = jnp.full(top.shape, NEGATIVE, F32)
            total[...] = jnp.zeros(total.shape, F32)
            target[...] = jnp.zeros(target.shape, F32)

        for at in range(0, count, CHUNK):
            span = slice(at, at + CHUNK)
            scores = matmul_nt(table_ref[0], rows_ref[span])
            logits[0, :, span] = scores
            best = jnp.maximum(top[:, span], jnp.max(scores, 0, keepdims=True))
            total[:, span] = total[:, span] * jnp.exp(top[:, span] - best) + jnp.sum(
                jnp.exp(scores - best), 0, keepdims=True
            )
            top[:, span] = best
            place = lax.broadcasted_iota(jnp.int32, scores.shape, 0)
            hit = place == wanted_ref[:, span] - part * part_rows
            target[:, span] += jnp.sum(jnp.where(hit, scores, 0.0), 0, keepdims=True)

    row = pl.BlockSpec((1, count), lambda p: (0, 0))
    return pl.pallas_call(
        body,
        grid=(parts,),
        in_specs=[
            pl.BlockSpec((count, width), lambda p: (0, 0)),
            pl.BlockSpec((1, part_rows, width), lambda p: (p, 0, 0)),
            row,
        ],
        out_specs=[pl.BlockSpec((1, part_rows, count), lambda p: (p, 0, 0)), row, row, row],
        out_shape=[jax.ShapeDtypeStruct((parts, part_rows, count), F32)]
        + [jax.ShapeDtypeStruct((1, count), F32)] * 3,
        compiler_params=pltpu.CompilerParams(vmem_limit_bytes=56 << 20),
        cost_estimate=pl.CostEstimate(
            flops=2 * parts * part_rows * count * width,
            bytes_accessed=4 * parts * part_rows * (count + width // 2),
            transcendentals=parts * part_rows * count,
        ),
        name="head_logits",
    )(rows, table, wanted)


def head_grad(logits, log_norm, weight, wanted, first):
    place = lax.broadcasted_iota(jnp.int32, logits.shape, 0)
    probs = jnp.exp(logits - log_norm)
    return (weight * jnp.where(place == wanted - first, probs - 1.0, probs)).astype(BF16)


def head_row_grads(logits, log_norm, weight, wanted, turned):
    parts, part_rows, count = logits.shape
    width, deep = turned.shape[1:]

    def body(logits_ref, log_norm_ref, weight_ref, wanted_ref, turned_ref, out, total):
        part = pl.program_id(0)
        @pl.when(part == 0)
        def _():
            total[...] = jnp.zeros(total.shape, F32)

        for at in range(0, count, CHUNK):
            span = slice(at, at + CHUNK)
            grad = head_grad(
                logits_ref[0, :, span],
                log_norm_ref[:, span],
                weight_ref[:, span],
                wanted_ref[:, span],
                part * part_rows,
            )
            if deep > part_rows:
                grad = jnp.concatenate([grad, jnp.zeros((deep - part_rows, CHUNK), BF16)], 0)
            total[:, span] += matmul(turned_ref[0], grad)

        @pl.when(part == parts - 1)
        def _():
            out[...] = total[...].T.astype(BF16)

    row = pl.BlockSpec((1, count), lambda p: (0, 0))
    return pl.pallas_call(
        body,
        grid=(parts,),
        in_specs=[
            pl.BlockSpec((1, part_rows, count), lambda p: (p, 0, 0)),
            row,
            row,
            row,
            pl.BlockSpec((1, width, deep), lambda p: (p, 0, 0)),
        ],
        out_specs=pl.BlockSpec((count, width), lambda p: (0, 0)),
        out_shape=jax.ShapeDtypeStruct((count, width), BF16),
        scratch_shapes=[pltpu.VMEM((width, count), F32)],
        compiler_params=pltpu.CompilerParams(vmem_limit_bytes=56 << 20),
        cost_estimate=pl.CostEstimate(
            flops=2 * parts * part_rows * count * width,
            bytes_accessed=4 * parts * part_rows * (count + width // 2),
            transcendentals=parts * part_rows * count,
        ),
        name="head_row_grads",
    )(logits, log_norm, weight, wanted, turned)


def head_table_grads(groups):
    parts, part_rows, count = groups[0][0].shape
    width = groups[0][4].shape[1]

    def body(*refs):
        out = refs[-1]
        total = jnp.zeros((part_rows, width), F32)
        for at in range(0, 5 * len(groups), 5):
            logits, log_norm, weight, wanted, rows = refs[at : at + 5]
            for start in range(0, count, CHUNK):
                span = slice(start, start + CHUNK)
                grad = head_grad(
                    logits[0, :, span],
                    log_norm[:, span],
                    weight[:, span],
                    wanted[:, span],
                    pl.program_id(0) * part_rows,
                )
                total += matmul(grad, rows[span])
        out[0] = total

    row = pl.BlockSpec((1, count), lambda p: (0, 0))
    specs = [
        pl.BlockSpec((1, part_rows, count), lambda p: (p, 0, 0)),
        row,
        row,
        row,
        pl.BlockSpec((count, width), lambda p: (0, 0)),
    ]
    return pl.pallas_call(
        body,
        grid=(parts,),
        in_specs=specs * len(groups),
        out_specs=pl.BlockSpec((1, part_rows, width), lambda p: (p, 0, 0)),
        out_shape=jax.ShapeDtypeStruct((parts, part_rows, width), F32),
        compiler_params=pltpu.CompilerParams(vmem_limit_bytes=58 << 20),
        cost_estimate=pl.CostEstimate(
            flops=2 * parts * part_rows * count * width * len(groups),
            bytes_accessed=4 * parts * part_rows * (count * len(groups) + width),
            transcendentals=parts * part_rows * count * len(groups),
        ),
        name="head_table_grads",
    )(*[value for group in groups for value in group])


def spread_piece(token_row, grads, table_grad, side, rows_of, dtype):
    part_rows = table_grad.shape[1]
    tokens = 1024
    first, second = rows_of

    def row_of(task):
        return first + task * (second - first)

    def body(token_ref, grads_ref, table_ref, out, total):
        step = pl.program_id(1)

        @pl.when(step == 0)
        def _():
            total[...] = table_ref[0]

        wanted = token_ref[...] - row_of(pl.program_id(0)) * part_rows
        hit = lax.broadcasted_iota(jnp.int32, (part_rows, tokens), 0) == wanted
        total[...] += matmul(jnp.where(hit, 1.0, 0.0).astype(BF16), grads_ref[...])

        @pl.when(step == pl.num_programs(1) - 1)
        def _():
            out[0] = total[...].astype(dtype)

    return pl.pallas_call(
        body,
        grid=(2, grads.shape[0] // tokens),
        in_specs=[
            pl.BlockSpec((1, tokens), lambda task, step: (0, step)),
            pl.BlockSpec((tokens, PIECE), lambda task, step: (step, side)),
            pl.BlockSpec((1, part_rows, PIECE), lambda task, step: (row_of(task), 0, side)),
        ],
        out_specs=pl.BlockSpec((1, part_rows, PIECE), lambda task, step: (task, 0, 0)),
        out_shape=jax.ShapeDtypeStruct((2, part_rows, PIECE), dtype),
        scratch_shapes=[pltpu.VMEM((part_rows, PIECE), F32)],
        compiler_params=pltpu.CompilerParams(vmem_limit_bytes=48 << 20),
        cost_estimate=pl.CostEstimate(
            flops=4 * part_rows * PIECE * grads.shape[0],
            bytes_accessed=12 << 20,
            transcendentals=0,
        ),
        name="spread_piece",
    )(token_row, grads, table_grad)


def column_blocks(rows):
    return jnp.concatenate(jnp.split(rows, rows.shape[1] // MODEL_WIDTH, 1), 0)


def bf16_parts(values):
    high = values.astype(BF16)
    rest = values - high.astype(F32)
    middle = rest.astype(BF16)
    low = (rest - middle.astype(F32)).astype(BF16)
    return high, middle, low


def per_device(token_ids, book_lengths, loss_mask, *state):
    masters, firsts, seconds = state[:7], state[7:14], state[14:]
    table_master, attn_in_m, attn_out_m, compress_m, ffn_in_m, ffn_out_m, gains_m = masters
    vocab_block = table_master.shape[0]
    batch_count = lax.axis_size("batch")
    seq_count = lax.axis_size(SEQ)
    plane_count = seq_count // 2
    share_count = batch_count * 2
    device_count = batch_count * seq_count
    segment = token_ids.shape[1]
    slots = -(-(segment // 3 + 1) // 16) * 16
    keep = segment // 2
    place = lax.axis_index(SEQ)
    offset = place * segment
    share_place = lax.axis_index(SHARE)
    width = MODEL_WIDTH

    own_tokens = token_ids.reshape(segment)
    share_tokens = lax.all_gather(own_tokens, SHARE, axis=0, tiled=True)
    rows_in = attn_in_m.size // width
    rows_out = attn_out_m.size // width
    rows_comp = compress_m.size // width
    rows_ffn = ffn_in_m.size // width
    rows_ffn_out = ffn_out_m.size // width
    gain_count = gains_m.size
    gain_block = jnp.zeros((16, width), BF16).at[0, :gain_count].set(
        gains_m.astype(BF16).reshape(-1)
    )
    mixer_block = jnp.concatenate(
        [
            column_blocks(attn_in_m.astype(BF16)),
            compress_m.astype(BF16),
            attn_out_m.astype(BF16),
            gain_block,
        ],
        0,
    )
    ffn_block = jnp.concatenate(
        [column_blocks(ffn_in_m.astype(BF16)), ffn_out_m.astype(BF16)], 0
    )
    own_table = lax.all_gather(table_master.astype(BF16), "far", axis=0, tiled=True)
    table_x, table_y = plane_swaps(own_table)
    mixer_line_all, ffn_line_all = line_gather(mixer_block), line_gather(ffn_block)
    table_x, table_y, mixer_line_all = lax.optimization_barrier(
        (table_x, table_y, mixer_line_all)
    )
    mixer_swaps = plane_swaps(mixer_line_all)
    part_rows = own_table.shape[0]
    table = jnp.zeros((4 * part_rows, width), BF16)
    for value, row, column in (
        (own_table, 0, 0),
        (table_x, 1, 0),
        (table_y, 2, 0),
        (swapped(table_x[:, :PIECE], "y"), 3, 0),
        (swapped(table_y[:, PIECE:], "x"), 3, PIECE),
    ):
        table = lax.dynamic_update_slice(table, value, (row * part_rows, column))

    def vocab_place(tokens):
        block = tokens // vocab_block
        seq_index = block % seq_count
        owner = block // seq_count * 2 + seq_index % 2
        chip = seq_index // 2 % 4
        part = chip ^ (lax.axis_index("y") * 2 + lax.axis_index("x"))
        inside = seq_index // 8 * vocab_block + tokens % vocab_block
        return owner, part * part_rows + inside

    share_owner, share_local = vocab_place(share_tokens)
    share_row = jnp.where(share_owner == share_place, share_local, -1)
    looked = jnp.where(
        (share_row >= 0)[:, None], table[jnp.maximum(share_row, 0)], jnp.zeros((), BF16)
    )

    looked, mixer_swaps, ffn_line_all = lax.optimization_barrier(
        (looked, mixer_swaps, ffn_line_all)
    )
    mixer_corners = plane_corners(mixer_swaps)
    table_again, mixer_corners, ffn_line_all = lax.optimization_barrier(
        (table, mixer_corners, ffn_line_all)
    )
    ffn_swaps = plane_swaps(ffn_line_all)
    mixer_all = plane_gather(mixer_line_all, mixer_swaps, mixer_corners)
    gains = mixer_all[:, rows_in + rows_comp + rows_out, :gain_count]
    token_rows = lax.psum_scatter(looked, SHARE, scatter_dimension=0, tiled=True)
    gains = gains.reshape(width, 3).astype(F32)
    table = table_again.reshape(4, part_rows, width)
    turned = jnp.pad(table, ((0, 0), (0, -part_rows % 128), (0, 0))).transpose(0, 2, 1)
    token_rows, turned, ffn_swaps = lax.optimization_barrier((token_rows, turned, ffn_swaps))
    part = attn_in_m.shape[0]
    mixer_all = grouped(mixer_all, (part, part, part, rows_comp, rows_out, 16))
    thin = width // GROUPS

    book_ends = jnp.cumsum(book_lengths.reshape(-1))
    own_pos = offset + jnp.arange(segment, dtype=jnp.int32)
    own_book = book_number(own_pos, book_ends)
    next_book = book_number(own_pos + 1, book_ends)
    own_mask = loss_mask.reshape(segment)
    numbers = jnp.arange(NBOOK, dtype=jnp.int32)
    live = own_mask.astype(F32) * (next_book == own_book).astype(F32)
    member = (own_book[:, None] == numbers[None, :]).astype(F32)
    book_counts = jnp.sum(member * live[:, None], 0)
    for axis in ("core", "x", "y"):
        book_counts = book_counts + swapped(book_counts, axis)
    book_counts = lax.psum(book_counts, "far")
    weight = live * jnp.sum(member / jnp.maximum(book_counts, 1.0)[None, :], -1)
    following = passed_along(own_tokens[:1], -1)
    targets = jnp.concatenate([own_tokens[1:], following])
    rank = jnp.cumsum(own_mask) - 1
    chosen = (rank[None, :] == jnp.arange(keep, dtype=jnp.int32)[:, None]) & (
        own_mask[None, :] > 0
    )
    picked_targets = jnp.sum(jnp.where(chosen, targets[None, :], 0), 1)
    picked_weight = jnp.sum(jnp.where(chosen, weight[None, :], 0.0), 1)

    embedded = token_rows.astype(F32) * width**0.5
    normed_one, unit_one, scale_one = norm_forward(embedded, gains[:, 0])
    attention_input = normed_one.astype(BF16)
    attention_input, ffn_swaps = lax.optimization_barrier((attention_input, ffn_swaps))
    ffn_all = plane_gather(ffn_line_all, ffn_swaps, plane_corners(ffn_swaps))
    ffn_all = grouped(ffn_all, (part,) * (rows_ffn // part) + (rows_ffn_out,))
    projected = matmul_packed(attention_input, mixer_all, thin, 0, 3)
    memory_rows = passed_along(attention_input, 1)
    tail_rows = passed_along(attention_input[segment - 2 :], 1)
    first_cell = jnp.mod(2 - offset, 3)
    padding = 3 * slots - segment + 2
    extended = jnp.concatenate([tail_rows, attention_input, jnp.zeros((padding, width), BF16)], 0)
    slot_rows = lax.dynamic_slice_in_dim(extended, first_cell, 3 * slots, 0).reshape(
        slots, 3 * width
    )
    compressed = matmul_packed(slot_rows, mixer_all, 3 * thin, 1, 1)
    other_rows = [memory_rows]
    spare = -(segment + 3 * slots) % BLOCK
    book_parts = [own_book, book_number(own_pos - segment, book_ends)]
    pos_parts = [own_pos, own_pos - segment]
    for hop in (2, 3, 4):
        other_rows.append(passed_along(compressed, hop))
        owner = place - hop
        last_pos = (
            owner * segment
            + jnp.mod(2 - owner * segment, 3)
            + 3 * jnp.arange(slots, dtype=jnp.int32)
        )
        last_book = book_number(last_pos, book_ends)
        usable = (owner >= 0) & (last_pos < owner * segment + segment)
        usable = usable & (book_number(last_pos - 2, book_ends) == last_book)
        book_parts.append(jnp.where(usable, last_book, -2))
        pos_parts.append(jnp.full((slots,), -1, jnp.int32))
    book_parts.append(jnp.full((spare,), -2, jnp.int32))
    pos_parts.append(jnp.full((spare,), -1, jnp.int32))
    other_rows.append(jnp.zeros((spare, width), BF16))
    marks = (
        jnp.concatenate(book_parts)[:, None],
        jnp.concatenate(pos_parts)[:, None],
        own_book[None, :],
        own_pos[None, :],
    )
    other_rows = jnp.concatenate(other_rows, 0)
    memory_pairs = matmul_packed(other_rows, mixer_all, thin, 1, 2)
    attended, log_total = attention_forward(projected, memory_pairs, marks)
    w_out = mixer_all[:, 6 * thin : 7 * thin].reshape(width, width)
    residual = embedded + matmul(attended, w_out)

    normed_two, unit_two, scale_two = norm_forward(residual, gains[:, 1])
    ffn_input = normed_two.astype(BF16)
    output_rows, pre_act, activated_turned = feed_forward(
        ffn_input, ffn_all, residual, rows_ffn_out
    )
    normed_three, unit_three, scale_three = norm_forward(output_rows, gains[:, 2])
    final_rows = normed_three.astype(BF16)

    chosen_bf16 = chosen.astype(BF16)
    picked_rows = matmul(chosen_bf16, final_rows).astype(BF16)
    high, middle, low = bf16_parts(picked_weight)
    side = jnp.concatenate(
        [
            (picked_targets // 256).astype(BF16),
            (picked_targets % 256).astype(BF16),
            high,
            middle,
            low,
        ]
    )
    side_rows = jnp.zeros((16 * width,), BF16).at[: 5 * keep].set(side).reshape(16, width)
    half = keep // 2
    head_one = lax.all_gather(
        jnp.concatenate([picked_rows[:half], side_rows], 0), SHARE, axis=0, tiled=False
    )
    slot_spare = -slots % BLOCK
    slot_tall = jnp.concatenate([slot_rows, jnp.zeros((slot_spare, 3 * width), BF16)], 0)
    halves = [
        core_halves(value)
        for value in (
            grouped_transpose(ffn_input),
            activated_turned,
            grouped_transpose(attention_input),
            grouped_transpose(other_rows),
            grouped_transpose(slot_tall),
            grouped_transpose(attended),
        )
    ]
    rows_one = head_one[:, :half].reshape(share_count * half, width)
    side_all = head_one[:, half:].reshape(share_count, 16 * width)[:, : 5 * keep]
    rows_one, next_rows, halves = lax.optimization_barrier((rows_one, picked_rows[half:], halves))
    rows_two = lax.all_gather(next_rows, SHARE, axis=0, tiled=True)
    side_all = side_all.reshape(share_count, 5, 2, half).astype(F32)
    side_all = side_all.transpose(1, 2, 0, 3).reshape(5, 2, share_count * half)
    wanted_all = (side_all[0] * 256.0 + side_all[1]).astype(jnp.int32)
    weight_all = side_all[2] + side_all[3] + side_all[4]
    wanted_owner, wanted_local = vocab_place(wanted_all)
    wanted_all = jnp.where(wanted_owner == share_place, wanted_local, -1)
    mine = (jnp.arange(share_count * half) // half == share_place).astype(F32)
    loss_local = jnp.zeros((), F32)
    groups, stats = [], []
    for index, rows in enumerate((rows_one, rows_two)):
        wanted, row_weight = wanted_all[index][None], weight_all[index][None]
        logits, top, total, target_logit = head_logits(rows, table, wanted)
        loss_local -= jnp.sum(row_weight * target_logit)
        stats.append((top, total))
        groups.append([logits, row_weight, wanted, rows])
    log_norms = [share_combine(*stats[0]), None]
    stats[1], log_norms[0] = lax.optimization_barrier((stats[1], log_norms[0]))
    log_norms[1] = share_combine(*stats[1])
    for index, (logits, row_weight, wanted, rows) in enumerate(groups):
        loss_local += jnp.sum(row_weight * mine[None] * log_norms[index])
        groups[index] = (logits, log_norms[index], row_weight, wanted, rows)
    grad_picked = []
    for group in groups:
        grad_rows = head_row_grads(*group[:4], turned)
        grad_picked.append(lax.psum_scatter(grad_rows, SHARE, scatter_dimension=0, tiled=True))
    grad_picked = jnp.concatenate(grad_picked, 0)
    grad_table = head_table_grads(groups)
    grad_picked, grad_table = lax.optimization_barrier((grad_picked, grad_table))
    grad_final = matmul_tn(chosen_bf16, grad_picked)

    grad_output_rows, grad_gain_three = norm_backward(
        grad_final, unit_three, scale_three, gains[:, 2]
    )
    grad_branch = grad_output_rows.astype(BF16)
    grad_pre, grad_norm_two = feed_forward_back(grad_branch, pre_act, ffn_all)

    def product(pair, grad, lead=0):
        return pair + (grad[0], grad[1], lead)

    def with_other(grad):
        grad = grad if grad.ndim == 3 else grad[None]
        return grad, swapped(grad, "core")

    out_weights = [
        (
            [product(halves[1], with_other(grad_branch))],
            rows_ffn_out * device_count // width,
            False,
        ),
    ]
    ffn_weights = [
        ([product(halves[0], with_other(grad_pre))], ffn_in_m.shape[1] // width, True),
    ]
    out_sends = gradient_sends(out_weights, chip_place())
    out_sends, grad_norm_two = lax.optimization_barrier((out_sends, grad_norm_two))
    out_arrived = [swapped(send, axis) for send, axis in zip(out_sends, ("x", "y"))]
    grad_res_two, grad_gain_two = norm_backward(grad_norm_two, unit_two, scale_two, gains[:, 1])
    grad_residual = grad_output_rows + grad_res_two

    grad_attn_branch = grad_residual.astype(BF16)
    grad_attended = matmul_nt(grad_attn_branch, w_out).astype(BF16)
    ffn_weights.append(([product(halves[5], with_other(grad_attn_branch))], 1, True))
    grad_query, grad_own, grad_other = attention_backward(
        projected, memory_pairs, marks, log_total, grad_attended
    )
    grad_other, out_arrived = lax.optimization_barrier((grad_other, out_arrived))
    grad_other_rows = matmul_packed_back(grad_other, mixer_all, thin, 1).astype(BF16)
    back_memory = passed_along(grad_other_rows[:segment], -1)
    returned = []
    for hop in (2, 3, 4):
        first_row = segment + (hop - 2) * slots
        returned.append(passed_along(grad_other_rows[first_row : first_row + slots], -hop))
    place, grad_query = lax.optimization_barrier((chip_place(), grad_query))
    ffn_sends = gradient_sends(ffn_weights, place)
    grad_input = matmul_packed_back(grad_query[None], mixer_all, thin, 0)
    grad_input = matmul_packed_back(grad_own, mixer_all, thin, 1, grad_input)
    returned, ffn_sends, grad_input = lax.optimization_barrier(
        (returned, ffn_sends, grad_input)
    )
    ffn_arrived = [swapped(send, axis) for send, axis in zip(ffn_sends, ("x", "y"))]
    grad_compressed = sum(part.astype(F32) for part in returned).astype(BF16)
    grad_slots = matmul_packed_back(grad_compressed[None], mixer_all, 3 * thin, 1)
    grad_slots = grad_slots.reshape(3 * slots, width)
    grad_first = jnp.concatenate([jnp.zeros((2, width), F32), grad_slots[:2]], 0)
    grad_first = lax.dynamic_slice_in_dim(grad_first, 2 - first_cell, 2, 0)
    back_tail = passed_along(grad_first.astype(BF16), -1).astype(F32)
    grad_input = grad_input + lax.dynamic_slice_in_dim(grad_slots, 2 - first_cell, segment, 0)
    grad_input = grad_input + back_memory.astype(F32)
    grad_input = grad_input.at[segment - 2 :].add(back_tail)
    grad_embed, grad_gain_one = norm_backward(grad_input, unit_one, scale_one, gains[:, 0])
    grad_scaled = ((grad_embed + grad_residual) * width**0.5).astype(BF16)

    query_pair, own_pair = with_other(grad_query), with_other(grad_own)
    other_pair = with_other(grad_other)
    slot_pair = with_other(jnp.pad(grad_compressed, ((0, slot_spare), (0, 0))))
    small = jnp.concatenate(
        [
            jnp.stack([grad_gain_one, grad_gain_two, grad_gain_three], 1).reshape(-1),
            jnp.full((128,), loss_local, F32),
        ]
    )
    grad_scaled, place, query_pair, own_pair, other_pair = lax.optimization_barrier(
        (grad_scaled, place, query_pair, own_pair, other_pair)
    )
    small = SmallSum(small)
    share_grads = lax.all_gather(grad_scaled, SHARE, axis=0, tiled=True)
    mixer_weights = [
        ([product(halves[2], query_pair)], 1, True),
        ([product(halves[2], own_pair, 0), product(halves[3], other_pair, 0)], 1, True),
        ([product(halves[2], own_pair, 1), product(halves[3], other_pair, 1)], 1, True),
        ([product(halves[4], slot_pair)], 3, False),
    ]
    mixer_sends = gradient_sends(mixer_weights, place)
    mixer_sends, place, arrived = lax.optimization_barrier(
        (mixer_sends, place, small.exchange())
    )
    small.value += arrived
    mixer_arrived = [swapped(send, axis) for send, axis in zip(mixer_sends, ("x", "y"))]
    out_sums = plane_sums(out_arrived, gradient_keeps(out_weights, place))
    out_sums, place, arrived = lax.optimization_barrier((out_sums, place, small.exchange()))
    small.value += arrived
    ffn_keeps = gradient_keeps(ffn_weights, place)
    ffn_keeps, place = lax.optimization_barrier((ffn_keeps, place))
    mixer_keeps = gradient_keeps(mixer_weights, place)
    ffn_arrived, mixer_keeps = lax.optimization_barrier((ffn_arrived, mixer_keeps))
    ffn_sums = plane_sums(ffn_arrived, ffn_keeps)
    mixer_sums = plane_sums(mixer_arrived, mixer_keeps)
    token_row, ffn_sums, mixer_sums, arrived = lax.optimization_barrier(
        (share_row[None, :], ffn_sums, mixer_sums, small.exchange())
    )
    small.value += arrived
    def spread(token_row, side, rows_of, dtype):
        piece = spread_piece(token_row, share_grads, grad_table, side, rows_of, dtype)
        return lax.optimization_barrier((piece, token_row))

    send_one, token_row = spread(token_row, 0, (1, 3), BF16)
    send_two, token_row = spread(token_row, 1, (2, 3), BF16)
    table_arrived = [swapped(send_one, "x"), swapped(send_two, "y")]
    others = [plane_others(sums) for sums in (out_sums, ffn_sums, mixer_sums)]
    others, token_row = lax.optimization_barrier((others, token_row))
    line = line_open(
        jnp.concatenate(
            [
                line_parts(out_weights, out_sums, others[0]),
                line_parts(ffn_weights, ffn_sums, others[1]),
                line_parts(mixer_weights, mixer_sums, others[2]),
            ],
            1,
        )
    )
    moves, token_row = lax.optimization_barrier((line_sends(line), token_row))
    line = line_move(line, moves)
    keep_one, token_row = spread(token_row, 0, (0, 2), F32)
    keep_two, token_row = spread(token_row, 1, (0, 1), F32)
    table_keeps = [keep_one, keep_two]
    table_keeps, table_arrived, moved = lax.optimization_barrier(
        (table_keeps, table_arrived, line[1:3])
    )
    summed = line_close((line[0], *moved, line[3]))
    ends = (rows_ffn_out, rows_ffn_out + rows_ffn, rows_ffn_out + rows_ffn + rows_out)
    ffn_out_grad, ffn_in_grad, attn_out_grad, mixer_grads = jnp.split(summed, ends)
    halves_new = []
    for arrived, keep_part, axis in zip(table_arrived, table_keeps, ("y", "x")):
        other = (keep_part[1] + arrived[1].astype(F32)).astype(BF16)
        mine = keep_part[0] + arrived[0].astype(F32)
        halves_new.append(mine + swapped(other, axis).astype(F32))
    halves_new, small.value = lax.optimization_barrier((halves_new, small.value))
    grad_table = jnp.concatenate(halves_new, 1)
    if lax.axis_size("far") > 1:
        grad_table = lax.psum_scatter(
            grad_table.astype(BF16), "far", scatter_dimension=0, tiled=True
        )

    small = small.total()
    loss_total = small[3 * width]
    device = lax.axis_index(ALL)
    gain_grads = lax.dynamic_slice_in_dim(small, device * gain_count, gain_count, 0)

    def side_by_side(rows, count):
        return jnp.concatenate(jnp.split(rows, count, 0), 1)

    low, high = rows_in, rows_in + rows_comp
    grads = (
        grad_table,
        side_by_side(mixer_grads[:low], 3),
        attn_out_grad,
        mixer_grads[low:high],
        side_by_side(ffn_in_grad, rows_ffn // attn_in_m.shape[0]),
        ffn_out_grad,
        gain_grads.reshape(gains_m.shape),
    )
    results = []
    for master, first, second, grad, rate in zip(masters, firsts, seconds, grads, STEP_RATES):
        results.extend(adam_update(master, first, second, grad.astype(F32), rate))
    return (loss_total,) + tuple(results)


def solution(mesh):
    batch_count, seq_count = mesh.shape["batch"], mesh.shape["seq"]
    devices = mesh.devices.reshape(batch_count, seq_count // 8, 2, 2, 2)
    grid = Mesh(devices, ALL)
    rows = P(ALL, None)
    return jax.shard_map(
        per_device,
        mesh=grid,
        in_specs=(P("batch", SEQ), P("batch", None), P("batch", SEQ)) + (rows,) * 21,
        out_specs=(P(),) + (rows,) * 21,
        check_vma=False,
    )
```

```python
import jax
import jax.numpy as jnp
from jax import lax
from jax.experimental import pallas as pl
from jax.experimental.pallas import tpu as pltpu
from jax.sharding import Mesh
from jax.sharding import PartitionSpec as P

MODEL_WIDTH = 1024
HEADS = 8
HEAD = 128
NBOOK = 8
STEP = 5

EPSILON = 1e-05
NEGATIVE = -1e30
BETA_ONE = 0.9
BETA_TWO = 0.95
ADAM_EPSILON = 1e-08
WEIGHT_DECAY = 0.1
STEP_RATES = (0.06, 0.03, 0.4, 0.02, 0.03, 0.04, 0.5)

SEQ = ("far", "y", "x", "core")
PLANE = ("far", "y", "x")
SHARE = ("batch", "core")
LINE = ("batch", "far")
ALL = ("batch", "far", "y", "x", "core")
PIECE = 512
BLOCK = 128
GROUPS = 32
CHUNK = 256
TOGETHER = 2
STRIP = TOGETHER * HEAD
BF16 = jnp.bfloat16
F32 = jnp.float32


def passed_along(value, steps):
    count = lax.axis_size(SEQ)
    initial, last = (max(0, -steps), min(count, count - steps))
    return lax.ppermute(value, SEQ, [(source, source + steps) for source in range(initial, last)])


def norm_forward(values, gain):
    center = values - jnp.mean(values, -1, keepdims=True)
    scaler = lax.rsqrt(jnp.mean(center * center, -1, keepdims=True) + EPSILON)
    unit_rows = center * scaler
    return (unit_rows * gain, unit_rows, scaler)


def norm_backward(grad_out, unit_rows, scaler, gain):
    scaled = grad_out * gain
    grad_gain = jnp.sum(grad_out * unit_rows, axis=0)
    grad_in = scaler * (
        scaled
        - jnp.mean(scaled, -1, keepdims=True)
        - unit_rows * jnp.mean(scaled * unit_rows, -1, keepdims=True)
    )
    return (grad_in, grad_gain)


def book_number(positions, book_ends):
    inside = jnp.sum((positions[:, None] >= book_ends[None, :]).astype(jnp.int32), -1)
    return jnp.where(positions < 0, -1, inside)


def matmul(left, right):
    return jnp.dot(left, right, preferred_element_type=F32)


def matmul_nt(left, right):
    return lax.dot_general(left, right, (((1,), (1,)), ((), ())), preferred_element_type=F32)


def matmul_tn(left, right):
    return lax.dot_general(left, right, (((0,), (0,)), ((), ())), preferred_element_type=F32)


def fill_bias(bias, key_book, key_pos, query_book, query_pos):
    allowed = (key_book[...] == query_book[...]) & (key_pos[...] <= query_pos[...])
    bias[...] = jnp.where(allowed, 0.0, NEGATIVE)


def attention_forward_body(*refs):
    query, own_k, own_v, mem_k, mem_v = refs[:5]
    marks, (out, log_total, bias) = refs[5:9], refs[9:]

    @pl.when(pl.program_id(0) == 0)
    def _():
        fill_bias(bias, *marks)

    for index in range(TOGETHER):
        head = slice(index * HEAD, (index + 1) * HEAD)
        keys = jnp.concatenate([own_k[:, head], mem_k[:, head]], 0)
        values = jnp.concatenate([own_v[:, head], mem_v[:, head]], 0)
        scores = matmul_nt(keys, query[:, head]) * HEAD ** (-0.5) + bias[...]
        top = jnp.max(scores, 0, keepdims=True)
        probs = jnp.exp(scores - top)
        total = jnp.sum(probs, 0, keepdims=True)
        log_total[index] = top + jnp.log(total)
        probs = (probs * (1.0 / total)).astype(BF16)
        out[:, head] = matmul_tn(values, probs).T.astype(BF16)


def attention_backward_body(*refs):
    query, own_k, own_v, mem_k, mem_v = refs[:5]
    marks = refs[5:9]
    log_total, grad_out, grad_query, grad_own, grad_mem, bias = refs[9:]

    @pl.when(pl.program_id(0) == 0)
    def _():
        fill_bias(bias, *marks)

    for index in range(TOGETHER):
        head = slice(index * HEAD, (index + 1) * HEAD)
        keys = jnp.concatenate([own_k[:, head], mem_k[:, head]], 0)
        values = jnp.concatenate([own_v[:, head], mem_v[:, head]], 0)
        scores = matmul_nt(keys, query[:, head]) * HEAD ** (-0.5) + bias[...]
        probs = jnp.exp(scores - log_total[index])
        grad_probs = matmul_nt(values, grad_out[:, head])
        inner = jnp.sum(probs * grad_probs, 0, keepdims=True)
        grad_scores = (probs * (grad_probs - inner) * HEAD ** (-0.5)).astype(BF16)
        grad_query[:, head] = matmul_tn(keys, grad_scores).T.astype(BF16)
        pair = (
            matmul(grad_scores, query[:, head]),
            matmul(probs.astype(BF16), grad_out[:, head]),
        )
        at = 0
        for part in (grad_own, grad_mem):
            count = part.shape[1]
            for side in (0, 1):
                part[side, :, head] = pair[side][at : at + count].astype(part.dtype)
            at += count


def attention_specs(segment, others):
    def column(rows, shift):
        return pl.BlockSpec((rows, STRIP), lambda h: (0, h + shift * HEADS // TOGETHER))

    mark_k = pl.BlockSpec((segment + others, 1), lambda h: (0, 0))
    mark_q = pl.BlockSpec((1, segment), lambda h: (0, 0))
    specs = [column(segment, 0), column(segment, 1), column(segment, 2)]
    specs += [column(others, 0), column(others, 1)]
    return specs + [mark_k, mark_k, mark_q, mark_q]


def attention_forward(projected, memory, marks):
    segment, others = projected.shape[0], memory.shape[0]
    keys = segment + others
    return pl.pallas_call(
        attention_forward_body,
        grid=(HEADS // TOGETHER,),
        in_specs=attention_specs(segment, others),
        out_specs=[
            pl.BlockSpec((segment, STRIP), lambda h: (0, h)),
            pl.BlockSpec((TOGETHER, 1, segment), lambda h: (h, 0, 0)),
        ],
        out_shape=[
            jax.ShapeDtypeStruct((segment, HEADS * HEAD), BF16),
            jax.ShapeDtypeStruct((HEADS, 1, segment), F32),
        ],
        scratch_shapes=[pltpu.VMEM((keys, segment), F32)],
        compiler_params=pltpu.CompilerParams(vmem_limit_bytes=56 << 20),
        cost_estimate=pl.CostEstimate(
            flops=4 * HEADS * keys * segment * HEAD,
            bytes_accessed=12 << 20,
            transcendentals=HEADS * keys * segment,
        ),
        name="attention_forward",
    )(projected, projected, projected, memory, memory, *marks)


def attention_backward(projected, memory, marks, log_total, grad_out):
    segment, others = projected.shape[0], memory.shape[0]
    keys = segment + others
    width = HEADS * HEAD

    def pair_spec(rows):
        return pl.BlockSpec((2, rows, STRIP), lambda h: (0, 0, h))

    return pl.pallas_call(
        attention_backward_body,
        grid=(HEADS // TOGETHER,),
        in_specs=attention_specs(segment, others)
        + [
            pl.BlockSpec((TOGETHER, 1, segment), lambda h: (h, 0, 0)),
            pl.BlockSpec((segment, STRIP), lambda h: (0, h)),
        ],
        out_specs=[pl.BlockSpec((segment, STRIP), lambda h: (0, h))]
        + [pair_spec(segment), pair_spec(others)],
        out_shape=[
            jax.ShapeDtypeStruct((segment, width), BF16),
            jax.ShapeDtypeStruct((2, segment, width), BF16),
            jax.ShapeDtypeStruct((2, others, width), BF16),
        ],
        scratch_shapes=[pltpu.VMEM((keys, segment), F32)],
        compiler_params=pltpu.CompilerParams(vmem_limit_bytes=56 << 20),
        cost_estimate=pl.CostEstimate(
            flops=10 * HEADS * keys * segment * HEAD,
            bytes_accessed=24 << 20,
            transcendentals=HEADS * keys * segment,
        ),
        name="attention_backward",
    )(projected, projected, projected, memory, memory, *marks, log_total, grad_out)


def adam_update(master, first, second, grad, rate):
    new_first = BETA_ONE * first + (1.0 - BETA_ONE) * grad
    new_second = BETA_TWO * second + (1.0 - BETA_TWO) * grad * grad
    first_hat = new_first / (1.0 - BETA_ONE**STEP)
    second_hat = new_second / (1.0 - BETA_TWO**STEP)
    new_master = master - rate * (
        first_hat / (jnp.sqrt(second_hat) + ADAM_EPSILON) + WEIGHT_DECAY * master
    )
    return [new_first, new_second, new_master]


def swapped(value, axis):
    return lax.ppermute(value, axis, [(0, 1), (1, 0)])


def grouped(buffer, sections):
    if buffer.shape[0] == GROUPS:
        return buffer
    parts, at = [], 0
    for count in sections:
        parts.append(buffer[:, at : at + count].reshape(GROUPS, -1, buffer.shape[2]))
        at += count
    return jnp.concatenate(parts, 1)


def matmul_packed(value, buffer, rows, first, count):
    size, depth = value.shape

    def body(value_ref, weight_ref, out):
        weight = weight_ref[...].reshape(depth, PIECE)
        out[...] = matmul(value_ref[...], weight).astype(BF16)

    return pl.pallas_call(
        body,
        grid=(count, 2),
        in_specs=[
            pl.BlockSpec((size, depth), lambda j, h: (0, 0)),
            pl.BlockSpec((GROUPS, rows, PIECE), lambda j, h: (0, first + j, h)),
        ],
        out_specs=pl.BlockSpec((size, PIECE), lambda j, h: (0, 2 * j + h)),
        out_shape=jax.ShapeDtypeStruct((size, count * 2 * PIECE), BF16),
        compiler_params=pltpu.CompilerParams(vmem_limit_bytes=48 << 20),
        cost_estimate=pl.CostEstimate(
            flops=4 * size * depth * count * PIECE,
            bytes_accessed=2 * depth * count * 1024,
            transcendentals=0,
        ),
        name="matmul_packed",
    )(value, buffer)


def matmul_packed_back(grads, buffer, rows, first, start=None):
    count, size, width = grads.shape
    depth = GROUPS * rows
    extra = [] if start is None else [start]

    def body(grad_ref, weight_ref, *rest):
        out = rest[-1]

        @pl.when(pl.program_id(0) == 0)
        def _():
            out[...] = jnp.zeros(out.shape, F32) if start is None else rest[0][...]

        out[...] += matmul_nt(grad_ref[0], weight_ref[...].reshape(depth, width))

    return pl.pallas_call(
        body,
        grid=(count,),
        in_specs=[
            pl.BlockSpec((1, size, width), lambda j: (j, 0, 0)),
            pl.BlockSpec((GROUPS, rows, width), lambda j: (0, first + j, 0)),
        ]
        + [pl.BlockSpec((size, depth), lambda j: (0, 0)) for _ in extra],
        out_specs=pl.BlockSpec((size, depth), lambda j: (0, 0)),
        out_shape=jax.ShapeDtypeStruct((size, depth), F32),
        compiler_params=pltpu.CompilerParams(vmem_limit_bytes=48 << 20),
        cost_estimate=pl.CostEstimate(
            flops=2 * size * depth * count * width,
            bytes_accessed=2 * depth * count * width,
            transcendentals=0,
        ),
        name="matmul_packed_back",
    )(grads, buffer, *extra)


GELU_SCALE = 0.7978845608028654
GELU_CUBE = 0.044715


def feed_forward(value, buffer, residual, chunk):
    size, width = value.shape
    blocks = (buffer.shape[1] - BLOCK) * GROUPS // width
    lines = width // (8 * chunk)

    def body(value_ref, first_ref, second_ref, residual_ref, out, pre, turned):
        @pl.when(pl.program_id(0) == 0)
        def _():
            out[...] = residual_ref[...]

        parts = []
        for at in range(0, size, CHUNK):
            span = slice(at, at + CHUNK)
            hidden = matmul(value_ref[span], first_ref[...].reshape(width, width))
            pre[span] = hidden
            inner = jnp.tanh(GELU_SCALE * (hidden + GELU_CUBE * hidden * hidden * hidden))
            active = (0.5 * hidden * (1.0 + inner)).astype(BF16)
            out[span] += matmul(active, second_ref[...].reshape(width, width))
            parts.append(active)
        active = jnp.concatenate(parts, 0)
        columns = active.T
        for line in range(lines):
            for place in range(8):
                target = place % 2 * 4 + place // 2
                at = (line * 8 + place) * chunk
                turned[target, line * chunk : (line + 1) * chunk] = columns[at : at + chunk]

    return pl.pallas_call(
        body,
        grid=(blocks,),
        in_specs=[
            pl.BlockSpec((size, width), lambda j: (0, 0)),
            pl.BlockSpec((GROUPS, width // GROUPS, width), lambda j: (0, j, 0)),
            pl.BlockSpec((width // BLOCK, BLOCK, width), lambda j: (j, 1, 0)),
            pl.BlockSpec((size, width), lambda j: (0, 0)),
        ],
        out_specs=[
            pl.BlockSpec((size, width), lambda j: (0, 0)),
            pl.BlockSpec((size, width), lambda j: (0, j)),
            pl.BlockSpec((8, width // 8, size), lambda j: (0, j, 0)),
        ],
        out_shape=[
            jax.ShapeDtypeStruct((size, width), F32),
            jax.ShapeDtypeStruct((size, blocks * width), F32),
            jax.ShapeDtypeStruct((8, blocks * width // 8, size), BF16),
        ],
        compiler_params=pltpu.CompilerParams(vmem_limit_bytes=56 << 20),
        cost_estimate=pl.CostEstimate(
            flops=4 * size * width * width * blocks,
            bytes_accessed=32 << 20,
            transcendentals=size * width * blocks,
        ),
        name="feed_forward",
    )(value, buffer, buffer, residual)


def feed_forward_back(grad, pre, buffer):
    size, width = grad.shape
    blocks = pre.shape[1] // width

    def body(grad_ref, pre_ref, first_ref, second_ref, grad_pre, out):
        @pl.when(pl.program_id(0) == 0)
        def _():
            out[...] = jnp.zeros(out.shape, F32)

        for at in range(0, size, CHUNK):
            span = slice(at, at + CHUNK)
            grad_active = matmul_nt(grad_ref[span], second_ref[...].reshape(width, width))
            hidden = pre_ref[span]
            square = hidden * hidden
            inner = jnp.tanh(GELU_SCALE * hidden * (1.0 + GELU_CUBE * square))
            slope = 0.5 * (1.0 + inner) + 0.5 * hidden * (1.0 - inner * inner) * GELU_SCALE * (
                1.0 + 3.0 * GELU_CUBE * square
            )
            back = (grad_active * slope).astype(BF16)
            grad_pre[span] = back
            out[span] += matmul_nt(back, first_ref[...].reshape(width, width))

    return pl.pallas_call(
        body,
        grid=(blocks,),
        in_specs=[
            pl.BlockSpec((size, width), lambda j: (0, 0)),
            pl.BlockSpec((size, width), lambda j: (0, j)),
            pl.BlockSpec((GROUPS, width // GROUPS, width), lambda j: (0, j, 0)),
            pl.BlockSpec((width // BLOCK, BLOCK, width), lambda j: (j, 1, 0)),
        ],
        out_specs=[
            pl.BlockSpec((size, width), lambda j: (0, j)),
            pl.BlockSpec((size, width), lambda j: (0, 0)),
        ],
        out_shape=[
            jax.ShapeDtypeStruct((size, blocks * width), BF16),
            jax.ShapeDtypeStruct((size, width), F32),
        ],
        compiler_params=pltpu.CompilerParams(vmem_limit_bytes=56 << 20),
        cost_estimate=pl.CostEstimate(
            flops=4 * size * width * width * blocks,
            bytes_accessed=32 << 20,
            transcendentals=size * width * blocks,
        ),
        name="feed_forward_back",
    )(grad, pre, buffer, buffer)


def grouped_transpose(rows):
    tokens, columns = rows.shape
    line = lax.axis_size(LINE)
    split = rows.reshape(tokens, line, 2, 2, 2, columns // (line * 8))
    return split.transpose(4, 2, 3, 1, 5, 0).reshape(8, columns // 8, tokens)


def core_halves(grouped):
    core = lax.axis_index("core")
    mine = lax.dynamic_slice_in_dim(grouped, 4 * core, 4, 0)
    other = lax.dynamic_slice_in_dim(grouped, 4 * (1 - core), 4, 0)
    return mine, swapped(other, "core")


def gradient_piece(weights, place, half, axis, moved, dtype):
    operands, specs, plan = [], [], []
    first = 0
    for products, blocks, wide in weights:
        for own, other, rhs_own, rhs_other, lead in products:
            tokens = own.shape[2]

            def inner(step, first=first, blocks=blocks):
                return jnp.clip(step - first, 0, blocks - 1)

            for side in (own, other):
                for free in (0, 1):
                    flip = 2 * free + moved if axis == "x" else 2 * moved + free

                    def lhs_map(step, me, flip=flip, inner=inner, wide=wide):
                        return (me[0] ^ flip, 0 if wide else inner(step), 0)

                    operands.append(side)
                    specs.append(pl.BlockSpec((1, BLOCK, tokens), lhs_map))
            for side in (rhs_own, rhs_other):

                def rhs_map(step, me, inner=inner, wide=wide, lead=lead):
                    return (lead, 0, 2 * inner(step) + half if wide else half)

                operands.append(side)
                specs.append(pl.BlockSpec((1, tokens, PIECE), rhs_map))
        plan.append((first, blocks, len(products)))
        first += blocks

    def body(me, *refs):
        out = refs[-1]
        step = pl.program_id(0)
        at = 0
        for start, blocks, count in plan:
            group = refs[at : at + 6 * count]

            @pl.when((step >= start) & (step < start + blocks))
            def _():
                total = jnp.zeros((2 * BLOCK, PIECE), F32)
                for k in range(0, 6 * count, 6):
                    near = jnp.concatenate([group[k][0], group[k + 1][0]], 0)
                    far = jnp.concatenate([group[k + 2][0], group[k + 3][0]], 0)
                    total += matmul(near, group[k + 4][0]) + matmul(far, group[k + 5][0])
                out[0] = total.astype(out.dtype)

            at += 6 * count

    return pl.pallas_call(
        body,
        grid_spec=pltpu.PrefetchScalarGridSpec(
            num_scalar_prefetch=1,
            grid=(first,),
            in_specs=specs,
            out_specs=pl.BlockSpec((1, 2 * BLOCK, PIECE), lambda step, me: (step, 0, 0)),
        ),
        out_shape=jax.ShapeDtypeStruct((first, 2 * BLOCK, PIECE), dtype),
        compiler_params=pltpu.CompilerParams(vmem_limit_bytes=40 << 20),
        cost_estimate=pl.CostEstimate(
            flops=first * 2 * 2 * BLOCK * PIECE * 1024,
            bytes_accessed=first * (3 << 20),
            transcendentals=0,
        ),
        name="gradient_piece",
    )(place, *operands)


def line_open(value):
    shape = value.shape[1:]
    count = lax.axis_size(LINE)
    return value, jnp.zeros(shape, BF16), jnp.zeros(shape, BF16), count - 1


def line_sends(state):
    value, upward, downward, steps = state
    count, index = lax.axis_size(LINE), lax.axis_index(LINE)
    above = lax.dynamic_index_in_dim(value, jnp.minimum(index + steps, count - 1), 0, False)
    below = lax.dynamic_index_in_dim(value, jnp.maximum(index - steps, 0), 0, False)
    return (above + upward.astype(F32)).astype(BF16), (below + downward.astype(F32)).astype(BF16)


def line_move(state, sends):
    steps = state[3]
    count = lax.axis_size(LINE)
    up = [(i, i + 1) for i in range(count - steps)]
    down = [(i, i - 1) for i in range(steps, count)]
    upward = lax.ppermute(sends[0], LINE, up)
    downward = lax.ppermute(sends[1], LINE, down)
    return state[0], upward, downward, steps - 1


def line_close(state):
    while state[3] > 0:
        state = line_move(state, lax.optimization_barrier(line_sends(state)))
    value, upward, downward, _ = state
    total = lax.dynamic_index_in_dim(value, lax.axis_index(LINE), 0, False)
    return total + upward.astype(F32) + downward.astype(F32)


def chip_place():
    place = lax.axis_index("y") * 2 + lax.axis_index("x")
    return jnp.reshape(place, (1,)).astype(jnp.int32)


def gradient_sends(weights, place):
    return [
        gradient_piece(weights, place, 0, "x", 1, BF16),
        gradient_piece(weights, place, 1, "y", 1, BF16),
    ]


def gradient_keeps(weights, place):
    return [
        gradient_piece(weights, place, 0, "x", 0, F32),
        gradient_piece(weights, place, 1, "y", 0, F32),
    ]


def plane_sums(sends, keeps):
    result = []
    for arrived, keep in zip(sends, keeps):
        count = keep.shape[1] // 2
        other = (keep[:, count:] + arrived[:, count:].astype(F32)).astype(BF16)
        result.append((keep[:, :count] + arrived[:, :count].astype(F32), other))
    return result


def plane_others(sums):
    return [swapped(other, axis) for (_, other), axis in zip(sums, ("y", "x"))]


def line_parts(weights, sums, others):
    line = lax.axis_size(LINE)
    joined = [mine + other.astype(F32) for (mine, _), other in zip(sums, others)]
    first, chunks = 0, []
    for weight in weights:
        blocks, wide = weight[1:]
        for part in range(blocks if wide else 1):
            count = 1 if wide else blocks
            pair = [
                half[first : first + count].reshape(line, count * BLOCK // line, PIECE)
                for half in joined
            ]
            chunks.append(jnp.concatenate(pair, -1))
            first += count
    return jnp.concatenate(chunks, 1)


class SmallSum:
    def __init__(self, value):
        count = lax.axis_size(LINE)
        self.value = value
        self.steps = [("core", 1)]
        step = 1
        while step < count:
            self.steps.append((LINE, step))
            step *= 2
        self.steps += [("x", 1), ("y", 1)]

    def exchange(self):
        axis, step = self.steps.pop(0)
        size = lax.axis_size(axis)
        return lax.ppermute(self.value, axis, [(i, i ^ step) for i in range(size)])

    def total(self):
        while self.steps:
            self.value = self.value + self.exchange()
        return self.value


def line_gather(block):
    return lax.all_gather(block, LINE, axis=0, tiled=False)


def plane_swaps(value):
    return swapped(value, "x"), swapped(value, "y")


def plane_corners(swaps):
    return swapped(swaps[0][..., :PIECE], "y"), swapped(swaps[1][..., PIECE:], "x")


def plane_gather(value, swaps, corners):
    line, rows, width = value.shape
    along_x, along_y = swaps
    pieces = (
        (value, 0, 0, 0),
        (along_x, 0, 1, 0),
        (along_y, 1, 0, 0),
        (corners[0], 1, 1, 0),
        (corners[1], 1, 1, PIECE),
    )
    y, x, core = (lax.axis_index(axis) for axis in ("y", "x", "core"))
    result = jnp.zeros((line, 2, 2, 2, rows, width), BF16)
    for piece, flip_y, flip_x, column in pieces:
        for flip in (0, 1):
            part = swapped(piece, "core") if flip else piece
            start = (0, y ^ flip_y, x ^ flip_x, core ^ flip, 0, column)
            result = lax.dynamic_update_slice(result, part[:, None, None, None], start)
    return result.reshape(8 * line, rows, width)


def share_combine(top, total):
    def merged(top, total, axis, pairs):
        pair = lax.ppermute(jnp.concatenate([top, total], 0), axis, pairs)
        best = jnp.maximum(top, pair[:1])
        return best, total * jnp.exp(top - best) + pair[1:] * jnp.exp(pair[:1] - best)

    top, total = merged(top, total, "core", [(0, 1), (1, 0)])
    count = lax.axis_size("batch")
    step = 1
    while step < count:
        top, total = merged(top, total, "batch", [(i, i ^ step) for i in range(count)])
        step *= 2
    return top + jnp.log(total)


def head_logits(rows, table, wanted):
    parts, part_rows, width = table.shape
    count = rows.shape[0]

    def body(rows_ref, table_ref, wanted_ref, logits, top, total, target):
        part = pl.program_id(0)

        @pl.when(part == 0)
        def _():
            top[...] = jnp.full(top.shape, NEGATIVE, F32)
            total[...] = jnp.zeros(total.shape, F32)
            target[...] = jnp.zeros(target.shape, F32)

        for at in range(0, count, CHUNK):
            span = slice(at, at + CHUNK)
            scores = matmul_nt(table_ref[0], rows_ref[span])
            logits[0, :, span] = scores
            best = jnp.maximum(top[:, span], jnp.max(scores, 0, keepdims=True))
            total[:, span] = total[:, span] * jnp.exp(top[:, span] - best) + jnp.sum(
                jnp.exp(scores - best), 0, keepdims=True
            )
            top[:, span] = best
            place = lax.broadcasted_iota(jnp.int32, scores.shape, 0)
            hit = place == wanted_ref[:, span] - part * part_rows
            target[:, span] += jnp.sum(jnp.where(hit, scores, 0.0), 0, keepdims=True)

    row = pl.BlockSpec((1, count), lambda p: (0, 0))
    return pl.pallas_call(
        body,
        grid=(parts,),
        in_specs=[
            pl.BlockSpec((count, width), lambda p: (0, 0)),
            pl.BlockSpec((1, part_rows, width), lambda p: (p, 0, 0)),
            row,
        ],
        out_specs=[pl.BlockSpec((1, part_rows, count), lambda p: (p, 0, 0)), row, row, row],
        out_shape=[jax.ShapeDtypeStruct((parts, part_rows, count), F32)]
        + [jax.ShapeDtypeStruct((1, count), F32)] * 3,
        compiler_params=pltpu.CompilerParams(vmem_limit_bytes=56 << 20),
        cost_estimate=pl.CostEstimate(
            flops=2 * parts * part_rows * count * width,
            bytes_accessed=4 * parts * part_rows * (count + width // 2),
            transcendentals=parts * part_rows * count,
        ),
        name="head_logits",
    )(rows, table, wanted)


def head_grad(logits, log_norm, weight, wanted, first):
    place = lax.broadcasted_iota(jnp.int32, logits.shape, 0)
    probs = jnp.exp(logits - log_norm)
    return (weight * jnp.where(place == wanted - first, probs - 1.0, probs)).astype(BF16)


def head_row_grads(logits, log_norm, weight, wanted, turned):
    parts, part_rows, count = logits.shape
    width, deep = turned.shape[1:]

    def body(logits_ref, log_norm_ref, weight_ref, wanted_ref, turned_ref, out, total):
        part = pl.program_id(0)
        @pl.when(part == 0)
        def _():
            total[...] = jnp.zeros(total.shape, F32)

        for at in range(0, count, CHUNK):
            span = slice(at, at + CHUNK)
            grad = head_grad(
                logits_ref[0, :, span],
                log_norm_ref[:, span],
                weight_ref[:, span],
                wanted_ref[:, span],
                part * part_rows,
            )
            if deep > part_rows:
                grad = jnp.concatenate([grad, jnp.zeros((deep - part_rows, CHUNK), BF16)], 0)
            total[:, span] += matmul(turned_ref[0], grad)

        @pl.when(part == parts - 1)
        def _():
            out[...] = total[...].T.astype(BF16)

    row = pl.BlockSpec((1, count), lambda p: (0, 0))
    return pl.pallas_call(
        body,
        grid=(parts,),
        in_specs=[
            pl.BlockSpec((1, part_rows, count), lambda p: (p, 0, 0)),
            row,
            row,
            row,
            pl.BlockSpec((1, width, deep), lambda p: (p, 0, 0)),
        ],
        out_specs=pl.BlockSpec((count, width), lambda p: (0, 0)),
        out_shape=jax.ShapeDtypeStruct((count, width), BF16),
        scratch_shapes=[pltpu.VMEM((width, count), F32)],
        compiler_params=pltpu.CompilerParams(vmem_limit_bytes=56 << 20),
        cost_estimate=pl.CostEstimate(
            flops=2 * parts * part_rows * count * width,
            bytes_accessed=4 * parts * part_rows * (count + width // 2),
            transcendentals=parts * part_rows * count,
        ),
        name="head_row_grads",
    )(logits, log_norm, weight, wanted, turned)


def head_table_grads(groups):
    parts, part_rows, count = groups[0][0].shape
    width = groups[0][4].shape[1]

    def body(*refs):
        out = refs[-1]
        total = jnp.zeros((part_rows, width), F32)
        for at in range(0, 5 * len(groups), 5):
            logits, log_norm, weight, wanted, rows = refs[at : at + 5]
            for start in range(0, count, CHUNK):
                span = slice(start, start + CHUNK)
                grad = head_grad(
                    logits[0, :, span],
                    log_norm[:, span],
                    weight[:, span],
                    wanted[:, span],
                    pl.program_id(0) * part_rows,
                )
                total += matmul(grad, rows[span])
        out[0] = total

    row = pl.BlockSpec((1, count), lambda p: (0, 0))
    specs = [
        pl.BlockSpec((1, part_rows, count), lambda p: (p, 0, 0)),
        row,
        row,
        row,
        pl.BlockSpec((count, width), lambda p: (0, 0)),
    ]
    return pl.pallas_call(
        body,
        grid=(parts,),
        in_specs=specs * len(groups),
        out_specs=pl.BlockSpec((1, part_rows, width), lambda p: (p, 0, 0)),
        out_shape=jax.ShapeDtypeStruct((parts, part_rows, width), F32),
        compiler_params=pltpu.CompilerParams(vmem_limit_bytes=58 << 20),
        cost_estimate=pl.CostEstimate(
            flops=2 * parts * part_rows * count * width * len(groups),
            bytes_accessed=4 * parts * part_rows * (count * len(groups) + width),
            transcendentals=parts * part_rows * count * len(groups),
        ),
        name="head_table_grads",
    )(*[value for group in groups for value in group])


def spread_piece(token_row, grads, table_grad, side, rows_of, dtype):
    part_rows = table_grad.shape[1]
    tokens = 1024
    first, second = rows_of

    def row_of(task):
        return first + task * (second - first)

    def body(token_ref, grads_ref, table_ref, out, total):
        step = pl.program_id(1)

        @pl.when(step == 0)
        def _():
            total[...] = table_ref[0]

        wanted = token_ref[...] - row_of(pl.program_id(0)) * part_rows
        for at in range(0, part_rows, CHUNK):
            count = min(CHUNK, part_rows - at)
            hit = lax.broadcasted_iota(jnp.int32, (count, tokens), 0) == wanted - at
            total[at : at + count] += matmul(
                jnp.where(hit, 1.0, 0.0).astype(BF16), grads_ref[...]
            )

        @pl.when(step == pl.num_programs(1) - 1)
        def _():
            out[0] = total[...].astype(dtype)

    return pl.pallas_call(
        body,
        grid=(2, grads.shape[0] // tokens),
        in_specs=[
            pl.BlockSpec((1, tokens), lambda task, step: (0, step)),
            pl.BlockSpec((tokens, PIECE), lambda task, step: (step, side)),
            pl.BlockSpec((1, part_rows, PIECE), lambda task, step: (row_of(task), 0, side)),
        ],
        out_specs=pl.BlockSpec((1, part_rows, PIECE), lambda task, step: (task, 0, 0)),
        out_shape=jax.ShapeDtypeStruct((2, part_rows, PIECE), dtype),
        scratch_shapes=[pltpu.VMEM((part_rows, PIECE), F32)],
        compiler_params=pltpu.CompilerParams(vmem_limit_bytes=48 << 20),
        cost_estimate=pl.CostEstimate(
            flops=4 * part_rows * PIECE * grads.shape[0],
            bytes_accessed=12 << 20,
            transcendentals=0,
        ),
        name="spread_piece",
    )(token_row, grads, table_grad)


def column_blocks(rows):
    return jnp.concatenate(jnp.split(rows, rows.shape[1] // MODEL_WIDTH, 1), 0)


def bf16_parts(values):
    high = values.astype(BF16)
    rest = values - high.astype(F32)
    middle = rest.astype(BF16)
    low = (rest - middle.astype(F32)).astype(BF16)
    return high, middle, low


def per_device(token_ids, book_lengths, loss_mask, *state):
    masters, firsts, seconds = state[:7], state[7:14], state[14:]
    table_master, attn_in_m, attn_out_m, compress_m, ffn_in_m, ffn_out_m, gains_m = masters
    vocab_block = table_master.shape[0]
    batch_count = lax.axis_size("batch")
    seq_count = lax.axis_size(SEQ)
    plane_count = seq_count // 2
    share_count = batch_count * 2
    device_count = batch_count * seq_count
    segment = token_ids.shape[1]
    slots = -(-(segment // 3 + 1) // 16) * 16
    keep = segment // 2
    place = lax.axis_index(SEQ)
    offset = place * segment
    share_place = lax.axis_index(SHARE)
    width = MODEL_WIDTH

    own_tokens = token_ids.reshape(segment)
    share_tokens = lax.all_gather(own_tokens, SHARE, axis=0, tiled=True)
    rows_in = attn_in_m.size // width
    rows_out = attn_out_m.size // width
    rows_comp = compress_m.size // width
    rows_ffn = ffn_in_m.size // width
    rows_ffn_out = ffn_out_m.size // width
    gain_count = gains_m.size
    gain_block = jnp.zeros((16, width), BF16).at[0, :gain_count].set(
        gains_m.astype(BF16).reshape(-1)
    )
    mixer_block = jnp.concatenate(
        [
            column_blocks(attn_in_m.astype(BF16)),
            compress_m.astype(BF16),
            attn_out_m.astype(BF16),
            gain_block,
        ],
        0,
    )
    ffn_block = jnp.concatenate(
        [column_blocks(ffn_in_m.astype(BF16)), ffn_out_m.astype(BF16)], 0
    )
    own_table = lax.all_gather(table_master.astype(BF16), "far", axis=0, tiled=True)
    table_x, table_y = plane_swaps(own_table)
    mixer_line_all, ffn_line_all = line_gather(mixer_block), line_gather(ffn_block)
    table_x, table_y, mixer_line_all = lax.optimization_barrier(
        (table_x, table_y, mixer_line_all)
    )
    mixer_swaps = plane_swaps(mixer_line_all)
    part_rows = own_table.shape[0]
    table = jnp.zeros((4 * part_rows, width), BF16)
    for value, row, column in (
        (own_table, 0, 0),
        (table_x, 1, 0),
        (table_y, 2, 0),
        (swapped(table_x[:, :PIECE], "y"), 3, 0),
        (swapped(table_y[:, PIECE:], "x"), 3, PIECE),
    ):
        table = lax.dynamic_update_slice(table, value, (row * part_rows, column))

    def vocab_place(tokens):
        block = tokens // vocab_block
        seq_index = block % seq_count
        owner = block // seq_count * 2 + seq_index % 2
        chip = seq_index // 2 % 4
        part = chip ^ (lax.axis_index("y") * 2 + lax.axis_index("x"))
        inside = seq_index // 8 * vocab_block + tokens % vocab_block
        return owner, part * part_rows + inside

    share_owner, share_local = vocab_place(share_tokens)
    share_row = jnp.where(share_owner == share_place, share_local, -1)
    looked = jnp.where(
        (share_row >= 0)[:, None], table[jnp.maximum(share_row, 0)], jnp.zeros((), BF16)
    )

    looked, mixer_swaps, ffn_line_all = lax.optimization_barrier(
        (looked, mixer_swaps, ffn_line_all)
    )
    mixer_corners = plane_corners(mixer_swaps)
    table_again, mixer_corners, ffn_line_all = lax.optimization_barrier(
        (table, mixer_corners, ffn_line_all)
    )
    ffn_swaps = plane_swaps(ffn_line_all)
    mixer_all = plane_gather(mixer_line_all, mixer_swaps, mixer_corners)
    gains = mixer_all[:, rows_in + rows_comp + rows_out, :gain_count]
    token_rows = lax.psum_scatter(looked, SHARE, scatter_dimension=0, tiled=True)
    gains = gains.reshape(width, 3).astype(F32)
    table = table_again.reshape(4, part_rows, width)
    turned = jnp.pad(table, ((0, 0), (0, -part_rows % 128), (0, 0))).transpose(0, 2, 1)
    token_rows, turned, ffn_swaps = lax.optimization_barrier((token_rows, turned, ffn_swaps))
    part = attn_in_m.shape[0]
    mixer_all = grouped(mixer_all, (part, part, part, rows_comp, rows_out, 16))
    thin = width // GROUPS

    book_ends = jnp.cumsum(book_lengths.reshape(-1))
    own_pos = offset + jnp.arange(segment, dtype=jnp.int32)
    own_book = book_number(own_pos, book_ends)
    next_book = book_number(own_pos + 1, book_ends)
    own_mask = loss_mask.reshape(segment)
    numbers = jnp.arange(NBOOK, dtype=jnp.int32)
    live = own_mask.astype(F32) * (next_book == own_book).astype(F32)
    member = (own_book[:, None] == numbers[None, :]).astype(F32)
    book_counts = jnp.sum(member * live[:, None], 0)
    for axis in ("core", "x", "y"):
        book_counts = book_counts + swapped(book_counts, axis)
    book_counts = lax.psum(book_counts, "far")
    weight = live * jnp.sum(member / jnp.maximum(book_counts, 1.0)[None, :], -1)
    following = passed_along(own_tokens[:1], -1)
    targets = jnp.concatenate([own_tokens[1:], following])
    rank = jnp.cumsum(own_mask) - 1
    chosen = (rank[None, :] == jnp.arange(keep, dtype=jnp.int32)[:, None]) & (
        own_mask[None, :] > 0
    )
    picked_targets = jnp.sum(jnp.where(chosen, targets[None, :], 0), 1)
    picked_weight = jnp.sum(jnp.where(chosen, weight[None, :], 0.0), 1)

    embedded = token_rows.astype(F32) * width**0.5
    normed_one, unit_one, scale_one = norm_forward(embedded, gains[:, 0])
    attention_input = normed_one.astype(BF16)
    attention_input, ffn_swaps = lax.optimization_barrier((attention_input, ffn_swaps))
    ffn_all = plane_gather(ffn_line_all, ffn_swaps, plane_corners(ffn_swaps))
    ffn_all = grouped(ffn_all, (part,) * (rows_ffn // part) + (rows_ffn_out,))
    projected = matmul_packed(attention_input, mixer_all, thin, 0, 3)
    memory_rows = passed_along(attention_input, 1)
    tail_rows = passed_along(attention_input[segment - 2 :], 1)
    first_cell = jnp.mod(2 - offset, 3)
    padding = 3 * slots - segment + 2
    extended = jnp.concatenate([tail_rows, attention_input, jnp.zeros((padding, width), BF16)], 0)
    slot_rows = lax.dynamic_slice_in_dim(extended, first_cell, 3 * slots, 0).reshape(
        slots, 3 * width
    )
    compressed = matmul_packed(slot_rows, mixer_all, 3 * thin, 1, 1)
    other_rows = [memory_rows]
    spare = -(segment + 3 * slots) % BLOCK
    book_parts = [own_book, book_number(own_pos - segment, book_ends)]
    pos_parts = [own_pos, own_pos - segment]
    for hop in (2, 3, 4):
        other_rows.append(passed_along(compressed, hop))
        owner = place - hop
        last_pos = (
            owner * segment
            + jnp.mod(2 - owner * segment, 3)
            + 3 * jnp.arange(slots, dtype=jnp.int32)
        )
        last_book = book_number(last_pos, book_ends)
        usable = (owner >= 0) & (last_pos < owner * segment + segment)
        usable = usable & (book_number(last_pos - 2, book_ends) == last_book)
        book_parts.append(jnp.where(usable, last_book, -2))
        pos_parts.append(jnp.full((slots,), -1, jnp.int32))
    book_parts.append(jnp.full((spare,), -2, jnp.int32))
    pos_parts.append(jnp.full((spare,), -1, jnp.int32))
    other_rows.append(jnp.zeros((spare, width), BF16))
    marks = (
        jnp.concatenate(book_parts)[:, None],
        jnp.concatenate(pos_parts)[:, None],
        own_book[None, :],
        own_pos[None, :],
    )
    other_rows = jnp.concatenate(other_rows, 0)
    memory_pairs = matmul_packed(other_rows, mixer_all, thin, 1, 2)
    attended, log_total = attention_forward(projected, memory_pairs, marks)
    w_out = mixer_all[:, 6 * thin : 7 * thin].reshape(width, width)
    residual = embedded + matmul(attended, w_out)

    normed_two, unit_two, scale_two = norm_forward(residual, gains[:, 1])
    ffn_input = normed_two.astype(BF16)
    output_rows, pre_act, activated_turned = feed_forward(
        ffn_input, ffn_all, residual, rows_ffn_out
    )
    normed_three, unit_three, scale_three = norm_forward(output_rows, gains[:, 2])
    final_rows = normed_three.astype(BF16)

    chosen_bf16 = chosen.astype(BF16)
    picked_rows = matmul(chosen_bf16, final_rows).astype(BF16)
    high, middle, low = bf16_parts(picked_weight)
    side = jnp.concatenate(
        [
            (picked_targets // 256).astype(BF16),
            (picked_targets % 256).astype(BF16),
            high,
            middle,
            low,
        ]
    )
    side_rows = jnp.zeros((16 * width,), BF16).at[: 5 * keep].set(side).reshape(16, width)
    half = keep // 2
    head_one = lax.all_gather(
        jnp.concatenate([picked_rows[:half], side_rows], 0), SHARE, axis=0, tiled=False
    )
    slot_spare = -slots % BLOCK
    slot_tall = jnp.concatenate([slot_rows, jnp.zeros((slot_spare, 3 * width), BF16)], 0)
    halves = [
        core_halves(value)
        for value in (
            grouped_transpose(ffn_input),
            activated_turned,
            grouped_transpose(attention_input),
            grouped_transpose(other_rows),
            grouped_transpose(slot_tall),
            grouped_transpose(attended),
        )
    ]
    rows_one = head_one[:, :half].reshape(share_count * half, width)
    side_all = head_one[:, half:].reshape(share_count, 16 * width)[:, : 5 * keep]
    rows_one, next_rows, halves = lax.optimization_barrier((rows_one, picked_rows[half:], halves))
    rows_two = lax.all_gather(next_rows, SHARE, axis=0, tiled=True)
    side_all = side_all.reshape(share_count, 5, 2, half).astype(F32)
    side_all = side_all.transpose(1, 2, 0, 3).reshape(5, 2, share_count * half)
    wanted_all = (side_all[0] * 256.0 + side_all[1]).astype(jnp.int32)
    weight_all = side_all[2] + side_all[3] + side_all[4]
    wanted_owner, wanted_local = vocab_place(wanted_all)
    wanted_all = jnp.where(wanted_owner == share_place, wanted_local, -1)
    mine = (jnp.arange(share_count * half) // half == share_place).astype(F32)
    loss_local = jnp.zeros((), F32)
    groups, stats = [], []
    for index, rows in enumerate((rows_one, rows_two)):
        wanted, row_weight = wanted_all[index][None], weight_all[index][None]
        logits, top, total, target_logit = head_logits(rows, table, wanted)
        loss_local -= jnp.sum(row_weight * target_logit)
        stats.append((top, total))
        groups.append([logits, row_weight, wanted, rows])
    log_norms = [share_combine(*stats[0]), None]
    stats[1], log_norms[0] = lax.optimization_barrier((stats[1], log_norms[0]))
    log_norms[1] = share_combine(*stats[1])
    for index, (logits, row_weight, wanted, rows) in enumerate(groups):
        loss_local += jnp.sum(row_weight * mine[None] * log_norms[index])
        groups[index] = (logits, log_norms[index], row_weight, wanted, rows)
    grad_picked = []
    for group in groups:
        grad_rows = head_row_grads(*group[:4], turned)
        grad_picked.append(lax.psum_scatter(grad_rows, SHARE, scatter_dimension=0, tiled=True))
    grad_picked = jnp.concatenate(grad_picked, 0)
    grad_table = head_table_grads(groups)
    grad_picked, grad_table = lax.optimization_barrier((grad_picked, grad_table))
    grad_final = matmul_tn(chosen_bf16, grad_picked)

    grad_output_rows, grad_gain_three = norm_backward(
        grad_final, unit_three, scale_three, gains[:, 2]
    )
    grad_branch = grad_output_rows.astype(BF16)
    grad_pre, grad_norm_two = feed_forward_back(grad_branch, pre_act, ffn_all)

    def product(pair, grad, lead=0):
        return pair + (grad[0], grad[1], lead)

    def with_other(grad):
        grad = grad if grad.ndim == 3 else grad[None]
        return grad, swapped(grad, "core")

    out_weights = [
        (
            [product(halves[1], with_other(grad_branch))],
            rows_ffn_out * device_count // width,
            False,
        ),
    ]
    ffn_weights = [
        ([product(halves[0], with_other(grad_pre))], ffn_in_m.shape[1] // width, True),
    ]
    out_sends = gradient_sends(out_weights, chip_place())
    out_sends, grad_norm_two = lax.optimization_barrier((out_sends, grad_norm_two))
    out_arrived = [swapped(send, axis) for send, axis in zip(out_sends, ("x", "y"))]
    grad_res_two, grad_gain_two = norm_backward(grad_norm_two, unit_two, scale_two, gains[:, 1])
    grad_residual = grad_output_rows + grad_res_two

    grad_attn_branch = grad_residual.astype(BF16)
    grad_attended = matmul_nt(grad_attn_branch, w_out).astype(BF16)
    ffn_weights.append(([product(halves[5], with_other(grad_attn_branch))], 1, True))
    grad_query, grad_own, grad_other = attention_backward(
        projected, memory_pairs, marks, log_total, grad_attended
    )
    grad_other, out_arrived = lax.optimization_barrier((grad_other, out_arrived))
    grad_other_rows = matmul_packed_back(grad_other, mixer_all, thin, 1).astype(BF16)
    back_memory = passed_along(grad_other_rows[:segment], -1)
    returned = []
    for hop in (2, 3, 4):
        first_row = segment + (hop - 2) * slots
        returned.append(passed_along(grad_other_rows[first_row : first_row + slots], -hop))
    place, grad_query = lax.optimization_barrier((chip_place(), grad_query))
    ffn_sends = gradient_sends(ffn_weights, place)
    grad_input = matmul_packed_back(grad_query[None], mixer_all, thin, 0)
    grad_input = matmul_packed_back(grad_own, mixer_all, thin, 1, grad_input)
    returned, ffn_sends, grad_input = lax.optimization_barrier(
        (returned, ffn_sends, grad_input)
    )
    ffn_arrived = [swapped(send, axis) for send, axis in zip(ffn_sends, ("x", "y"))]
    grad_compressed = sum(part.astype(F32) for part in returned).astype(BF16)
    grad_slots = matmul_packed_back(grad_compressed[None], mixer_all, 3 * thin, 1)
    grad_slots = grad_slots.reshape(3 * slots, width)
    grad_first = jnp.concatenate([jnp.zeros((2, width), F32), grad_slots[:2]], 0)
    grad_first = lax.dynamic_slice_in_dim(grad_first, 2 - first_cell, 2, 0)
    back_tail = passed_along(grad_first.astype(BF16), -1).astype(F32)
    grad_input = grad_input + lax.dynamic_slice_in_dim(grad_slots, 2 - first_cell, segment, 0)
    grad_input = grad_input + back_memory.astype(F32)
    grad_input = grad_input.at[segment - 2 :].add(back_tail)
    grad_embed, grad_gain_one = norm_backward(grad_input, unit_one, scale_one, gains[:, 0])
    grad_scaled = ((grad_embed + grad_residual) * width**0.5).astype(BF16)

    query_pair, own_pair = with_other(grad_query), with_other(grad_own)
    other_pair = with_other(grad_other)
    slot_pair = with_other(jnp.pad(grad_compressed, ((0, slot_spare), (0, 0))))
    small = jnp.concatenate(
        [
            jnp.stack([grad_gain_one, grad_gain_two, grad_gain_three], 1).reshape(-1),
            jnp.full((128,), loss_local, F32),
        ]
    )
    grad_scaled, place, query_pair, own_pair, other_pair = lax.optimization_barrier(
        (grad_scaled, place, query_pair, own_pair, other_pair)
    )
    small = SmallSum(small)
    share_grads = lax.all_gather(grad_scaled, SHARE, axis=0, tiled=True)
    mixer_weights = [
        ([product(halves[2], query_pair)], 1, True),
        ([product(halves[2], own_pair, 0), product(halves[3], other_pair, 0)], 1, True),
        ([product(halves[2], own_pair, 1), product(halves[3], other_pair, 1)], 1, True),
        ([product(halves[4], slot_pair)], 3, False),
    ]
    mixer_sends = gradient_sends(mixer_weights, place)
    mixer_sends, place, arrived = lax.optimization_barrier(
        (mixer_sends, place, small.exchange())
    )
    small.value += arrived
    mixer_arrived = [swapped(send, axis) for send, axis in zip(mixer_sends, ("x", "y"))]
    out_sums = plane_sums(out_arrived, gradient_keeps(out_weights, place))
    out_sums, place, arrived = lax.optimization_barrier((out_sums, place, small.exchange()))
    small.value += arrived
    ffn_keeps = gradient_keeps(ffn_weights, place)
    ffn_keeps, place = lax.optimization_barrier((ffn_keeps, place))
    mixer_keeps = gradient_keeps(mixer_weights, place)
    ffn_arrived, mixer_keeps = lax.optimization_barrier((ffn_arrived, mixer_keeps))
    ffn_sums = plane_sums(ffn_arrived, ffn_keeps)
    mixer_sums = plane_sums(mixer_arrived, mixer_keeps)
    token_row, ffn_sums, mixer_sums, arrived = lax.optimization_barrier(
        (share_row[None, :], ffn_sums, mixer_sums, small.exchange())
    )
    small.value += arrived
    def spread(token_row, side, rows_of, dtype):
        piece = spread_piece(token_row, share_grads, grad_table, side, rows_of, dtype)
        return lax.optimization_barrier((piece, token_row))

    send_one, token_row = spread(token_row, 0, (1, 3), BF16)
    send_two, token_row = spread(token_row, 1, (2, 3), BF16)
    table_arrived = [swapped(send_one, "x"), swapped(send_two, "y")]
    others = [plane_others(sums) for sums in (out_sums, ffn_sums, mixer_sums)]
    others, token_row = lax.optimization_barrier((others, token_row))
    line = line_open(
        jnp.concatenate(
            [
                line_parts(out_weights, out_sums, others[0]),
                line_parts(ffn_weights, ffn_sums, others[1]),
                line_parts(mixer_weights, mixer_sums, others[2]),
            ],
            1,
        )
    )
    moves, token_row = lax.optimization_barrier((line_sends(line), token_row))
    line = line_move(line, moves)
    keep_one, token_row = spread(token_row, 0, (0, 2), F32)
    keep_two, token_row = spread(token_row, 1, (0, 1), F32)
    table_keeps = [keep_one, keep_two]
    table_keeps, table_arrived, moved = lax.optimization_barrier(
        (table_keeps, table_arrived, line[1:3])
    )
    summed = line_close((line[0], *moved, line[3]))
    ends = (rows_ffn_out, rows_ffn_out + rows_ffn, rows_ffn_out + rows_ffn + rows_out)
    ffn_out_grad, ffn_in_grad, attn_out_grad, mixer_grads = jnp.split(summed, ends)
    halves_new = []
    for arrived, keep_part, axis in zip(table_arrived, table_keeps, ("y", "x")):
        other = (keep_part[1] + arrived[1].astype(F32)).astype(BF16)
        mine = keep_part[0] + arrived[0].astype(F32)
        halves_new.append(mine + swapped(other, axis).astype(F32))
    halves_new, small.value = lax.optimization_barrier((halves_new, small.value))
    grad_table = jnp.concatenate(halves_new, 1)
    if lax.axis_size("far") > 1:
        grad_table = lax.psum_scatter(
            grad_table.astype(BF16), "far", scatter_dimension=0, tiled=True
        )

    small = small.total()
    loss_total = small[3 * width]
    device = lax.axis_index(ALL)
    gain_grads = lax.dynamic_slice_in_dim(small, device * gain_count, gain_count, 0)

    def side_by_side(rows, count):
        return jnp.concatenate(jnp.split(rows, count, 0), 1)

    low, high = rows_in, rows_in + rows_comp
    grads = (
        grad_table,
        side_by_side(mixer_grads[:low], 3),
        attn_out_grad,
        mixer_grads[low:high],
        side_by_side(ffn_in_grad, rows_ffn // attn_in_m.shape[0]),
        ffn_out_grad,
        gain_grads.reshape(gains_m.shape),
    )
    results = []
    for master, first, second, grad, rate in zip(masters, firsts, seconds, grads, STEP_RATES):
        results.extend(adam_update(master, first, second, grad.astype(F32), rate))
    return (loss_total,) + tuple(results)


def solution(mesh):
    batch_count, seq_count = mesh.shape["batch"], mesh.shape["seq"]
    devices = mesh.devices.reshape(batch_count, seq_count // 8, 2, 2, 2)
    grid = Mesh(devices, ALL)
    rows = P(ALL, None)
    return jax.shard_map(
        per_device,
        mesh=grid,
        in_specs=(P("batch", SEQ), P("batch", None), P("batch", SEQ)) + (rows,) * 21,
        out_specs=(P(),) + (rows,) * 21,
        check_vma=False,
    )
```

```python
import jax
import jax.numpy as jnp
from jax import lax
from jax.experimental import pallas as pl
from jax.experimental.pallas import tpu as pltpu
from jax.sharding import Mesh
from jax.sharding import PartitionSpec as P

MODEL_WIDTH = 1024
HEADS = 8
HEAD = 128
NBOOK = 8
STEP = 5

EPSILON = 1e-05
NEGATIVE = -1e30
BETA_ONE = 0.9
BETA_TWO = 0.95
ADAM_EPSILON = 1e-08
WEIGHT_DECAY = 0.1
STEP_RATES = (0.06, 0.03, 0.4, 0.02, 0.03, 0.04, 0.5)

SEQ = ("far", "y", "x", "core")
PLANE = ("far", "y", "x")
SHARE = ("batch", "core")
LINE = ("batch", "far")
ALL = ("batch", "far", "y", "x", "core")
PIECE = 512
BLOCK = 128
GROUPS = 32
CHUNK = 256
TOGETHER = 2
STRIP = TOGETHER * HEAD
BF16 = jnp.bfloat16
F32 = jnp.float32


def passed_along(value, steps):
    count = lax.axis_size(SEQ)
    initial, last = (max(0, -steps), min(count, count - steps))
    return lax.ppermute(value, SEQ, [(source, source + steps) for source in range(initial, last)])


def norm_forward(values, gain):
    center = values - jnp.mean(values, -1, keepdims=True)
    scaler = lax.rsqrt(jnp.mean(center * center, -1, keepdims=True) + EPSILON)
    unit_rows = center * scaler
    return (unit_rows * gain, unit_rows, scaler)


def norm_backward(grad_out, unit_rows, scaler, gain):
    scaled = grad_out * gain
    grad_gain = jnp.sum(grad_out * unit_rows, axis=0)
    grad_in = scaler * (
        scaled
        - jnp.mean(scaled, -1, keepdims=True)
        - unit_rows * jnp.mean(scaled * unit_rows, -1, keepdims=True)
    )
    return (grad_in, grad_gain)


def book_number(positions, book_ends):
    inside = jnp.sum((positions[:, None] >= book_ends[None, :]).astype(jnp.int32), -1)
    return jnp.where(positions < 0, -1, inside)


def matmul(left, right):
    return jnp.dot(left, right, preferred_element_type=F32)


def matmul_nt(left, right):
    return lax.dot_general(left, right, (((1,), (1,)), ((), ())), preferred_element_type=F32)


def matmul_tn(left, right):
    return lax.dot_general(left, right, (((0,), (0,)), ((), ())), preferred_element_type=F32)


def fill_bias(bias, key_book, key_pos, query_book, query_pos):
    allowed = (key_book[...] == query_book[...]) & (key_pos[...] <= query_pos[...])
    bias[...] = jnp.where(allowed, 0.0, NEGATIVE)


def attention_forward_body(*refs):
    query, own_k, own_v, mem_k, mem_v = refs[:5]
    marks, (out, log_total, bias) = refs[5:9], refs[9:]

    @pl.when(pl.program_id(0) == 0)
    def _():
        fill_bias(bias, *marks)

    for index in range(TOGETHER):
        head = slice(index * HEAD, (index + 1) * HEAD)
        keys = jnp.concatenate([own_k[:, head], mem_k[:, head]], 0)
        values = jnp.concatenate([own_v[:, head], mem_v[:, head]], 0)
        scores = matmul_nt(keys, query[:, head]) * HEAD ** (-0.5) + bias[...]
        top = jnp.max(scores, 0, keepdims=True)
        probs = jnp.exp(scores - top)
        total = jnp.sum(probs, 0, keepdims=True)
        log_total[index] = top + jnp.log(total)
        probs = (probs * (1.0 / total)).astype(BF16)
        out[:, head] = matmul_tn(values, probs).T.astype(BF16)


def attention_backward_body(*refs):
    query, own_k, own_v, mem_k, mem_v = refs[:5]
    marks = refs[5:9]
    log_total, grad_out, grad_query, grad_own, grad_mem, bias = refs[9:]

    @pl.when(pl.program_id(0) == 0)
    def _():
        fill_bias(bias, *marks)

    for index in range(TOGETHER):
        head = slice(index * HEAD, (index + 1) * HEAD)
        keys = jnp.concatenate([own_k[:, head], mem_k[:, head]], 0)
        values = jnp.concatenate([own_v[:, head], mem_v[:, head]], 0)
        scores = matmul_nt(keys, query[:, head]) * HEAD ** (-0.5) + bias[...]
        probs = jnp.exp(scores - log_total[index])
        grad_probs = matmul_nt(values, grad_out[:, head])
        inner = jnp.sum(probs * grad_probs, 0, keepdims=True)
        grad_scores = (probs * (grad_probs - inner) * HEAD ** (-0.5)).astype(BF16)
        grad_query[:, head] = matmul_tn(keys, grad_scores).T.astype(BF16)
        pair = (
            matmul(grad_scores, query[:, head]),
            matmul(probs.astype(BF16), grad_out[:, head]),
        )
        at = 0
        for part in (grad_own, grad_mem):
            count = part.shape[1]
            for side in (0, 1):
                part[side, :, head] = pair[side][at : at + count].astype(part.dtype)
            at += count


def attention_specs(segment, others):
    def column(rows, shift):
        return pl.BlockSpec((rows, STRIP), lambda h: (0, h + shift * HEADS // TOGETHER))

    mark_k = pl.BlockSpec((segment + others, 1), lambda h: (0, 0))
    mark_q = pl.BlockSpec((1, segment), lambda h: (0, 0))
    specs = [column(segment, 0), column(segment, 1), column(segment, 2)]
    specs += [column(others, 0), column(others, 1)]
    return specs + [mark_k, mark_k, mark_q, mark_q]


def attention_forward(projected, memory, marks):
    segment, others = projected.shape[0], memory.shape[0]
    keys = segment + others
    return pl.pallas_call(
        attention_forward_body,
        grid=(HEADS // TOGETHER,),
        in_specs=attention_specs(segment, others),
        out_specs=[
            pl.BlockSpec((segment, STRIP), lambda h: (0, h)),
            pl.BlockSpec((TOGETHER, 1, segment), lambda h: (h, 0, 0)),
        ],
        out_shape=[
            jax.ShapeDtypeStruct((segment, HEADS * HEAD), BF16),
            jax.ShapeDtypeStruct((HEADS, 1, segment), F32),
        ],
        scratch_shapes=[pltpu.VMEM((keys, segment), F32)],
        compiler_params=pltpu.CompilerParams(vmem_limit_bytes=56 << 20),
        cost_estimate=pl.CostEstimate(
            flops=4 * HEADS * keys * segment * HEAD,
            bytes_accessed=12 << 20,
            transcendentals=HEADS * keys * segment,
        ),
        name="attention_forward",
    )(projected, projected, projected, memory, memory, *marks)


def attention_backward(projected, memory, marks, log_total, grad_out):
    segment, others = projected.shape[0], memory.shape[0]
    keys = segment + others
    width = HEADS * HEAD

    def pair_spec(rows):
        return pl.BlockSpec((2, rows, STRIP), lambda h: (0, 0, h))

    return pl.pallas_call(
        attention_backward_body,
        grid=(HEADS // TOGETHER,),
        in_specs=attention_specs(segment, others)
        + [
            pl.BlockSpec((TOGETHER, 1, segment), lambda h: (h, 0, 0)),
            pl.BlockSpec((segment, STRIP), lambda h: (0, h)),
        ],
        out_specs=[pl.BlockSpec((segment, STRIP), lambda h: (0, h))]
        + [pair_spec(segment), pair_spec(others)],
        out_shape=[
            jax.ShapeDtypeStruct((segment, width), BF16),
            jax.ShapeDtypeStruct((2, segment, width), BF16),
            jax.ShapeDtypeStruct((2, others, width), BF16),
        ],
        scratch_shapes=[pltpu.VMEM((keys, segment), F32)],
        compiler_params=pltpu.CompilerParams(vmem_limit_bytes=56 << 20),
        cost_estimate=pl.CostEstimate(
            flops=10 * HEADS * keys * segment * HEAD,
            bytes_accessed=24 << 20,
            transcendentals=HEADS * keys * segment,
        ),
        name="attention_backward",
    )(projected, projected, projected, memory, memory, *marks, log_total, grad_out)


def adam_update(master, first, second, grad, rate):
    new_first = BETA_ONE * first + (1.0 - BETA_ONE) * grad
    new_second = BETA_TWO * second + (1.0 - BETA_TWO) * grad * grad
    first_hat = new_first / (1.0 - BETA_ONE**STEP)
    second_hat = new_second / (1.0 - BETA_TWO**STEP)
    new_master = master - rate * (
        first_hat / (jnp.sqrt(second_hat) + ADAM_EPSILON) + WEIGHT_DECAY * master
    )
    return [new_first, new_second, new_master]


def swapped(value, axis):
    return lax.ppermute(value, axis, [(0, 1), (1, 0)])


def grouped(buffer, sections):
    if buffer.shape[0] == GROUPS:
        return buffer
    parts, at = [], 0
    for count in sections:
        parts.append(buffer[:, at : at + count].reshape(GROUPS, -1, buffer.shape[2]))
        at += count
    return jnp.concatenate(parts, 1)


def matmul_packed(value, buffer, rows, first, count):
    size, depth = value.shape

    def body(value_ref, weight_ref, out):
        weight = weight_ref[...].reshape(depth, PIECE)
        out[...] = matmul(value_ref[...], weight).astype(BF16)

    return pl.pallas_call(
        body,
        grid=(count, 2),
        in_specs=[
            pl.BlockSpec((size, depth), lambda j, h: (0, 0)),
            pl.BlockSpec((GROUPS, rows, PIECE), lambda j, h: (0, first + j, h)),
        ],
        out_specs=pl.BlockSpec((size, PIECE), lambda j, h: (0, 2 * j + h)),
        out_shape=jax.ShapeDtypeStruct((size, count * 2 * PIECE), BF16),
        compiler_params=pltpu.CompilerParams(vmem_limit_bytes=48 << 20),
        cost_estimate=pl.CostEstimate(
            flops=4 * size * depth * count * PIECE,
            bytes_accessed=2 * depth * count * 1024,
            transcendentals=0,
        ),
        name="matmul_packed",
    )(value, buffer)


def matmul_packed_back(grads, buffer, rows, first, start=None):
    count, size, width = grads.shape
    depth = GROUPS * rows
    extra = [] if start is None else [start]

    def body(grad_ref, weight_ref, *rest):
        out = rest[-1]

        @pl.when(pl.program_id(0) == 0)
        def _():
            out[...] = jnp.zeros(out.shape, F32) if start is None else rest[0][...]

        out[...] += matmul_nt(grad_ref[0], weight_ref[...].reshape(depth, width))

    return pl.pallas_call(
        body,
        grid=(count,),
        in_specs=[
            pl.BlockSpec((1, size, width), lambda j: (j, 0, 0)),
            pl.BlockSpec((GROUPS, rows, width), lambda j: (0, first + j, 0)),
        ]
        + [pl.BlockSpec((size, depth), lambda j: (0, 0)) for _ in extra],
        out_specs=pl.BlockSpec((size, depth), lambda j: (0, 0)),
        out_shape=jax.ShapeDtypeStruct((size, depth), F32),
        compiler_params=pltpu.CompilerParams(vmem_limit_bytes=48 << 20),
        cost_estimate=pl.CostEstimate(
            flops=2 * size * depth * count * width,
            bytes_accessed=2 * depth * count * width,
            transcendentals=0,
        ),
        name="matmul_packed_back",
    )(grads, buffer, *extra)


GELU_SCALE = 0.7978845608028654
GELU_CUBE = 0.044715


def feed_forward(value, buffer, residual, chunk):
    size, width = value.shape
    blocks = (buffer.shape[1] - BLOCK) * GROUPS // width
    lines = width // (8 * chunk)

    def body(value_ref, first_ref, second_ref, residual_ref, out, pre, turned):
        @pl.when(pl.program_id(0) == 0)
        def _():
            out[...] = residual_ref[...]

        parts = []
        for at in range(0, size, CHUNK):
            span = slice(at, at + CHUNK)
            hidden = matmul(value_ref[span], first_ref[...].reshape(width, width))
            pre[span] = hidden
            inner = jnp.tanh(GELU_SCALE * (hidden + GELU_CUBE * hidden * hidden * hidden))
            active = (0.5 * hidden * (1.0 + inner)).astype(BF16)
            out[span] += matmul(active, second_ref[...].reshape(width, width))
            parts.append(active)
        active = jnp.concatenate(parts, 0)
        columns = active.T
        for line in range(lines):
            for place in range(8):
                target = place % 2 * 4 + place // 2
                at = (line * 8 + place) * chunk
                turned[target, line * chunk : (line + 1) * chunk] = columns[at : at + chunk]

    return pl.pallas_call(
        body,
        grid=(blocks,),
        in_specs=[
            pl.BlockSpec((size, width), lambda j: (0, 0)),
            pl.BlockSpec((GROUPS, width // GROUPS, width), lambda j: (0, j, 0)),
            pl.BlockSpec((width // BLOCK, BLOCK, width), lambda j: (j, 1, 0)),
            pl.BlockSpec((size, width), lambda j: (0, 0)),
        ],
        out_specs=[
            pl.BlockSpec((size, width), lambda j: (0, 0)),
            pl.BlockSpec((size, width), lambda j: (0, j)),
            pl.BlockSpec((8, width // 8, size), lambda j: (0, j, 0)),
        ],
        out_shape=[
            jax.ShapeDtypeStruct((size, width), F32),
            jax.ShapeDtypeStruct((size, blocks * width), F32),
            jax.ShapeDtypeStruct((8, blocks * width // 8, size), BF16),
        ],
        compiler_params=pltpu.CompilerParams(vmem_limit_bytes=56 << 20),
        cost_estimate=pl.CostEstimate(
            flops=4 * size * width * width * blocks,
            bytes_accessed=32 << 20,
            transcendentals=size * width * blocks,
        ),
        name="feed_forward",
    )(value, buffer, buffer, residual)


def feed_forward_back(grad, pre, buffer):
    size, width = grad.shape
    blocks = pre.shape[1] // width

    def body(grad_ref, pre_ref, first_ref, second_ref, grad_pre, out):
        @pl.when(pl.program_id(0) == 0)
        def _():
            out[...] = jnp.zeros(out.shape, F32)

        for at in range(0, size, CHUNK):
            span = slice(at, at + CHUNK)
            grad_active = matmul_nt(grad_ref[span], second_ref[...].reshape(width, width))
            hidden = pre_ref[span]
            square = hidden * hidden
            inner = jnp.tanh(GELU_SCALE * hidden * (1.0 + GELU_CUBE * square))
            slope = 0.5 * (1.0 + inner) + 0.5 * hidden * (1.0 - inner * inner) * GELU_SCALE * (
                1.0 + 3.0 * GELU_CUBE * square
            )
            back = (grad_active * slope).astype(BF16)
            grad_pre[span] = back
            out[span] += matmul_nt(back, first_ref[...].reshape(width, width))

    return pl.pallas_call(
        body,
        grid=(blocks,),
        in_specs=[
            pl.BlockSpec((size, width), lambda j: (0, 0)),
            pl.BlockSpec((size, width), lambda j: (0, j)),
            pl.BlockSpec((GROUPS, width // GROUPS, width), lambda j: (0, j, 0)),
            pl.BlockSpec((width // BLOCK, BLOCK, width), lambda j: (j, 1, 0)),
        ],
        out_specs=[
            pl.BlockSpec((size, width), lambda j: (0, j)),
            pl.BlockSpec((size, width), lambda j: (0, 0)),
        ],
        out_shape=[
            jax.ShapeDtypeStruct((size, blocks * width), BF16),
            jax.ShapeDtypeStruct((size, width), F32),
        ],
        compiler_params=pltpu.CompilerParams(vmem_limit_bytes=56 << 20),
        cost_estimate=pl.CostEstimate(
            flops=4 * size * width * width * blocks,
            bytes_accessed=32 << 20,
            transcendentals=size * width * blocks,
        ),
        name="feed_forward_back",
    )(grad, pre, buffer, buffer)


def grouped_transpose(rows):
    tokens, columns = rows.shape
    line = lax.axis_size(LINE)
    split = rows.reshape(tokens, line, 2, 2, 2, columns // (line * 8))
    return split.transpose(4, 2, 3, 1, 5, 0).reshape(8, columns // 8, tokens)


def core_halves(grouped):
    core = lax.axis_index("core")
    mine = lax.dynamic_slice_in_dim(grouped, 4 * core, 4, 0)
    other = lax.dynamic_slice_in_dim(grouped, 4 * (1 - core), 4, 0)
    return mine, swapped(other, "core")


def gradient_piece(weights, place, half, axis, moved, dtype):
    operands, specs, plan = [], [], []
    first = 0
    for products, blocks, wide in weights:
        for own, other, rhs_own, rhs_other, lead in products:
            tokens = own.shape[2]

            def inner(step, first=first, blocks=blocks):
                return jnp.clip(step - first, 0, blocks - 1)

            for side in (own, other):
                for free in (0, 1):
                    flip = 2 * free + moved if axis == "x" else 2 * moved + free

                    def lhs_map(step, me, flip=flip, inner=inner, wide=wide):
                        return (me[0] ^ flip, 0 if wide else inner(step), 0)

                    operands.append(side)
                    specs.append(pl.BlockSpec((1, BLOCK, tokens), lhs_map))
            for side in (rhs_own, rhs_other):

                def rhs_map(step, me, inner=inner, wide=wide, lead=lead):
                    return (lead, 0, 2 * inner(step) + half if wide else half)

                operands.append(side)
                specs.append(pl.BlockSpec((1, tokens, PIECE), rhs_map))
        plan.append((first, blocks, len(products)))
        first += blocks

    def body(me, *refs):
        out = refs[-1]
        step = pl.program_id(0)
        at = 0
        for start, blocks, count in plan:
            group = refs[at : at + 6 * count]

            @pl.when((step >= start) & (step < start + blocks))
            def _():
                total = jnp.zeros((2 * BLOCK, PIECE), F32)
                for k in range(0, 6 * count, 6):
                    near = jnp.concatenate([group[k][0], group[k + 1][0]], 0)
                    far = jnp.concatenate([group[k + 2][0], group[k + 3][0]], 0)
                    total += matmul(near, group[k + 4][0]) + matmul(far, group[k + 5][0])
                out[0] = total.astype(out.dtype)

            at += 6 * count

    return pl.pallas_call(
        body,
        grid_spec=pltpu.PrefetchScalarGridSpec(
            num_scalar_prefetch=1,
            grid=(first,),
            in_specs=specs,
            out_specs=pl.BlockSpec((1, 2 * BLOCK, PIECE), lambda step, me: (step, 0, 0)),
        ),
        out_shape=jax.ShapeDtypeStruct((first, 2 * BLOCK, PIECE), dtype),
        compiler_params=pltpu.CompilerParams(vmem_limit_bytes=40 << 20),
        cost_estimate=pl.CostEstimate(
            flops=first * 2 * 2 * BLOCK * PIECE * 1024,
            bytes_accessed=first * (3 << 20),
            transcendentals=0,
        ),
        name="gradient_piece",
    )(place, *operands)


def line_open(value):
    shape = value.shape[1:]
    count = lax.axis_size(LINE)
    return value, jnp.zeros(shape, BF16), jnp.zeros(shape, BF16), count - 1


def line_sends(state):
    value, upward, downward, steps = state
    count, index = lax.axis_size(LINE), lax.axis_index(LINE)
    above = lax.dynamic_index_in_dim(value, jnp.minimum(index + steps, count - 1), 0, False)
    below = lax.dynamic_index_in_dim(value, jnp.maximum(index - steps, 0), 0, False)
    return (above + upward.astype(F32)).astype(BF16), (below + downward.astype(F32)).astype(BF16)


def line_move(state, sends):
    steps = state[3]
    count = lax.axis_size(LINE)
    up = [(i, i + 1) for i in range(count - steps)]
    down = [(i, i - 1) for i in range(steps, count)]
    upward = lax.ppermute(sends[0], LINE, up)
    downward = lax.ppermute(sends[1], LINE, down)
    return state[0], upward, downward, steps - 1


def line_close(state):
    while state[3] > 0:
        state = line_move(state, lax.optimization_barrier(line_sends(state)))
    value, upward, downward, _ = state
    total = lax.dynamic_index_in_dim(value, lax.axis_index(LINE), 0, False)
    return total + upward.astype(F32) + downward.astype(F32)


def chip_place():
    place = lax.axis_index("y") * 2 + lax.axis_index("x")
    return jnp.reshape(place, (1,)).astype(jnp.int32)


def gradient_sends(weights, place):
    return [
        gradient_piece(weights, place, 0, "x", 1, BF16),
        gradient_piece(weights, place, 1, "y", 1, BF16),
    ]


def gradient_keeps(weights, place):
    return [
        gradient_piece(weights, place, 0, "x", 0, F32),
        gradient_piece(weights, place, 1, "y", 0, F32),
    ]


def plane_sums(sends, keeps):
    result = []
    for arrived, keep in zip(sends, keeps):
        count = keep.shape[1] // 2
        other = (keep[:, count:] + arrived[:, count:].astype(F32)).astype(BF16)
        result.append((keep[:, :count] + arrived[:, :count].astype(F32), other))
    return result


def plane_others(sums):
    return [swapped(other, axis) for (_, other), axis in zip(sums, ("y", "x"))]


def line_parts(weights, sums, others):
    line = lax.axis_size(LINE)
    joined = [mine + other.astype(F32) for (mine, _), other in zip(sums, others)]
    first, chunks = 0, []
    for weight in weights:
        blocks, wide = weight[1:]
        for part in range(blocks if wide else 1):
            count = 1 if wide else blocks
            pair = [
                half[first : first + count].reshape(line, count * BLOCK // line, PIECE)
                for half in joined
            ]
            chunks.append(jnp.concatenate(pair, -1))
            first += count
    return jnp.concatenate(chunks, 1)


class SmallSum:
    def __init__(self, value):
        count = lax.axis_size(LINE)
        self.value = value
        self.steps = [("core", 1)]
        step = 1
        while step < count:
            self.steps.append((LINE, step))
            step *= 2
        self.steps += [("x", 1), ("y", 1)]

    def exchange(self):
        axis, step = self.steps.pop(0)
        size = lax.axis_size(axis)
        return lax.ppermute(self.value, axis, [(i, i ^ step) for i in range(size)])

    def total(self):
        while self.steps:
            self.value = self.value + self.exchange()
        return self.value


def line_gather(block):
    return lax.all_gather(block, LINE, axis=0, tiled=False)


def plane_swaps(value):
    return swapped(value, "x"), swapped(value, "y")


def plane_corners(swaps):
    return swapped(swaps[0][..., :PIECE], "y"), swapped(swaps[1][..., PIECE:], "x")


def plane_gather(value, swaps, corners):
    line, rows, width = value.shape
    along_x, along_y = swaps
    pieces = (
        (value, 0, 0, 0),
        (along_x, 0, 1, 0),
        (along_y, 1, 0, 0),
        (corners[0], 1, 1, 0),
        (corners[1], 1, 1, PIECE),
    )
    y, x, core = (lax.axis_index(axis) for axis in ("y", "x", "core"))
    result = jnp.zeros((line, 2, 2, 2, rows, width), BF16)
    for piece, flip_y, flip_x, column in pieces:
        for flip in (0, 1):
            part = swapped(piece, "core") if flip else piece
            start = (0, y ^ flip_y, x ^ flip_x, core ^ flip, 0, column)
            result = lax.dynamic_update_slice(result, part[:, None, None, None], start)
    return result.reshape(8 * line, rows, width)


def share_combine(top, total):
    def merged(top, total, axis, pairs):
        pair = lax.ppermute(jnp.concatenate([top, total], 0), axis, pairs)
        best = jnp.maximum(top, pair[:1])
        return best, total * jnp.exp(top - best) + pair[1:] * jnp.exp(pair[:1] - best)

    top, total = merged(top, total, "core", [(0, 1), (1, 0)])
    count = lax.axis_size("batch")
    step = 1
    while step < count:
        top, total = merged(top, total, "batch", [(i, i ^ step) for i in range(count)])
        step *= 2
    return top + jnp.log(total)


def head_logits(rows, table, wanted):
    parts, part_rows, width = table.shape
    count = rows.shape[0]

    def body(rows_ref, table_ref, wanted_ref, logits, top, total, target):
        part = pl.program_id(0)

        @pl.when(part == 0)
        def _():
            top[...] = jnp.full(top.shape, NEGATIVE, F32)
            total[...] = jnp.zeros(total.shape, F32)
            target[...] = jnp.zeros(target.shape, F32)

        for at in range(0, count, CHUNK):
            span = slice(at, at + CHUNK)
            scores = matmul_nt(table_ref[0], rows_ref[span])
            logits[0, :, span] = scores
            best = jnp.maximum(top[:, span], jnp.max(scores, 0, keepdims=True))
            total[:, span] = total[:, span] * jnp.exp(top[:, span] - best) + jnp.sum(
                jnp.exp(scores - best), 0, keepdims=True
            )
            top[:, span] = best
            place = lax.broadcasted_iota(jnp.int32, scores.shape, 0)
            hit = place == wanted_ref[:, span] - part * part_rows
            target[:, span] += jnp.sum(jnp.where(hit, scores, 0.0), 0, keepdims=True)

    row = pl.BlockSpec((1, count), lambda p: (0, 0))
    return pl.pallas_call(
        body,
        grid=(parts,),
        in_specs=[
            pl.BlockSpec((count, width), lambda p: (0, 0)),
            pl.BlockSpec((1, part_rows, width), lambda p: (p, 0, 0)),
            row,
        ],
        out_specs=[pl.BlockSpec((1, part_rows, count), lambda p: (p, 0, 0)), row, row, row],
        out_shape=[jax.ShapeDtypeStruct((parts, part_rows, count), F32)]
        + [jax.ShapeDtypeStruct((1, count), F32)] * 3,
        compiler_params=pltpu.CompilerParams(vmem_limit_bytes=56 << 20),
        cost_estimate=pl.CostEstimate(
            flops=2 * parts * part_rows * count * width,
            bytes_accessed=4 * parts * part_rows * (count + width // 2),
            transcendentals=parts * part_rows * count,
        ),
        name="head_logits",
    )(rows, table, wanted)


def head_grad(logits, log_norm, weight, wanted, first):
    place = lax.broadcasted_iota(jnp.int32, logits.shape, 0)
    probs = jnp.exp(logits - log_norm)
    return (weight * jnp.where(place == wanted - first, probs - 1.0, probs)).astype(BF16)


def head_row_grads(logits, log_norm, weight, wanted, turned):
    parts, part_rows, count = logits.shape
    width, deep = turned.shape[1:]

    def body(logits_ref, log_norm_ref, weight_ref, wanted_ref, turned_ref, out, total):
        part = pl.program_id(0)
        @pl.when(part == 0)
        def _():
            total[...] = jnp.zeros(total.shape, F32)

        for at in range(0, count, CHUNK):
            span = slice(at, at + CHUNK)
            grad = head_grad(
                logits_ref[0, :, span],
                log_norm_ref[:, span],
                weight_ref[:, span],
                wanted_ref[:, span],
                part * part_rows,
            )
            if deep > part_rows:
                grad = jnp.concatenate([grad, jnp.zeros((deep - part_rows, CHUNK), BF16)], 0)
            total[:, span] += matmul(turned_ref[0], grad)

        @pl.when(part == parts - 1)
        def _():
            out[...] = total[...].T.astype(BF16)

    row = pl.BlockSpec((1, count), lambda p: (0, 0))
    return pl.pallas_call(
        body,
        grid=(parts,),
        in_specs=[
            pl.BlockSpec((1, part_rows, count), lambda p: (p, 0, 0)),
            row,
            row,
            row,
            pl.BlockSpec((1, width, deep), lambda p: (p, 0, 0)),
        ],
        out_specs=pl.BlockSpec((count, width), lambda p: (0, 0)),
        out_shape=jax.ShapeDtypeStruct((count, width), BF16),
        scratch_shapes=[pltpu.VMEM((width, count), F32)],
        compiler_params=pltpu.CompilerParams(vmem_limit_bytes=56 << 20),
        cost_estimate=pl.CostEstimate(
            flops=2 * parts * part_rows * count * width,
            bytes_accessed=4 * parts * part_rows * (count + width // 2),
            transcendentals=parts * part_rows * count,
        ),
        name="head_row_grads",
    )(logits, log_norm, weight, wanted, turned)


def head_table_grads(groups):
    parts, part_rows, count = groups[0][0].shape
    width = groups[0][4].shape[1]

    def body(*refs):
        out = refs[-1]
        total = jnp.zeros((part_rows, width), F32)
        for at in range(0, 5 * len(groups), 5):
            logits, log_norm, weight, wanted, rows = refs[at : at + 5]
            for start in range(0, count, CHUNK):
                span = slice(start, start + CHUNK)
                grad = head_grad(
                    logits[0, :, span],
                    log_norm[:, span],
                    weight[:, span],
                    wanted[:, span],
                    pl.program_id(0) * part_rows,
                )
                total += matmul(grad, rows[span])
        out[0] = total

    row = pl.BlockSpec((1, count), lambda p: (0, 0))
    specs = [
        pl.BlockSpec((1, part_rows, count), lambda p: (p, 0, 0)),
        row,
        row,
        row,
        pl.BlockSpec((count, width), lambda p: (0, 0)),
    ]
    return pl.pallas_call(
        body,
        grid=(parts,),
        in_specs=specs * len(groups),
        out_specs=pl.BlockSpec((1, part_rows, width), lambda p: (p, 0, 0)),
        out_shape=jax.ShapeDtypeStruct((parts, part_rows, width), F32),
        compiler_params=pltpu.CompilerParams(vmem_limit_bytes=58 << 20),
        cost_estimate=pl.CostEstimate(
            flops=2 * parts * part_rows * count * width * len(groups),
            bytes_accessed=4 * parts * part_rows * (count * len(groups) + width),
            transcendentals=parts * part_rows * count * len(groups),
        ),
        name="head_table_grads",
    )(*[value for group in groups for value in group])


def spread_piece(token_row, grads, table_grad, side, rows_of, dtype):
    part_rows = table_grad.shape[1]
    tokens = 1024
    first, second = rows_of

    def row_of(task):
        return first + task * (second - first)

    def body(token_ref, grads_ref, table_ref, out, total):
        step = pl.program_id(1)

        @pl.when(step == 0)
        def _():
            total[...] = table_ref[0]

        wanted = token_ref[...] - row_of(pl.program_id(0)) * part_rows
        for at in range(0, part_rows, CHUNK):
            count = min(CHUNK, part_rows - at)
            hit = lax.broadcasted_iota(jnp.int32, (count, tokens), 0) == wanted - at
            total[at : at + count] += matmul(
                jnp.where(hit, 1.0, 0.0).astype(BF16), grads_ref[...]
            )

        @pl.when(step == pl.num_programs(1) - 1)
        def _():
            out[0] = total[...].astype(dtype)

    return pl.pallas_call(
        body,
        grid=(2, grads.shape[0] // tokens),
        in_specs=[
            pl.BlockSpec((1, tokens), lambda task, step: (0, step)),
            pl.BlockSpec((tokens, PIECE), lambda task, step: (step, side)),
            pl.BlockSpec((1, part_rows, PIECE), lambda task, step: (row_of(task), 0, side)),
        ],
        out_specs=pl.BlockSpec((1, part_rows, PIECE), lambda task, step: (task, 0, 0)),
        out_shape=jax.ShapeDtypeStruct((2, part_rows, PIECE), dtype),
        scratch_shapes=[pltpu.VMEM((part_rows, PIECE), F32)],
        compiler_params=pltpu.CompilerParams(vmem_limit_bytes=48 << 20),
        cost_estimate=pl.CostEstimate(
            flops=4 * part_rows * PIECE * grads.shape[0],
            bytes_accessed=12 << 20,
            transcendentals=0,
        ),
        name="spread_piece",
    )(token_row, grads, table_grad)


def column_blocks(rows):
    return jnp.concatenate(jnp.split(rows, rows.shape[1] // MODEL_WIDTH, 1), 0)


def bf16_parts(values):
    high = values.astype(BF16)
    rest = values - high.astype(F32)
    middle = rest.astype(BF16)
    low = (rest - middle.astype(F32)).astype(BF16)
    return high, middle, low


def per_device(token_ids, book_lengths, loss_mask, *state):
    masters, firsts, seconds = state[:7], state[7:14], state[14:]
    table_master, attn_in_m, attn_out_m, compress_m, ffn_in_m, ffn_out_m, gains_m = masters
    vocab_block = table_master.shape[0]
    batch_count = lax.axis_size("batch")
    seq_count = lax.axis_size(SEQ)
    plane_count = seq_count // 2
    share_count = batch_count * 2
    device_count = batch_count * seq_count
    segment = token_ids.shape[1]
    slots = -(-(segment // 3 + 1) // 16) * 16
    keep = segment // 2
    place = lax.axis_index(SEQ)
    offset = place * segment
    share_place = lax.axis_index(SHARE)
    width = MODEL_WIDTH

    own_tokens = token_ids.reshape(segment)
    share_tokens = lax.all_gather(own_tokens, SHARE, axis=0, tiled=True)
    rows_in = attn_in_m.size // width
    rows_out = attn_out_m.size // width
    rows_comp = compress_m.size // width
    rows_ffn = ffn_in_m.size // width
    rows_ffn_out = ffn_out_m.size // width
    gain_count = gains_m.size
    gain_block = jnp.zeros((16, width), BF16).at[0, :gain_count].set(
        gains_m.astype(BF16).reshape(-1)
    )
    mixer_block = jnp.concatenate(
        [
            column_blocks(attn_in_m.astype(BF16)),
            compress_m.astype(BF16),
            attn_out_m.astype(BF16),
            gain_block,
        ],
        0,
    )
    ffn_block = jnp.concatenate(
        [column_blocks(ffn_in_m.astype(BF16)), ffn_out_m.astype(BF16)], 0
    )
    own_table = lax.all_gather(table_master.astype(BF16), "far", axis=0, tiled=True)
    table_x, table_y = plane_swaps(own_table)
    mixer_line_all, ffn_line_all = line_gather(mixer_block), line_gather(ffn_block)
    table_x, table_y, mixer_line_all = lax.optimization_barrier(
        (table_x, table_y, mixer_line_all)
    )
    mixer_swaps = plane_swaps(mixer_line_all)
    part_rows = own_table.shape[0]
    table = jnp.zeros((4 * part_rows, width), BF16)
    for value, row, column in (
        (own_table, 0, 0),
        (table_x, 1, 0),
        (table_y, 2, 0),
        (swapped(table_x[:, :PIECE], "y"), 3, 0),
        (swapped(table_y[:, PIECE:], "x"), 3, PIECE),
    ):
        table = lax.dynamic_update_slice(table, value, (row * part_rows, column))

    def vocab_place(tokens):
        block = tokens // vocab_block
        seq_index = block % seq_count
        owner = block // seq_count * 2 + seq_index % 2
        chip = seq_index // 2 % 4
        part = chip ^ (lax.axis_index("y") * 2 + lax.axis_index("x"))
        inside = seq_index // 8 * vocab_block + tokens % vocab_block
        return owner, part * part_rows + inside

    share_owner, share_local = vocab_place(share_tokens)
    share_row = jnp.where(share_owner == share_place, share_local, -1)
    looked = jnp.where(
        (share_row >= 0)[:, None], table[jnp.maximum(share_row, 0)], jnp.zeros((), BF16)
    )

    looked, mixer_swaps, ffn_line_all = lax.optimization_barrier(
        (looked, mixer_swaps, ffn_line_all)
    )
    mixer_corners = plane_corners(mixer_swaps)
    table_again, mixer_corners, ffn_line_all = lax.optimization_barrier(
        (table, mixer_corners, ffn_line_all)
    )
    ffn_swaps = plane_swaps(ffn_line_all)
    mixer_all = plane_gather(mixer_line_all, mixer_swaps, mixer_corners)
    gains = mixer_all[:, rows_in + rows_comp + rows_out, :gain_count]
    token_rows = lax.psum_scatter(looked, SHARE, scatter_dimension=0, tiled=True)
    gains = gains.reshape(width, 3).astype(F32)
    table = table_again.reshape(4, part_rows, width)
    turned = jnp.pad(table, ((0, 0), (0, -part_rows % 128), (0, 0))).transpose(0, 2, 1)
    token_rows, turned, ffn_swaps = lax.optimization_barrier((token_rows, turned, ffn_swaps))
    part = attn_in_m.shape[0]
    mixer_all = grouped(mixer_all, (part, part, part, rows_comp, rows_out, 16))
    thin = width // GROUPS

    book_ends = jnp.cumsum(book_lengths.reshape(-1))
    own_pos = offset + jnp.arange(segment, dtype=jnp.int32)
    own_book = book_number(own_pos, book_ends)
    next_book = book_number(own_pos + 1, book_ends)
    own_mask = loss_mask.reshape(segment)
    numbers = jnp.arange(NBOOK, dtype=jnp.int32)
    live = own_mask.astype(F32) * (next_book == own_book).astype(F32)
    member = (own_book[:, None] == numbers[None, :]).astype(F32)
    book_counts = jnp.sum(member * live[:, None], 0)
    for axis in ("core", "x", "y"):
        book_counts = book_counts + swapped(book_counts, axis)
    book_counts = lax.psum(book_counts, "far")
    weight = live * jnp.sum(member / jnp.maximum(book_counts, 1.0)[None, :], -1)
    following = passed_along(own_tokens[:1], -1)
    targets = jnp.concatenate([own_tokens[1:], following])
    rank = jnp.cumsum(own_mask) - 1
    chosen = (rank[None, :] == jnp.arange(keep, dtype=jnp.int32)[:, None]) & (
        own_mask[None, :] > 0
    )
    picked_targets = jnp.sum(jnp.where(chosen, targets[None, :], 0), 1)
    picked_weight = jnp.sum(jnp.where(chosen, weight[None, :], 0.0), 1)

    embedded = token_rows.astype(F32) * width**0.5
    normed_one, unit_one, scale_one = norm_forward(embedded, gains[:, 0])
    attention_input = normed_one.astype(BF16)
    attention_input, ffn_swaps = lax.optimization_barrier((attention_input, ffn_swaps))
    ffn_all = plane_gather(ffn_line_all, ffn_swaps, plane_corners(ffn_swaps))
    ffn_all = grouped(ffn_all, (part,) * (rows_ffn // part) + (rows_ffn_out,))
    projected = matmul_packed(attention_input, mixer_all, thin, 0, 3)
    memory_rows = passed_along(attention_input, 1)
    tail_rows = passed_along(attention_input[segment - 2 :], 1)
    first_cell = jnp.mod(2 - offset, 3)
    padding = 3 * slots - segment + 2
    extended = jnp.concatenate([tail_rows, attention_input, jnp.zeros((padding, width), BF16)], 0)
    slot_rows = lax.dynamic_slice_in_dim(extended, first_cell, 3 * slots, 0).reshape(
        slots, 3 * width
    )
    compressed = matmul_packed(slot_rows, mixer_all, 3 * thin, 1, 1)
    other_rows = [memory_rows]
    spare = -(segment + 3 * slots) % BLOCK
    book_parts = [own_book, book_number(own_pos - segment, book_ends)]
    pos_parts = [own_pos, own_pos - segment]
    for hop in (2, 3, 4):
        other_rows.append(passed_along(compressed, hop))
        owner = place - hop
        last_pos = (
            owner * segment
            + jnp.mod(2 - owner * segment, 3)
            + 3 * jnp.arange(slots, dtype=jnp.int32)
        )
        last_book = book_number(last_pos, book_ends)
        usable = (owner >= 0) & (last_pos < owner * segment + segment)
        usable = usable & (book_number(last_pos - 2, book_ends) == last_book)
        book_parts.append(jnp.where(usable, last_book, -2))
        pos_parts.append(jnp.full((slots,), -1, jnp.int32))
    book_parts.append(jnp.full((spare,), -2, jnp.int32))
    pos_parts.append(jnp.full((spare,), -1, jnp.int32))
    other_rows.append(jnp.zeros((spare, width), BF16))
    marks = (
        jnp.concatenate(book_parts)[:, None],
        jnp.concatenate(pos_parts)[:, None],
        own_book[None, :],
        own_pos[None, :],
    )
    other_rows = jnp.concatenate(other_rows, 0)
    memory_pairs = matmul_packed(other_rows, mixer_all, thin, 1, 2)
    attended, log_total = attention_forward(projected, memory_pairs, marks)
    w_out = mixer_all[:, 6 * thin : 7 * thin].reshape(width, width)
    residual = embedded + matmul(attended, w_out)

    normed_two, unit_two, scale_two = norm_forward(residual, gains[:, 1])
    ffn_input = normed_two.astype(BF16)
    output_rows, pre_act, activated_turned = feed_forward(
        ffn_input, ffn_all, residual, rows_ffn_out
    )
    normed_three, unit_three, scale_three = norm_forward(output_rows, gains[:, 2])
    final_rows = normed_three.astype(BF16)

    chosen_bf16 = chosen.astype(BF16)
    picked_rows = matmul(chosen_bf16, final_rows).astype(BF16)
    high, middle, low = bf16_parts(picked_weight)
    side = jnp.concatenate(
        [
            (picked_targets // 256).astype(BF16),
            (picked_targets % 256).astype(BF16),
            high,
            middle,
            low,
        ]
    )
    side_rows = jnp.zeros((16 * width,), BF16).at[: 5 * keep].set(side).reshape(16, width)
    half = keep // 2
    head_one = lax.all_gather(
        jnp.concatenate([picked_rows[:half], side_rows], 0), SHARE, axis=0, tiled=False
    )
    slot_spare = -slots % BLOCK
    slot_tall = jnp.concatenate([slot_rows, jnp.zeros((slot_spare, 3 * width), BF16)], 0)
    halves = [
        core_halves(value)
        for value in (
            grouped_transpose(ffn_input),
            activated_turned,
            grouped_transpose(attention_input),
            grouped_transpose(other_rows),
            grouped_transpose(slot_tall),
            grouped_transpose(attended),
        )
    ]
    rows_one = head_one[:, :half].reshape(share_count * half, width)
    side_all = head_one[:, half:].reshape(share_count, 16 * width)[:, : 5 * keep]
    rows_one, next_rows, halves = lax.optimization_barrier((rows_one, picked_rows[half:], halves))
    rows_two = lax.all_gather(next_rows, SHARE, axis=0, tiled=True)
    side_all = side_all.reshape(share_count, 5, 2, half).astype(F32)
    side_all = side_all.transpose(1, 2, 0, 3).reshape(5, 2, share_count * half)
    wanted_all = (side_all[0] * 256.0 + side_all[1]).astype(jnp.int32)
    weight_all = side_all[2] + side_all[3] + side_all[4]
    wanted_owner, wanted_local = vocab_place(wanted_all)
    wanted_all = jnp.where(wanted_owner == share_place, wanted_local, -1)
    mine = (jnp.arange(share_count * half) // half == share_place).astype(F32)
    loss_local = jnp.zeros((), F32)
    groups, stats = [], []
    for index, rows in enumerate((rows_one, rows_two)):
        wanted, row_weight = wanted_all[index][None], weight_all[index][None]
        logits, top, total, target_logit = head_logits(rows, table, wanted)
        loss_local -= jnp.sum(row_weight * target_logit)
        stats.append((top, total))
        groups.append([logits, row_weight, wanted, rows])
    log_norms = [share_combine(*stats[0]), None]
    stats[1], log_norms[0] = lax.optimization_barrier((stats[1], log_norms[0]))
    log_norms[1] = share_combine(*stats[1])
    for index, (logits, row_weight, wanted, rows) in enumerate(groups):
        loss_local += jnp.sum(row_weight * mine[None] * log_norms[index])
        groups[index] = (logits, log_norms[index], row_weight, wanted, rows)
    grad_picked = []
    for group in groups:
        grad_rows = head_row_grads(*group[:4], turned)
        grad_picked.append(lax.psum_scatter(grad_rows, SHARE, scatter_dimension=0, tiled=True))
    grad_picked = jnp.concatenate(grad_picked, 0)
    grad_table = head_table_grads(groups)
    grad_picked, grad_table = lax.optimization_barrier((grad_picked, grad_table))
    grad_final = matmul_tn(chosen_bf16, grad_picked)

    grad_output_rows, grad_gain_three = norm_backward(
        grad_final, unit_three, scale_three, gains[:, 2]
    )
    grad_branch = grad_output_rows.astype(BF16)
    grad_pre, grad_norm_two = feed_forward_back(grad_branch, pre_act, ffn_all)

    def product(pair, grad, lead=0):
        return pair + (grad[0], grad[1], lead)

    def with_other(grad):
        grad = grad if grad.ndim == 3 else grad[None]
        return grad, swapped(grad, "core")

    out_weights = [
        (
            [product(halves[1], with_other(grad_branch))],
            rows_ffn_out * device_count // width,
            False,
        ),
    ]
    ffn_weights = [
        ([product(halves[0], with_other(grad_pre))], ffn_in_m.shape[1] // width, True),
    ]
    out_sends = gradient_sends(out_weights, chip_place())
    out_sends, grad_norm_two = lax.optimization_barrier((out_sends, grad_norm_two))
    out_arrived = [swapped(send, axis) for send, axis in zip(out_sends, ("x", "y"))]
    grad_res_two, grad_gain_two = norm_backward(grad_norm_two, unit_two, scale_two, gains[:, 1])
    grad_residual = grad_output_rows + grad_res_two

    grad_attn_branch = grad_residual.astype(BF16)
    grad_attended = matmul_nt(grad_attn_branch, w_out).astype(BF16)
    ffn_weights.append(([product(halves[5], with_other(grad_attn_branch))], 1, True))
    grad_query, grad_own, grad_other = attention_backward(
        projected, memory_pairs, marks, log_total, grad_attended
    )
    grad_other, out_arrived = lax.optimization_barrier((grad_other, out_arrived))
    grad_other_rows = matmul_packed_back(grad_other, mixer_all, thin, 1).astype(BF16)
    grad_other_rows, grad_query = lax.optimization_barrier((grad_other_rows, grad_query))
    back_memory = passed_along(grad_other_rows[:segment], -1)
    returned = []
    for hop in (2, 3, 4):
        first_row = segment + (hop - 2) * slots
        returned.append(passed_along(grad_other_rows[first_row : first_row + slots], -hop))
    place = chip_place()
    ffn_sends = gradient_sends(ffn_weights, place)
    grad_input = matmul_packed_back(grad_query[None], mixer_all, thin, 0)
    grad_input = matmul_packed_back(grad_own, mixer_all, thin, 1, grad_input)
    returned, ffn_sends, grad_input = lax.optimization_barrier(
        (returned, ffn_sends, grad_input)
    )
    ffn_arrived = [swapped(send, axis) for send, axis in zip(ffn_sends, ("x", "y"))]
    grad_compressed = sum(part.astype(F32) for part in returned).astype(BF16)
    grad_slots = matmul_packed_back(grad_compressed[None], mixer_all, 3 * thin, 1)
    grad_slots = grad_slots.reshape(3 * slots, width)
    grad_first = jnp.concatenate([jnp.zeros((2, width), F32), grad_slots[:2]], 0)
    grad_first = lax.dynamic_slice_in_dim(grad_first, 2 - first_cell, 2, 0)
    back_tail = passed_along(grad_first.astype(BF16), -1).astype(F32)
    grad_input = grad_input + lax.dynamic_slice_in_dim(grad_slots, 2 - first_cell, segment, 0)
    grad_input = grad_input + back_memory.astype(F32)
    grad_input = grad_input.at[segment - 2 :].add(back_tail)
    grad_embed, grad_gain_one = norm_backward(grad_input, unit_one, scale_one, gains[:, 0])
    grad_scaled = ((grad_embed + grad_residual) * width**0.5).astype(BF16)

    query_pair, own_pair = with_other(grad_query), with_other(grad_own)
    other_pair = with_other(grad_other)
    slot_pair = with_other(jnp.pad(grad_compressed, ((0, slot_spare), (0, 0))))
    small = jnp.concatenate(
        [
            jnp.stack([grad_gain_one, grad_gain_two, grad_gain_three], 1).reshape(-1),
            jnp.full((128,), loss_local, F32),
        ]
    )
    grad_scaled, place, query_pair, own_pair, other_pair = lax.optimization_barrier(
        (grad_scaled, place, query_pair, own_pair, other_pair)
    )
    small = SmallSum(small)
    share_grads = lax.all_gather(grad_scaled, SHARE, axis=0, tiled=True)
    mixer_weights = [
        ([product(halves[2], query_pair)], 1, True),
        ([product(halves[2], own_pair, 0), product(halves[3], other_pair, 0)], 1, True),
        ([product(halves[2], own_pair, 1), product(halves[3], other_pair, 1)], 1, True),
        ([product(halves[4], slot_pair)], 3, False),
    ]
    mixer_sends = gradient_sends(mixer_weights, place)
    mixer_sends, place, arrived = lax.optimization_barrier(
        (mixer_sends, place, small.exchange())
    )
    small.value += arrived
    mixer_arrived = [swapped(send, axis) for send, axis in zip(mixer_sends, ("x", "y"))]
    out_sums = plane_sums(out_arrived, gradient_keeps(out_weights, place))
    out_sums, place, arrived = lax.optimization_barrier((out_sums, place, small.exchange()))
    small.value += arrived
    ffn_keeps = gradient_keeps(ffn_weights, place)
    ffn_keeps, place = lax.optimization_barrier((ffn_keeps, place))
    mixer_keeps = gradient_keeps(mixer_weights, place)
    ffn_arrived, mixer_keeps = lax.optimization_barrier((ffn_arrived, mixer_keeps))
    ffn_sums = plane_sums(ffn_arrived, ffn_keeps)
    mixer_sums = plane_sums(mixer_arrived, mixer_keeps)
    token_row, ffn_sums, mixer_sums, arrived = lax.optimization_barrier(
        (share_row[None, :], ffn_sums, mixer_sums, small.exchange())
    )
    small.value += arrived
    def spread(token_row, side, rows_of, dtype):
        piece = spread_piece(token_row, share_grads, grad_table, side, rows_of, dtype)
        return lax.optimization_barrier((piece, token_row))

    send_one, token_row = spread(token_row, 0, (1, 3), BF16)
    send_two, token_row = spread(token_row, 1, (2, 3), BF16)
    table_arrived = [swapped(send_one, "x"), swapped(send_two, "y")]
    others = [plane_others(sums) for sums in (out_sums, ffn_sums, mixer_sums)]
    others, token_row = lax.optimization_barrier((others, token_row))
    line = line_open(
        jnp.concatenate(
            [
                line_parts(out_weights, out_sums, others[0]),
                line_parts(ffn_weights, ffn_sums, others[1]),
                line_parts(mixer_weights, mixer_sums, others[2]),
            ],
            1,
        )
    )
    moves, token_row = lax.optimization_barrier((line_sends(line), token_row))
    line = line_move(line, moves)
    keep_one, token_row = spread(token_row, 0, (0, 2), F32)
    keep_two, token_row = spread(token_row, 1, (0, 1), F32)
    table_keeps = [keep_one, keep_two]
    table_keeps, table_arrived, moved = lax.optimization_barrier(
        (table_keeps, table_arrived, line[1:3])
    )
    summed = line_close((line[0], *moved, line[3]))
    ends = (rows_ffn_out, rows_ffn_out + rows_ffn, rows_ffn_out + rows_ffn + rows_out)
    ffn_out_grad, ffn_in_grad, attn_out_grad, mixer_grads = jnp.split(summed, ends)
    halves_new = []
    for arrived, keep_part, axis in zip(table_arrived, table_keeps, ("y", "x")):
        other = (keep_part[1] + arrived[1].astype(F32)).astype(BF16)
        mine = keep_part[0] + arrived[0].astype(F32)
        halves_new.append(mine + swapped(other, axis).astype(F32))
    halves_new, small.value = lax.optimization_barrier((halves_new, small.value))
    grad_table = jnp.concatenate(halves_new, 1)
    if lax.axis_size("far") > 1:
        grad_table = lax.psum_scatter(
            grad_table.astype(BF16), "far", scatter_dimension=0, tiled=True
        )

    small = small.total()
    loss_total = small[3 * width]
    device = lax.axis_index(ALL)
    gain_grads = lax.dynamic_slice_in_dim(small, device * gain_count, gain_count, 0)

    def side_by_side(rows, count):
        return jnp.concatenate(jnp.split(rows, count, 0), 1)

    low, high = rows_in, rows_in + rows_comp
    grads = (
        grad_table,
        side_by_side(mixer_grads[:low], 3),
        attn_out_grad,
        mixer_grads[low:high],
        side_by_side(ffn_in_grad, rows_ffn // attn_in_m.shape[0]),
        ffn_out_grad,
        gain_grads.reshape(gains_m.shape),
    )
    results = []
    for master, first, second, grad, rate in zip(masters, firsts, seconds, grads, STEP_RATES):
        results.extend(adam_update(master, first, second, grad.astype(F32), rate))
    return (loss_total,) + tuple(results)


def solution(mesh):
    batch_count, seq_count = mesh.shape["batch"], mesh.shape["seq"]
    devices = mesh.devices.reshape(batch_count, seq_count // 8, 2, 2, 2)
    grid = Mesh(devices, ALL)
    rows = P(ALL, None)
    return jax.shard_map(
        per_device,
        mesh=grid,
        in_specs=(P("batch", SEQ), P("batch", None), P("batch", SEQ)) + (rows,) * 21,
        out_specs=(P(),) + (rows,) * 21,
        check_vma=False,
    )
```
